128 devices in a mesh: dp: 8 (over z, core), seq: 4 (over y), head: 4 (over x).
Axes of the slice: x: 4, y: 4, z: 4, core: 2. Of those that a mesh axis runs over, the one named last changes fastest.
Arguments:
- tokens: bfloat16 [16, 1024, 2048], P('dp', ('seq', 'head')), may hold values from -6 to 6
- w_qkv: bfloat16 [2048, 2688], replicated, may hold values from -0.125 to 0.125
- w_out: bfloat16 [1792, 2048], replicated, may hold values from -1 to 1
- w_ffn_in: bfloat16 [7168, 2, 2048], P(('seq', 'head')), may hold values from -0.125 to 0.125
- w_ffn_out: bfloat16 [7168, 2048], P(('seq', 'head')), may hold values from -0.0625 to 0.0625
- g_attn: float32 [2048], replicated, may hold values from 0.5 to 1.5
- g_ffn: float32 [2048], replicated, may hold values from 0.5 to 1.5
- q_gain: float32 [64], replicated, may hold values from 0.1 to 1.9
- k_gain: float32 [64], replicated, may hold values from 0.1 to 1.9
- doc_starts: int32 [16, 4], P('dp'), may hold values from 0 to 1023, as said below
- d_out: bfloat16 [16, 1024, 2048], P('dp', ('seq', 'head')), may hold values from -6 to 6
Outputs:
- output: bfloat16 [16, 1024, 2048], P('dp', ('seq', 'head'))
- grad_tokens: bfloat16 [16, 1024, 2048], P('dp', ('seq', 'head'))
- grad_w_qkv: float32 [2048, 2688], P(('dp', 'seq', 'head'))
- grad_w_out: float32 [1792, 2048], P(None, ('dp', 'seq', 'head'))
- grad_w_ffn_in: float32 [7168, 2, 2048], P(('seq', 'head'))
- grad_w_ffn_out: float32 [7168, 2048], P(('seq', 'head'))
- grad_g_attn: float32 [2048], replicated
- grad_g_ffn: float32 [2048], replicated
- grad_q_gain: float32 [64], replicated
- grad_k_gain: float32 [64], replicated
The draws below stay inside these ranges and needn't reach their ends.
Inputs may be any that keep to these rules, and one draw needn't show every extreme that they name: `doc_starts`: each row holds 4 documents; its offsets rise and the first is 0. In every row one document begins within the first 256 positions and ends within the last 256.
All inputs are finite; a program needn't handle non-finite values.
Results may differ from the reference program's by a relative error of at most 0.02.
Values may be sent and summed in bfloat16 or wider, within the bound.
A program may use at most 256 MiB of HBM per device.

```python
import math
import jax
import jax.numpy as jnp
from jax import lax

D = 2048
FF = 7168
HEADS = 28
KV = 7
HD = 64
ROW_LEN = 1024
DOCS = 4
NROWS = 16
SPAN = 256
GROUP = 4
QKVW = 2688


def draw_doc_starts(key, part):
    key = jax.random.fold_in(key, 11)
    short_key, place_key = jax.random.split(key)
    shorts = jax.random.randint(short_key, (NROWS, DOCS - 1), 1, SPAN // 4 + 1)
    place = jax.random.randint(place_key, (NROWS, 1), 0, DOCS)
    slot = jnp.arange(DOCS)[None, :]
    index = jnp.clip(slot - (slot > place).astype(jnp.int32), 0, DOCS - 2)
    picked = jnp.take_along_axis(shorts, jnp.broadcast_to(index, (NROWS, DOCS)), axis=1)
    longest = ROW_LEN - jnp.sum(shorts, axis=1, keepdims=True)
    lengths = jnp.where(slot == place, longest, picked)
    return (jnp.cumsum(lengths, axis=1) - lengths).astype(jnp.int32)


def block_scale(own_key, extent, cuts, smallest, largest):
    loudness, own = 1.0, jax.random.fold_in(own_key, 6)
    for dim, blocks in cuts:
        draws = jnp.exp(jax.random.uniform(jax.random.fold_in(own, dim), (blocks,), jnp.float32, smallest / len(cuts), largest / len(cuts)))
        loudness = loudness * jnp.repeat(draws, extent[dim] // blocks).reshape([-1 if axis == dim else 1 for axis in range(len(extent))])
    return loudness


def normal_values(key, extent, scale, reach, cuts=(), held_as=jnp.bfloat16):
    result = scale * jax.random.normal(key, extent, jnp.float32)
    if cuts:
        result = result * block_scale(key, extent, cuts, -0.22, 0.18)
    return jnp.clip(result, -reach, reach).astype(held_as)


def setup_inputs(seed: int = 0) -> dict:
    key_of = jax.random.split(jax.random.key(seed), 12)
    tokens = normal_values(key_of[0], (NROWS, ROW_LEN, D), 1.0, 6.0, ((0, 8), (1, 16)))
    w_qkv = normal_values(key_of[1], (D, QKVW), D ** -0.5, 0.125)
    w_out = normal_values(key_of[2], (HEADS * HD, D), (HEADS * HD // 64) ** -0.5, 1.0)
    w_ffn_in = normal_values(key_of[3], (FF, 2, D), D ** -0.5, 0.125, ((0, 16),))
    w_ffn_out = normal_values(key_of[4], (FF, D), FF ** -0.5, 0.0625, ((0, 16),))
    g_attn = jnp.clip(1.0 + 0.1 * jax.random.normal(key_of[5], (D,), jnp.float32), 0.5, 1.5)
    g_ffn = jnp.clip(1.0 + 0.1 * jax.random.normal(key_of[6], (D,), jnp.float32), 0.5, 1.5)
    q_gain = jnp.clip(1.0 + 0.18 * jax.random.normal(key_of[7], (HD,), jnp.float32), 0.1, 1.9)
    k_gain = jnp.clip(1.0 + 0.18 * jax.random.normal(key_of[8], (HD,), jnp.float32), 0.1, 1.9)
    doc_starts = draw_doc_starts(jax.random.fold_in(key_of[11], 71), 0)
    d_out = normal_values(key_of[10], (NROWS, ROW_LEN, D), 1.0, 6.0, ((0, 8), (1, 16)))
    return dict(tokens=tokens, w_qkv=w_qkv, w_out=w_out, w_ffn_in=w_ffn_in, w_ffn_out=w_ffn_out, g_attn=g_attn, g_ffn=g_ffn, q_gain=q_gain, k_gain=k_gain, doc_starts=doc_starts, d_out=d_out)


@jax.custom_vjp
def low(v):
    return lax.optimization_barrier(v.astype(jnp.bfloat16)).astype(jnp.float32)

@jax.custom_vjp
def low_back(v):
    return v

def low_keep(v):
    return (low(v), None)

def low_pass(kept, grad):
    return (grad,)

def back_keep(v):
    return (v, None)

def back_low(kept, grad):
    return (low(grad),)
low.defvjp(low_keep, low_pass)
low_back.defvjp(back_keep, back_low)
EPS = 1e-06
SCALE = 0.125
NEGATIVE = -1e+30
HIGH = lax.Precision.HIGHEST

def rms_norm(v):
    return v * lax.rsqrt(lax.optimization_barrier(jnp.mean(v * v, axis=-1, keepdims=True)) + EPS)

def rotate(v, cosine, sine):
    half = v.shape[-1] // 2
    first = v[..., :half]
    second = v[..., half:]
    return jnp.concatenate([first * cosine - second * sine, second * cosine + first * sine], -1)

def angle_tables(positions, width):
    half = width // 2
    freq = jnp.exp(jnp.arange(half, dtype=jnp.float32) * (-2.0 * math.log(10000.0) / width))
    angle = positions.astype(jnp.float32)[:, None] * freq[None, :]
    return (jnp.cos(angle), jnp.sin(angle))

def row_forward(x, w_qkv, w_out, w_ffn_in, w_ffn_out, g_attn, g_ffn, q_gain, k_gain, starts):
    length = x.shape[0]
    positions = jnp.arange(length, dtype=jnp.int32)
    cosine, sine = angle_tables(positions, HD)
    cosine = cosine[:, None, :]
    sine = sine[:, None, :]
    n1 = rms_norm(x)
    h1 = low(n1 * g_attn)
    qkv = low_back(jnp.dot(h1, w_qkv, precision=HIGH))
    queries = qkv[:, :HEADS * HD].reshape(length, HEADS, HD)
    keys = qkv[:, HEADS * HD:(HEADS + KV) * HD].reshape(length, KV, HD)
    values = qkv[:, (HEADS + KV) * HD:].reshape(length, KV, HD)
    queries = low_back(low(rotate(rms_norm(queries) * q_gain, cosine, sine)))
    keys = low_back(low(rotate(rms_norm(keys) * k_gain, cosine, sine)))
    values = low_back(low(values))
    docs = lax.optimization_barrier(jnp.sum((starts[None, :] <= positions[:, None]).astype(jnp.int32), axis=1))
    allowed = (positions[None, :] <= positions[:, None]) & (docs[None, :] == docs[:, None])
    grouped = queries.reshape(length, KV, GROUP, HD).transpose(1, 2, 0, 3)
    key_heads = keys.transpose(1, 0, 2)
    value_heads = values.transpose(1, 0, 2)

    def one_group(pieces):
        query, key, value = pieces
        scores = low_back(jnp.einsum('hqa,ka->hqk', query, key, precision=HIGH) * SCALE)
        scores = jnp.where(allowed[None], scores, NEGATIVE)
        probs = jax.nn.softmax(scores, axis=-1)
        return jnp.einsum('hqk,ka->hqa', low(probs), value, precision=HIGH)
    mixed = lax.map(jax.checkpoint(one_group), (grouped, key_heads, value_heads))
    mixed = low_back(low(mixed.transpose(2, 0, 1, 3).reshape(length, HEADS * HD)))
    r1 = x + low_back(jnp.dot(mixed, w_out, precision=HIGH))
    h2 = low(rms_norm(r1) * g_ffn)
    both = jnp.einsum('fcd,td->tcf', w_ffn_in, h2, precision=HIGH)
    gate = low_back(both[:, 0])
    up = low_back(both[:, 1])
    hidden = low(jax.nn.silu(gate) * up)
    return r1 + jnp.dot(hidden, w_ffn_out, precision=HIGH)

def reference(tokens, w_qkv, w_out, w_ffn_in, w_ffn_out, g_attn, g_ffn, q_gain, k_gain, doc_starts, d_out):
    weights = (w_qkv.astype(jnp.float32), w_out.astype(jnp.float32), w_ffn_in.astype(jnp.float32), w_ffn_out.astype(jnp.float32), g_attn.astype(jnp.float32), g_ffn.astype(jnp.float32), q_gain.astype(jnp.float32), k_gain.astype(jnp.float32))
    zeros = tuple((jnp.zeros(w.shape, jnp.float32) for w in weights))

    def row_step(totals, row):
        x_row, dy_row, starts = row

        def forward(x_in, a, b, c, d, e, f, g, h):
            return row_forward(x_in, a, b, c, d, e, f, g, h, starts)
        out, pull = jax.vjp(forward, x_row.astype(jnp.float32), *weights)
        grads = pull(dy_row.astype(jnp.float32))
        totals = tuple((t + g for t, g in zip(totals, grads[1:])))
        return (totals, (out.astype(jnp.bfloat16), grads[0].astype(jnp.bfloat16)))
    totals, (outputs, grad_x) = lax.scan(row_step, zeros, (tokens, d_out, doc_starts))
    return (outputs, grad_x, totals[0], totals[1], totals[2], totals[3], totals[4], totals[5], totals[6], totals[7])
```

```python
import functools
import math

import jax
import jax.numpy as jnp
from jax import lax
from jax.experimental import pallas as pl
from jax.experimental.pallas import tpu as pltpu
from jax.sharding import Mesh
from jax.sharding import PartitionSpec as P

HEADS = 28
KV = 7
HD = 64
PER_GROUP = HEADS // KV
DP_SEQ_HEAD = ("dp_0", "dp_1", "seq", "head")
DP = ("dp_0", "dp_1")
RING = 4
BLOCK = 64
MESH = pl.DeviceIdType.MESH
EPS = 1e-06
SCALE = 0.125
f32 = jnp.float32
bf16 = jnp.bfloat16
VMEM_BYTES = 60 * 2**20


def nt(a, b):
    return lax.dot_general(a, b, (((1,), (1,)), ((), ())), preferred_element_type=f32)


def nn(a, b):
    return lax.dot_general(a, b, (((1,), (0,)), ((), ())), preferred_element_type=f32)


def tn(a, b):
    return lax.dot_general(a, b, (((0,), (0,)), ((), ())), preferred_element_type=f32)


def shift(index, by):
    return lax.rem(index + (by + RING), RING)


def barrier_with(axes):
    barrier = pltpu.get_barrier_semaphore()
    for axis in axes:
        index = lax.axis_index(axis)
        for by in (1, -1):
            pl.semaphore_signal(
                barrier, inc=1, device_id={axis: shift(index, by)}, device_id_type=MESH
            )
    pl.semaphore_wait(barrier, 2 * len(axes))


class Copies:
    def __init__(self, send, recv):
        self.send = send
        self.recv = recv
        self.started = []

    def start(self, slot, src, dst, axis, by):
        copy = pltpu.make_async_remote_copy(
            src_ref=src,
            dst_ref=dst,
            send_sem=self.send.at[slot],
            recv_sem=self.recv.at[slot],
            device_id={axis: shift(lax.axis_index(axis), by)},
            device_id_type=MESH,
        )
        copy.start()
        self.started.append(copy)
        return copy

    def finish(self):
        for copy in self.started:
            copy.wait_send()


INNER = ("head", "seq")
GROUP = ("seq", "head")


class PlaneGather:
    def __init__(self, copies, base, half, own, buf):
        self.c = copies
        self.base = base + 8 * half
        self.half = half
        self.own = own
        self.buf = buf
        self.i = lax.axis_index(INNER[half])
        self.g = lax.axis_index(GROUP[half])

    def row(self, by=0):
        return 4 * self.half + shift(self.g, by)

    def step1(self):
        ax = INNER[self.half]
        dst = self.buf.at[self.row(), self.i]
        self.a = self.c.start(self.base, self.own, dst, ax, 1)
        self.b = self.c.start(self.base + 1, self.own, dst, ax, -1)

    def step2(self):
        ax = INNER[self.half]
        n = self.buf.shape[2] // 2
        self.a.wait_recv()
        left = self.buf.at[self.row(), shift(self.i, -1), pl.ds(0, n)]
        self.a = self.c.start(self.base + 2, left, left, ax, 1)
        self.b.wait_recv()
        right = self.buf.at[self.row(), shift(self.i, 1), pl.ds(n, n)]
        self.b = self.c.start(self.base + 3, right, right, ax, -1)

    def step3(self):
        ax = GROUP[self.half]
        self.a.wait_recv()
        self.b.wait_recv()
        rows = self.buf.at[self.row()]
        self.a = self.c.start(self.base + 4, rows, rows, ax, 1)
        self.b = self.c.start(self.base + 5, rows, rows, ax, -1)

    def step4(self):
        ax = GROUP[self.half]
        self.a.wait_recv()
        left = self.buf.at[self.row(-1), pl.ds(0, 2)]
        self.a = self.c.start(self.base + 6, left, left, ax, 1)
        self.b.wait_recv()
        right = self.buf.at[self.row(1), pl.ds(2, 2)]
        self.b = self.c.start(self.base + 7, right, right, ax, -1)

    def finish(self):
        self.a.wait_recv()
        self.b.wait_recv()


class PlaneSum:
    def __init__(self, copies, base, half, part, land1, land2, land3, land4):
        self.c = copies
        self.base = base + 8 * half
        self.half = half
        self.part = part
        self.l1, self.l2, self.l3, self.l4 = (
            ref.at[half] for ref in (land1, land2, land3, land4)
        )
        self.i = lax.axis_index(INNER[half])
        self.g = lax.axis_index(GROUP[half])

    def row(self, by=0):
        return 4 * self.half + shift(self.g, by)

    def add(self, ref, other):
        ref[...] = (ref[...].astype(f32) + other[...].astype(f32)).astype(ref.dtype)

    def step1(self):
        ax = GROUP[self.half]
        row = self.row(2)
        self.a = self.c.start(self.base, self.part.at[row, pl.ds(0, 2)], self.l1.at[0], ax, 1)
        self.b = self.c.start(self.base + 1, self.part.at[row, pl.ds(2, 2)], self.l1.at[1], ax, -1)

    def step2(self):
        ax = GROUP[self.half]
        self.a.wait_recv()
        self.add(self.part.at[self.row(1), pl.ds(0, 2)], self.l1.at[0])
        self.a = self.c.start(self.base + 2, self.part.at[self.row(1)], self.l2.at[0], ax, 1)
        self.b.wait_recv()
        self.add(self.part.at[self.row(-1), pl.ds(2, 2)], self.l1.at[1])
        self.b = self.c.start(self.base + 3, self.part.at[self.row(-1)], self.l2.at[1], ax, -1)

    def step3(self):
        ax = INNER[self.half]
        n = self.part.shape[2] // 2
        self.a.wait_recv()
        self.b.wait_recv()
        rows = self.part.at[self.row()]
        rows[...] = (
            rows[...].astype(f32) + self.l2[0].astype(f32) + self.l2[1].astype(f32)
        ).astype(rows.dtype)
        block = self.part.at[self.row(), shift(self.i, 2)]
        self.a = self.c.start(self.base + 4, block.at[pl.ds(0, n)], self.l3.at[0], ax, 1)
        self.b = self.c.start(self.base + 5, block.at[pl.ds(n, n)], self.l3.at[1], ax, -1)

    def step4(self):
        ax = INNER[self.half]
        n = self.part.shape[2] // 2
        self.a.wait_recv()
        right = self.part.at[self.row(), shift(self.i, 1)]
        self.add(right.at[pl.ds(0, n)], self.l3.at[0])
        self.a = self.c.start(self.base + 6, right, self.l4.at[0], ax, 1)
        self.b.wait_recv()
        left = self.part.at[self.row(), shift(self.i, -1)]
        self.add(left.at[pl.ds(n, n)], self.l3.at[1])
        self.b = self.c.start(self.base + 7, left, self.l4.at[1], ax, -1)

    def result(self):
        self.a.wait_recv()
        self.b.wait_recv()
        own = self.part[self.row(), self.i].astype(f32)
        return own + self.l4[0].astype(f32) + self.l4[1].astype(f32)


def sum_landings(columns):
    return [
        pltpu.VMEM((2, 2, 2, BLOCK, columns), bf16),
        pltpu.VMEM((2, 2, 4, BLOCK, columns), bf16),
        pltpu.VMEM((2, 2, BLOCK // 2, columns), bf16),
        pltpu.VMEM((2, 2, BLOCK, columns), bf16),
    ]


def ffn_kernel(
    h2_ref,
    dy_ref,
    win_ref,
    wdn_ref,
    outp_ref,
    dh2_ref,
    gin_ref,
    gdn_ref,
    h2a,
    dya,
    win,
    wdn,
    hid,
    dbo,
    dpt,
    l1,
    l2,
    l3,
    l4,
    stage,
    gstage,
    send,
    recv,
    lsem,
    osem,
    gsem,
):
    units = wdn.shape[0]
    width = wdn.shape[1]
    copies = Copies(send, recv)
    weights = [
        pltpu.make_async_copy(win_ref, win, lsem.at[8]),
        pltpu.make_async_copy(wdn_ref, wdn, lsem.at[9]),
    ]
    for copy in weights:
        copy.start()
    loads = []
    for j in range(4):
        loads.append(pltpu.make_async_copy(dy_ref.at[j, :, 0], dya.at[j], lsem.at[j]))
        loads.append(pltpu.make_async_copy(dy_ref.at[:, j, 1], dya.at[4 + j], lsem.at[4 + j]))
    for copy in loads:
        copy.start()
    barrier_with(("seq", "head"))
    gathers = [PlaneGather(copies, 0, half, h2_ref.at[half], h2a) for half in (0, 1)]
    for gather in gathers:
        gather.step1()
    for half in (0, 1):
        h2a[gathers[half].row(), gathers[half].i] = h2_ref[half]
    for gather in gathers:
        gather.step2()
    for copy in weights + loads:
        copy.wait()
    for gather in gathers:
        gather.step3()
    seq, head = lax.axis_index("seq"), lax.axis_index("head")

    def group(half, by):
        return 4 * half + lax.rem(seq + half * (head - seq) + by + 4, 4)

    def rows_of(ref, q):
        return ref[q].reshape(4 * BLOCK, width)

    def columns_of(q):
        return pl.ds(pl.multiple_of(q * 4 * BLOCK, 4 * BLOCK), 4 * BLOCK)

    def forward(q):
        both = nt(win[...], rows_of(h2a, q))
        d_hidden = nt(wdn[...], rows_of(dya, q))
        gate = both[:units]
        up = both[units:]
        sig = 1.0 / (1.0 + jnp.exp(-gate))
        act = gate * sig
        cols = columns_of(q)
        hid[:, cols] = (act * up).astype(bf16)
        dbo[:units, cols] = (d_hidden * up * (sig * (1.0 + gate * (1.0 - sig)))).astype(bf16)
        dbo[units:, cols] = (d_hidden * act).astype(bf16)

    def back(q):
        value = tn(dbo[:, columns_of(q)], win[...])
        dpt[q] = value.astype(bf16).reshape(4, BLOCK, width)

    @pl.loop(0, 2)
    def _(half):
        forward(group(half, 0))

    for gather in gathers:
        gather.step4()

    @pl.loop(0, 4)
    def _(k):
        forward(group(lax.div(k, 2), 1 - 2 * lax.rem(k, 2)))

    for gather in gathers:
        gather.finish()

    @pl.loop(0, 2)
    def _(half):
        forward(group(half, 2))
        back(group(half, 2))

    sums = [PlaneSum(copies, 16, half, dpt, l1, l2, l3, l4) for half in (0, 1)]
    for total in sums:
        total.step1()

    @pl.loop(0, 4)
    def _(k):
        back(group(lax.div(k, 2), 1 - 2 * lax.rem(k, 2)))

    for total in sums:
        total.step2()

    @pl.loop(0, 2)
    def _(half):
        back(group(half, 0))

    tile = gstage.shape[2]
    tiles = width // tile
    tokens = 8 * 4 * BLOCK
    gcopies = []
    for n in range(tiles):
        cols = pl.ds(n * tile, tile)
        if n >= 2:
            for copy in gcopies[n - 2]:
                copy.wait()
        slot = n % 2
        gstage[slot, : 2 * units] = nn(
            dbo[...], h2a[:, :, :, cols].reshape(tokens, tile)
        ).astype(bf16)
        gstage[slot, 2 * units :] = nn(
            hid[...], dya[:, :, :, cols].reshape(tokens, tile)
        ).astype(bf16)
        pair = [
            pltpu.make_async_copy(
                gstage.at[slot, pl.ds(0, 2 * units)], gin_ref.at[:, cols], gsem.at[slot, 0]
            ),
            pltpu.make_async_copy(
                gstage.at[slot, pl.ds(2 * units, units)], gdn_ref.at[:, cols], gsem.at[slot, 1]
            ),
        ]
        for copy in pair:
            copy.start()
        gcopies.append(pair)
    for total in sums:
        total.step3()
    for pair in gcopies[-2:]:
        for copy in pair:
            copy.wait()

    def out_copy(q):
        slot = q % 2
        place = outp_ref.at[q, :, 0] if q < 4 else outp_ref.at[:, q - 4, 1]
        return pltpu.make_async_copy(stage.at[slot], place, osem.at[slot])

    def out_part(q):
        if q >= 2:
            out_copy(q - 2).wait()
        value = tn(hid[:, pl.ds(q * 4 * BLOCK, 4 * BLOCK)], wdn[...])
        stage[q % 2] = value.astype(bf16).reshape(4, BLOCK, width)
        out_copy(q).start()

    for q in range(4):
        out_part(q)
    for total in sums:
        total.step4()
    for q in range(4, 8):
        out_part(q)
    for half in (0, 1):
        dh2_ref[half] = sums[half].result()
    out_copy(6).wait()
    out_copy(7).wait()
    copies.finish()


def ffn(h2, dy_all, w_in, w_down):
    units, width = w_down.shape
    tokens = 32 * BLOCK
    tile = 512
    any_spec = pl.BlockSpec(memory_space=pl.ANY)
    vmem_spec = pl.BlockSpec(memory_space=pltpu.VMEM)
    return pl.pallas_call(
        ffn_kernel,
        out_shape=(
            jax.ShapeDtypeStruct((4, 4, 2, BLOCK, width), bf16),
            jax.ShapeDtypeStruct((2, BLOCK, width), f32),
            jax.ShapeDtypeStruct((2 * units, width), bf16),
            jax.ShapeDtypeStruct((units, width), bf16),
        ),
        in_specs=[vmem_spec, any_spec, any_spec, any_spec],
        out_specs=(any_spec, vmem_spec, any_spec, any_spec),
        scratch_shapes=[
            pltpu.VMEM((8, 4, BLOCK, width), bf16),
            pltpu.VMEM((8, 4, BLOCK, width), bf16),
            pltpu.VMEM((2 * units, width), bf16),
            pltpu.VMEM((units, width), bf16),
            pltpu.VMEM((units, tokens), bf16),
            pltpu.VMEM((2 * units, tokens), bf16),
            pltpu.VMEM((8, 4, BLOCK, width), bf16),
            *sum_landings(width),
            pltpu.VMEM((2, 4, BLOCK, width), bf16),
            pltpu.VMEM((2, 3 * units, tile), bf16),
            pltpu.SemaphoreType.DMA((32,)),
            pltpu.SemaphoreType.DMA((32,)),
            pltpu.SemaphoreType.DMA((10,)),
            pltpu.SemaphoreType.DMA((2,)),
            pltpu.SemaphoreType.DMA((2, 2)),
        ],
        compiler_params=pltpu.CompilerParams(
            collective_id=1, has_side_effects=True, vmem_limit_bytes=VMEM_BYTES
        ),
        name="ffn",
    )(h2, dy_all, w_in, w_down)


def mask_rows(starts_ref, row, transposed, mask_ref):
    seq, head = lax.axis_index("seq"), lax.axis_index("head")
    keys = 16 * BLOCK
    index = lax.broadcasted_iota(jnp.int32, (1, keys), 1)
    if transposed:
        group = lax.div(index, 4 * BLOCK)
        inner = lax.rem(lax.div(index, BLOCK), 4)
        k_pos = (inner * 4 + group) * BLOCK + lax.rem(index, BLOCK)
    else:
        k_pos = index
    first = (seq * 4 + head) * BLOCK
    q_pos = first + lax.broadcasted_iota(jnp.int32, (BLOCK, 1), 0)
    k_doc = jnp.zeros((1, keys), jnp.int32)
    q_doc = jnp.zeros((BLOCK, 1), jnp.int32)
    for d in range(starts_ref.shape[1]):
        start = starts_ref[row, d]
        k_doc += (start <= k_pos).astype(jnp.int32)
        q_doc += (start <= q_pos).astype(jnp.int32)
    seen = (k_pos <= q_pos) & (k_doc == q_doc)
    mask_ref[row] = seen.astype(f32)


LOG2E_SCALE = SCALE * math.log2(math.e)


def stacked(block, where):
    rows = jnp.concatenate([block[:, h * HD : (h + 1) * HD] for h in range(PER_GROUP)], 0)
    zero = jnp.zeros_like(rows)
    return jnp.concatenate([rows, zero] if where == 0 else [zero, rows], 1)


def unstacked(rows):
    return jnp.concatenate([rows[h * BLOCK : (h + 1) * BLOCK] for h in range(PER_GROUP)], 1)


def weights_of(q_rows, kv_rows, mask):
    scores = nt(q_rows, kv_rows)
    keys = kv_rows.shape[0]
    e = jnp.exp2(scores * LOG2E_SCALE).reshape(PER_GROUP, BLOCK, keys) * mask[None]
    return e.reshape(PER_GROUP * BLOCK, keys)


def attend_kernel(starts_ref, q_ref, kv_ref, o_ref, kva_ref, kva, mask, send, recv, lsem):
    copies = Copies(send, recv)
    barrier_with(("seq", "head"))
    gathers = [PlaneGather(copies, 0, half, kv_ref.at[half], kva) for half in (0, 1)]
    for gather in gathers:
        gather.step1()
    for half in (0, 1):
        kva[gathers[half].row(), gathers[half].i] = kv_ref[half]
    mask_rows(starts_ref, 0, False, mask)
    mask_rows(starts_ref, 1, True, mask)
    for gather in gathers:
        gather.step2()
    for gather in gathers:
        gather.step3()
    for gather in gathers:
        gather.step4()
    for gather in gathers:
        gather.finish()
    keep = pltpu.make_async_copy(kva, kva_ref, lsem)
    keep.start()

    @pl.loop(0, 2)
    def _(row):
        for g in range(KV):
            rows = pl.ds(pl.multiple_of(row * BLOCK, BLOCK), BLOCK)
            cols = slice(g * PER_GROUP * HD, (g + 1) * PER_GROUP * HD)
            q_rows = stacked(q_ref[rows, cols], 0)
            kv_rows = kva[pl.ds(row * 4, 4), :, :, g * 2 * HD : (g + 1) * 2 * HD].reshape(
                16 * BLOCK, 2 * HD
            )
            e = weights_of(q_rows, kv_rows, mask[row])
            total = jnp.sum(e, axis=1, keepdims=True)
            mixed = nn(e.astype(bf16), kv_rows)[:, HD:] / total
            o_ref[rows, cols] = unstacked(mixed.astype(bf16))

    keep.wait()
    copies.finish()


def attend(starts, q, kv):
    vmem_spec = pl.BlockSpec(memory_space=pltpu.VMEM)
    return pl.pallas_call(
        attend_kernel,
        out_shape=(
            jax.ShapeDtypeStruct(q.shape, bf16),
            jax.ShapeDtypeStruct((8, 4, BLOCK, kv.shape[2]), bf16),
        ),
        in_specs=[pl.BlockSpec(memory_space=pltpu.SMEM), vmem_spec, vmem_spec],
        out_specs=(vmem_spec, pl.BlockSpec(memory_space=pl.ANY)),
        scratch_shapes=[
            pltpu.VMEM((8, 4, BLOCK, kv.shape[2]), bf16),
            pltpu.VMEM((2, BLOCK, 16 * BLOCK), f32),
            pltpu.SemaphoreType.DMA((16,)),
            pltpu.SemaphoreType.DMA((16,)),
            pltpu.SemaphoreType.DMA,
        ],
        compiler_params=pltpu.CompilerParams(
            collective_id=2, has_side_effects=True, vmem_limit_bytes=VMEM_BYTES
        ),
        name="attend",
    )(starts, q, kv)


def attend_back_kernel(
    starts_ref, q_ref, do_ref, kva_ref, dq_ref, dkv_ref, kva, part, mask, l1, l2, l3, l4, send, recv, lsem
):
    copies = Copies(send, recv)
    load = pltpu.make_async_copy(kva_ref, kva, lsem)
    load.start()
    barrier_with(("seq", "head"))
    mask_rows(starts_ref, 0, False, mask)
    mask_rows(starts_ref, 1, True, mask)
    load.wait()
    sums = [PlaneSum(copies, 0, half, part, l1, l2, l3, l4) for half in (0, 1)]

    @pl.loop(0, 2)
    def _(row):
        for g in range(KV):
            rows = pl.ds(pl.multiple_of(row * BLOCK, BLOCK), BLOCK)
            cols = slice(g * PER_GROUP * HD, (g + 1) * PER_GROUP * HD)
            lanes = slice(g * 2 * HD, (g + 1) * 2 * HD)
            q_rows = stacked(q_ref[rows, cols], 0)
            do_rows = stacked(do_ref[rows, cols], 1)
            kv_rows = kva[pl.ds(row * 4, 4), :, :, lanes].reshape(16 * BLOCK, 2 * HD)
            e = weights_of(q_rows, kv_rows, mask[row])
            probs = e * (1.0 / jnp.sum(e, axis=1, keepdims=True))
            d_probs = nt(do_rows, kv_rows)
            delta = jnp.sum(probs * d_probs, axis=1, keepdims=True)
            d_scores = (probs * (d_probs - delta)).astype(bf16)
            dq = nn(d_scores, kv_rows)[:, :HD] * SCALE
            dq_ref[rows, cols] = unstacked(dq.astype(bf16))
            dkv = tn(d_scores, q_rows * jnp.asarray(SCALE, bf16)) + tn(probs.astype(bf16), do_rows)
            part[pl.ds(row * 4, 4), :, :, lanes] = dkv.astype(bf16).reshape(4, 4, BLOCK, 2 * HD)

    for total in sums:
        total.step1()
    for total in sums:
        total.step2()
    for total in sums:
        total.step3()
    for total in sums:
        total.step4()
    for half in (0, 1):
        dkv_ref[half] = sums[half].result().astype(bf16)
    copies.finish()


def attend_back(starts, q, d_o, kva):
    vmem_spec = pl.BlockSpec(memory_space=pltpu.VMEM)
    columns = kva.shape[3]
    return pl.pallas_call(
        attend_back_kernel,
        out_shape=(
            jax.ShapeDtypeStruct(q.shape, bf16),
            jax.ShapeDtypeStruct((2, BLOCK, columns), bf16),
        ),
        in_specs=[
            pl.BlockSpec(memory_space=pltpu.SMEM),
            vmem_spec,
            vmem_spec,
            pl.BlockSpec(memory_space=pl.ANY),
        ],
        out_specs=(vmem_spec, vmem_spec),
        scratch_shapes=[
            pltpu.VMEM((8, 4, BLOCK, columns), bf16),
            pltpu.VMEM((8, 4, BLOCK, columns), bf16),
            pltpu.VMEM((2, BLOCK, 16 * BLOCK), f32),
            *sum_landings(columns),
            pltpu.SemaphoreType.DMA((16,)),
            pltpu.SemaphoreType.DMA((16,)),
            pltpu.SemaphoreType.DMA,
        ],
        compiler_params=pltpu.CompilerParams(
            collective_id=3, has_side_effects=True, vmem_limit_bytes=VMEM_BYTES
        ),
        name="attend_back",
    )(starts, q, d_o, kva)


AXIS_ORDERS = (("dp_0", "seq", "head"), ("seq", "head", "dp_0"), ("head", "dp_0", "seq"))
CHIP_AXES = ("dp_0", "seq", "head")


class RingSum:
    def __init__(self, copies, base, axis, part, half_land, full_land):
        self.c = copies
        self.base = base
        self.axis = axis
        self.part = part
        self.hl = half_land
        self.fl = full_land
        self.i = lax.axis_index(axis)

    def step1(self):
        far = self.part.at[shift(self.i, 2)]
        self.a = self.c.start(self.base, far.at[pl.ds(0, 2)], self.hl.at[0], self.axis, 1)
        self.b = self.c.start(self.base + 1, far.at[pl.ds(2, 2)], self.hl.at[1], self.axis, -1)

    def step2(self):
        for copy, by, side in ((self.a, 1, 0), (self.b, -1, 1)):
            copy.wait_recv()
            block = self.part.at[shift(self.i, by)]
            half = block.at[pl.ds(2 * side, 2)]
            half[...] = (half[...].astype(f32) + self.hl[side].astype(f32)).astype(bf16)
            new = self.c.start(self.base + 2 + side, block, self.fl.at[side], self.axis, by)
            if side == 0:
                self.a = new
            else:
                self.b = new

    def finish(self):
        self.a.wait_recv()
        self.b.wait_recv()
        own = self.part.at[self.i]
        own[...] = (
            own[...].astype(f32) + self.fl[0].astype(f32) + self.fl[1].astype(f32)
        ).astype(bf16)
        return own


def projections_kernel(
    h1_ref, da_ref, dqkv_ref, mix_ref, gain_ref, out_ref, gain_out, *scratch
):
    (h1c, dac, dqc, mxc, gsum) = scratch[:5]
    parts = scratch[5:8]
    half1, full1, half2, full2, last = (scratch[8 + 3 * k : 11 + 3 * k] for k in range(5))
    send, recv = scratch[23:]
    tokens = h1_ref.shape[0]
    copies = Copies(send, recv)
    barrier = pltpu.get_barrier_semaphore()
    core = lax.axis_index("dp_1")
    other = 1 - core
    for axis in CHIP_AXES:
        for by in (1, 2, 3):
            pl.semaphore_signal(
                barrier,
                inc=1,
                device_id={axis: shift(lax.axis_index(axis), by)},
                device_id_type=MESH,
            )
    pl.semaphore_signal(barrier, inc=1, device_id={"dp_1": other}, device_id_type=MESH)
    pl.semaphore_wait(barrier, 10)

    def to_other(slot, src, dst):
        copy = pltpu.make_async_remote_copy(
            src_ref=src,
            dst_ref=dst,
            send_sem=send.at[slot],
            recv_sem=recv.at[slot],
            device_id={"dp_1": other},
            device_id_type=MESH,
        )
        copy.start()
        copies.started.append(copy)
        return copy

    mine, theirs = pl.ds(0, tokens), pl.ds(tokens, tokens)

    def piece(z, which):
        return pl.ds(pl.multiple_of(z * 512 + which * 256, 256), 256)

    moves = [
        to_other(0, dqkv_ref, dqc.at[theirs]),
        to_other(1, mix_ref, mxc.at[theirs]),
    ]
    for z in range(4):
        cols = pl.ds(z * 256, 256)
        moves.append(to_other(2 + 2 * z, h1_ref.at[:, piece(z, other)], h1c.at[theirs, cols]))
        moves.append(to_other(3 + 2 * z, da_ref.at[:, piece(z, other)], dac.at[theirs, cols]))
    gain_move = to_other(10, gain_ref, gsum.at[3, core])
    for z in range(4):
        cols = pl.ds(z * 256, 256)
        h1c[mine, cols] = h1_ref[:, piece(z, core)]
        dac[mine, cols] = da_ref[:, piece(z, core)]
    dqc[mine] = dqkv_ref[...]
    mxc[mine] = mix_ref[...]
    for move in moves:
        move.wait_recv()

    widths = [part.shape[4] for part in parts]
    split = dqkv_ref.shape[1] - widths[0]
    sources = (
        ((h1c, dqc, 0, widths[0], 0),),
        ((h1c, dqc, widths[0], split, 0), (dac, mxc, 0, widths[1] - split, split)),
        ((dac, mxc, widths[1] - split, widths[2], 0),),
    )

    @pl.loop(0, 4)
    def _(z):
        cols = pl.ds(pl.multiple_of(z * 256, 256), 256)
        for k in range(3):
            for lhs, rhs, first, width, place in sources[k]:
                value = tn(lhs[:, cols], rhs[:, first : first + width]).astype(bf16)
                value = value.reshape(4, 4, 16, width)
                to = slice(place, place + width)
                if k == 0:
                    parts[0][z, :, :, :, to] = value
                elif k == 1:
                    parts[1][:, :, z, :, to] = value
                else:
                    for y in range(4):
                        parts[2][:, z, y, :, to] = value[y]

    def gain_step(k, axis, value):
        i = lax.axis_index(axis)
        gsum[k, i] = value
        out = []
        for n, by in enumerate((1, 2, 3)):
            src = gsum.at[k, i]
            out.append(copies.start(11 + 3 * k + n, src, src, axis, by))
        return out

    def gain_total(k, moves):
        for move in moves:
            move.wait_recv()
        return gsum[k, 0] + gsum[k, 1] + gsum[k, 2] + gsum[k, 3]

    base = 20
    rings = [
        RingSum(copies, base + 4 * k, AXIS_ORDERS[k][0], parts[k], half1[k], full1[k])
        for k in range(3)
    ]
    for ring in rings:
        ring.step1()
    gain_move.wait_recv()
    gsum[3, core] = gain_ref[...]
    total = gsum[3, 0] + gsum[3, 1]
    gmoves = gain_step(0, CHIP_AXES[0], total)
    for ring in rings:
        ring.step2()
    gmoves = gain_step(1, CHIP_AXES[1], gain_total(0, gmoves))
    owns = [ring.finish() for ring in rings]
    rings = [
        RingSum(copies, base + 12 + 4 * k, AXIS_ORDERS[k][1], owns[k], half2[k], full2[k])
        for k in range(3)
    ]
    for ring in rings:
        ring.step1()
    gmoves = gain_step(2, CHIP_AXES[2], gain_total(1, gmoves))
    for ring in rings:
        ring.step2()
    gain_out[...] = gain_total(2, gmoves)
    owns = [ring.finish() for ring in rings]
    ends = []
    for k in range(3):
        axis = AXIS_ORDERS[k][2]
        i = lax.axis_index(axis)
        for n, by in enumerate((1, 2, 3)):
            ends.append(
                copies.start(
                    base + 24 + 3 * k + n, owns[k].at[shift(i, by)], last[k].at[n], axis, by
                )
            )
    for end in ends:
        end.wait_recv()
    place = 0
    for k in range(3):
        i = lax.axis_index(AXIS_ORDERS[k][2])
        value = owns[k][i].astype(f32)
        for n in range(3):
            value = value + last[k][n].astype(f32)
        out_ref[:, place : place + widths[k]] = value
        place += widths[k]
    copies.finish()


def projections(h1, d_attn, d_qkv, mixed, gains):
    tokens, qkv_width = d_qkv.shape
    columns = qkv_width + mixed.shape[1]
    widths = (1536, 1536, columns - 3072)
    vmem_spec = pl.BlockSpec(memory_space=pltpu.VMEM)
    rows = h1.shape[1] // 2

    def each(make):
        return [pltpu.VMEM(make(width), bf16) for width in widths]

    return pl.pallas_call(
        projections_kernel,
        out_shape=(
            jax.ShapeDtypeStruct((16, columns), f32),
            jax.ShapeDtypeStruct(gains.shape, f32),
        ),
        in_specs=[vmem_spec] * 5,
        out_specs=(vmem_spec, vmem_spec),
        scratch_shapes=[
            pltpu.VMEM((2 * tokens, rows), bf16),
            pltpu.VMEM((2 * tokens, rows), bf16),
            pltpu.VMEM((2 * tokens, qkv_width), bf16),
            pltpu.VMEM((2 * tokens, mixed.shape[1]), bf16),
            pltpu.VMEM((4, 4, *gains.shape), f32),
            *each(lambda w: (4, 4, 4, 16, w)),
            *each(lambda w: (2, 2, 4, 16, w)),
            *each(lambda w: (2, 4, 4, 16, w)),
            *each(lambda w: (2, 2, 16, w)),
            *each(lambda w: (2, 4, 16, w)),
            *each(lambda w: (3, 16, w)),
            pltpu.SemaphoreType.DMA((53,)),
            pltpu.SemaphoreType.DMA((53,)),
        ],
        compiler_params=pltpu.CompilerParams(
            collective_id=4, has_side_effects=True, vmem_limit_bytes=VMEM_BYTES
        ),
        name="projections",
    )(h1, d_attn, d_qkv, mixed, gains)


def rms_parts(v):
    inverse = lax.rsqrt(jnp.mean(v * v, axis=-1, keepdims=True) + EPS)
    return (v * inverse, inverse)


def rms_back(grad, normed, inverse):
    return inverse * (grad - normed * jnp.mean(grad * normed, axis=-1, keepdims=True))


def rotate(v, cosine, sine):
    half = v.shape[-1] // 2
    first = v[..., :half]
    second = v[..., half:]
    return jnp.concatenate([first * cosine - second * sine, second * cosine + first * sine], -1)


def angle_tables(positions, width):
    half = width // 2
    freq = jnp.exp(jnp.arange(half, dtype=f32) * (-2.0 * math.log(10000.0) / width))
    angle = positions.astype(f32)[:, None] * freq[None, :]
    return (jnp.cos(angle), jnp.sin(angle))


def body(
    tokens, w_qkv, w_out, w_ffn_in, w_ffn_out, g_attn, g_ffn, q_gain, k_gain, doc_starts, d_out
):
    rows, tok, width = tokens.shape
    count = rows * tok
    n_seq = lax.axis_size("seq")
    n_head = lax.axis_size("head")
    span = tok * n_head
    seq_index = lax.axis_index("seq")
    head_index = lax.axis_index("head")
    tok_pos = seq_index * span + head_index * tok + jnp.arange(tok)
    cosine, sine = angle_tables(tok_pos, HD)
    cosine = cosine[None, :, None, :]
    sine = sine[None, :, None, :]
    dy_all = lax.all_gather(d_out[None], ("seq", "head"), axis=0, tiled=True)
    dy_all = dy_all.reshape(n_seq, n_head, rows, tok, width)
    w_in = w_ffn_in.transpose(1, 0, 2).reshape(-1, width)
    xf = tokens.reshape(count, width).astype(f32)
    dy = d_out.reshape(count, width).astype(f32)
    n1, inv1 = rms_parts(xf)
    h1 = (n1 * g_attn).astype(bf16)
    qkv = jnp.dot(h1, w_qkv, preferred_element_type=f32)
    q_raw = qkv[..., : HEADS * HD].reshape(rows, tok, HEADS, HD)
    k_raw = qkv[..., HEADS * HD : (HEADS + KV) * HD].reshape(rows, tok, KV, HD)
    v_raw = qkv[..., (HEADS + KV) * HD :].reshape(rows, tok, KV, HD)
    q_normed, inv_q = rms_parts(q_raw)
    k_normed, inv_k = rms_parts(k_raw)
    q_rot = rotate(q_normed * q_gain, cosine, sine).astype(bf16).reshape(count, HEADS * HD)
    k_rot = rotate(k_normed * k_gain, cosine, sine)
    kv = jnp.concatenate([k_rot, v_raw], -1).astype(bf16).reshape(rows, tok, KV * 2 * HD)
    mixed, kva = attend(doc_starts, q_rot, kv)
    attn = jnp.dot(mixed, w_out, preferred_element_type=f32)
    r1 = xf + attn
    n2, inv2 = rms_parts(r1)
    h2 = (n2 * g_ffn).astype(bf16)
    outp, d_h2, grad_in, grad_down = ffn(h2.reshape(rows, tok, width), dy_all, w_in, w_ffn_out)
    d_h2 = d_h2.reshape(count, width)
    ffn_sum = lax.psum_scatter(
        outp.reshape(n_seq * n_head * count, width), ("seq", "head"), scatter_dimension=0, tiled=True
    )
    grad_in_sum, grad_down_sum = (
        lax.psum(grad_in, DP).astype(f32),
        lax.psum(grad_down, DP).astype(f32),
    )
    grad_in_sum = grad_in_sum.reshape(2, -1, width).transpose(1, 0, 2)
    grad_gffn = jnp.sum(d_h2 * n2, axis=0)
    d_r1 = dy + rms_back(d_h2 * g_ffn, n2, inv2)
    d_attn = d_r1.astype(bf16)
    d_o = lax.dot_general(
        d_attn, w_out, (((1,), (1,)), ((), ())), preferred_element_type=f32
    ).astype(bf16)
    d_q, d_kv = attend_back(doc_starts, q_rot, d_o, kva)
    d_qrot = d_q.reshape(rows, tok, HEADS, HD).astype(f32)
    d_kv = d_kv.reshape(rows, tok, KV, 2 * HD)
    d_krot = d_kv[..., :HD].astype(f32)
    d_vraw = d_kv[..., HD:]
    d_qs = rotate(d_qrot, cosine, -sine)
    d_ks = rotate(d_krot, cosine, -sine)
    grad_qgain = jnp.sum(d_qs * q_normed, axis=(0, 1, 2))
    grad_kgain = jnp.sum(d_ks * k_normed, axis=(0, 1, 2))
    d_qraw = rms_back(d_qs * q_gain, q_normed, inv_q)
    d_kraw = rms_back(d_ks * k_gain, k_normed, inv_k)
    d_qkv = jnp.concatenate(
        [
            d_qraw.astype(bf16).reshape(count, HEADS * HD),
            d_kraw.astype(bf16).reshape(count, KV * HD),
            d_vraw.reshape(count, KV * HD),
        ],
        -1,
    )
    d_h1 = lax.dot_general(
        d_qkv, w_qkv, (((1,), (1,)), ((), ())), preferred_element_type=f32
    )
    grad_gattn = jnp.sum(d_h1 * n1, axis=0)
    grad_x = (d_r1 + rms_back(d_h1 * g_attn, n1, inv1)).astype(bf16)
    gains = jnp.concatenate([grad_gattn, grad_gffn, grad_qgain, grad_kgain])
    gains = jnp.pad(gains, (0, 40 * 128 - gains.shape[0])).reshape(40, 128)
    weight_part, gains = projections(h1, d_attn, d_qkv, mixed, gains)
    gains = gains.reshape(-1)
    output = (r1 + ffn_sum.astype(f32)).astype(bf16)
    qkv_width = w_qkv.shape[1]
    return (
        output.reshape(rows, tok, width),
        grad_x.reshape(rows, tok, width),
        weight_part[:, :qkv_width],
        weight_part[:, qkv_width:].T,
        grad_in_sum,
        grad_down_sum,
        gains[:width],
        gains[width : 2 * width],
        gains[2 * width : 2 * width + HD],
        gains[2 * width + HD : 2 * width + 2 * HD],
    )


def solution(mesh):
    split = Mesh(
        mesh.devices.reshape(4, 2, mesh.shape["seq"], mesh.shape["head"]),
        ("dp_0", "dp_1", "seq", "head"),
    )
    return jax.shard_map(
        body,
        mesh=split,
        in_specs=(
            P(DP, ("seq", "head"), None),
            P(),
            P(),
            P(("seq", "head"), None, None),
            P(("seq", "head"), None),
            P(),
            P(),
            P(),
            P(),
            P(DP, None),
            P(DP, ("seq", "head"), None),
        ),
        out_specs=(
            P(DP, ("seq", "head"), None),
            P(DP, ("seq", "head"), None),
            P(DP_SEQ_HEAD, None),
            P(None, DP_SEQ_HEAD),
            P(("seq", "head"), None, None),
            P(("seq", "head"), None),
            P(),
            P(),
            P(),
            P(),
        ),
        check_vma=False,
    )
```

```python
import functools
import math

import jax
import jax.numpy as jnp
from jax import lax
from jax.experimental import pallas as pl
from jax.experimental.pallas import tpu as pltpu
from jax.sharding import Mesh
from jax.sharding import PartitionSpec as P

HEADS = 28
KV = 7
HD = 64
PER_GROUP = HEADS // KV
DP_SEQ_HEAD = ("dp_0", "dp_1", "seq", "head")
DP = ("dp_0", "dp_1")
RING = 4
BLOCK = 64
MESH = pl.DeviceIdType.MESH
EPS = 1e-06
SCALE = 0.125
f32 = jnp.float32
bf16 = jnp.bfloat16
VMEM_BYTES = 62 * 2**20


def nt(a, b):
    return lax.dot_general(a, b, (((1,), (1,)), ((), ())), preferred_element_type=f32)


def nn(a, b):
    return lax.dot_general(a, b, (((1,), (0,)), ((), ())), preferred_element_type=f32)


def tn(a, b):
    return lax.dot_general(a, b, (((0,), (0,)), ((), ())), preferred_element_type=f32)


def shift(index, by):
    return lax.rem(index + (by + RING), RING)


def barrier_with(axes, core=False):
    barrier = pltpu.get_barrier_semaphore()
    for axis in axes:
        index = lax.axis_index(axis)
        for by in (1, -1):
            pl.semaphore_signal(
                barrier, inc=1, device_id={axis: shift(index, by)}, device_id_type=MESH
            )
    if core:
        other = 1 - lax.axis_index("dp_1")
        pl.semaphore_signal(barrier, inc=1, device_id={"dp_1": other}, device_id_type=MESH)
    pl.semaphore_wait(barrier, 2 * len(axes) + int(core))


class Copies:
    def __init__(self, send, recv):
        self.send = send
        self.recv = recv
        self.started = []

    def start(self, slot, src, dst, axis, by):
        copy = pltpu.make_async_remote_copy(
            src_ref=src,
            dst_ref=dst,
            send_sem=self.send.at[slot],
            recv_sem=self.recv.at[slot],
            device_id={axis: shift(lax.axis_index(axis), by)},
            device_id_type=MESH,
        )
        copy.start()
        self.started.append(copy)
        return copy

    def start_to_core(self, slot, src, dst):
        copy = pltpu.make_async_remote_copy(
            src_ref=src,
            dst_ref=dst,
            send_sem=self.send.at[slot],
            recv_sem=self.recv.at[slot],
            device_id={"dp_1": 1 - lax.axis_index("dp_1")},
            device_id_type=MESH,
        )
        copy.start()
        self.started.append(copy)
        return copy

    def finish(self):
        for copy in self.started:
            copy.wait_send()


INNER = ("head", "seq")
GROUP = ("seq", "head")


class PlaneGather:
    def __init__(self, copies, base, half, own, buf):
        self.c = copies
        self.base = base + 8 * half
        self.half = half
        self.own = own
        self.buf = buf
        self.i = lax.axis_index(INNER[half])
        self.g = lax.axis_index(GROUP[half])

    def row(self, by=0):
        return 4 * self.half + shift(self.g, by)

    def step1(self):
        ax = INNER[self.half]
        dst = self.buf.at[self.row(), self.i]
        self.a = self.c.start(self.base, self.own, dst, ax, 1)
        self.b = self.c.start(self.base + 1, self.own, dst, ax, -1)

    def step2(self):
        ax = INNER[self.half]
        n = self.buf.shape[2] // 2
        self.a.wait_recv()
        left = self.buf.at[self.row(), shift(self.i, -1), pl.ds(0, n)]
        self.a = self.c.start(self.base + 2, left, left, ax, 1)
        self.b.wait_recv()
        right = self.buf.at[self.row(), shift(self.i, 1), pl.ds(n, n)]
        self.b = self.c.start(self.base + 3, right, right, ax, -1)

    def step3(self):
        ax = GROUP[self.half]
        self.a.wait_recv()
        self.b.wait_recv()
        rows = self.buf.at[self.row()]
        self.a = self.c.start(self.base + 4, rows, rows, ax, 1)
        self.b = self.c.start(self.base + 5, rows, rows, ax, -1)

    def step4(self):
        ax = GROUP[self.half]
        self.a.wait_recv()
        left = self.buf.at[self.row(-1), pl.ds(0, 2)]
        self.a = self.c.start(self.base + 6, left, left, ax, 1)
        self.b.wait_recv()
        right = self.buf.at[self.row(1), pl.ds(2, 2)]
        self.b = self.c.start(self.base + 7, right, right, ax, -1)

    def finish(self):
        self.a.wait_recv()
        self.b.wait_recv()


class PlaneSum:
    def __init__(self, copies, base, half, part, land1, land2, land3, land4):
        self.c = copies
        self.base = base + 8 * half
        self.half = half
        self.part = part
        self.l1, self.l2, self.l3, self.l4 = (
            ref.at[half] for ref in (land1, land2, land3, land4)
        )
        self.i = lax.axis_index(INNER[half])
        self.g = lax.axis_index(GROUP[half])

    def row(self, by=0):
        return 4 * self.half + shift(self.g, by)

    def add(self, ref, other):
        ref[...] = (ref[...].astype(f32) + other[...].astype(f32)).astype(ref.dtype)

    def step1(self):
        ax = GROUP[self.half]
        row = self.row(2)
        self.a = self.c.start(self.base, self.part.at[row, pl.ds(0, 2)], self.l1.at[0], ax, 1)
        self.b = self.c.start(self.base + 1, self.part.at[row, pl.ds(2, 2)], self.l1.at[1], ax, -1)

    def step2(self):
        ax = GROUP[self.half]
        self.a.wait_recv()
        self.add(self.part.at[self.row(1), pl.ds(0, 2)], self.l1.at[0])
        self.a = self.c.start(self.base + 2, self.part.at[self.row(1)], self.l2.at[0], ax, 1)
        self.b.wait_recv()
        self.add(self.part.at[self.row(-1), pl.ds(2, 2)], self.l1.at[1])
        self.b = self.c.start(self.base + 3, self.part.at[self.row(-1)], self.l2.at[1], ax, -1)

    def step3(self):
        ax = INNER[self.half]
        n = self.part.shape[2] // 2
        self.a.wait_recv()
        self.b.wait_recv()
        rows = self.part.at[self.row()]
        rows[...] = (
            rows[...].astype(f32) + self.l2[0].astype(f32) + self.l2[1].astype(f32)
        ).astype(rows.dtype)
        block = self.part.at[self.row(), shift(self.i, 2)]
        self.a = self.c.start(self.base + 4, block.at[pl.ds(0, n)], self.l3.at[0], ax, 1)
        self.b = self.c.start(self.base + 5, block.at[pl.ds(n, n)], self.l3.at[1], ax, -1)

    def step4(self):
        ax = INNER[self.half]
        n = self.part.shape[2] // 2
        self.a.wait_recv()
        right = self.part.at[self.row(), shift(self.i, 1)]
        self.add(right.at[pl.ds(0, n)], self.l3.at[0])
        self.a = self.c.start(self.base + 6, right, self.l4.at[0], ax, 1)
        self.b.wait_recv()
        left = self.part.at[self.row(), shift(self.i, -1)]
        self.add(left.at[pl.ds(n, n)], self.l3.at[1])
        self.b = self.c.start(self.base + 7, left, self.l4.at[1], ax, -1)

    def result(self):
        self.a.wait_recv()
        self.b.wait_recv()
        own = self.part[self.row(), self.i].astype(f32)
        return own + self.l4[0].astype(f32) + self.l4[1].astype(f32)


def sum_landings(columns):
    return [
        pltpu.VMEM((2, 2, 2, BLOCK, columns), bf16),
        pltpu.VMEM((2, 2, 4, BLOCK, columns), bf16),
        pltpu.VMEM((2, 2, BLOCK // 2, columns), bf16),
        pltpu.VMEM((2, 2, BLOCK, columns), bf16),
    ]


class RingSum:
    def __init__(self, copies, base, axis, part, half_land, full_land):
        self.c = copies
        self.base = base
        self.axis = axis
        self.part = part
        self.hl = half_land
        self.fl = full_land
        self.i = lax.axis_index(axis)

    def step1(self):
        far = self.part.at[shift(self.i, 2)]
        n = far.shape[0] // 2
        self.a = self.c.start(self.base, far.at[pl.ds(0, n)], self.hl.at[0], self.axis, 1)
        self.b = self.c.start(self.base + 1, far.at[pl.ds(n, n)], self.hl.at[1], self.axis, -1)

    def step2(self):
        for copy, by, side in ((self.a, 1, 0), (self.b, -1, 1)):
            copy.wait_recv()
            block = self.part.at[shift(self.i, by)]
            n = block.shape[0] // 2
            half = block.at[pl.ds(n * side, n)]
            half[...] = (half[...].astype(f32) + self.hl[side].astype(f32)).astype(bf16)
            new = self.c.start(self.base + 2 + side, block, self.fl.at[side], self.axis, by)
            if side == 0:
                self.a = new
            else:
                self.b = new

    def finish(self):
        self.a.wait_recv()
        self.b.wait_recv()
        own = self.part.at[self.i]
        own[...] = (
            own[...].astype(f32) + self.fl[0].astype(f32) + self.fl[1].astype(f32)
        ).astype(bf16)
        return own


class RingGather:
    def __init__(self, copies, base, axis, full):
        self.c = copies
        self.base = base
        self.axis = axis
        self.full = full
        self.i = lax.axis_index(axis)

    def step1(self):
        own = self.full.at[self.i]
        self.a = self.c.start(self.base, own, own, self.axis, 1)
        self.b = self.c.start(self.base + 1, own, own, self.axis, -1)

    def step2(self):
        n = self.full.shape[1] // 2
        self.a.wait_recv()
        left = self.full.at[shift(self.i, -1), pl.ds(0, n)]
        self.a = self.c.start(self.base + 2, left, left, self.axis, 1)
        self.b.wait_recv()
        right = self.full.at[shift(self.i, 1), pl.ds(n, n)]
        self.b = self.c.start(self.base + 3, right, right, self.axis, -1)

    def finish(self):
        self.a.wait_recv()
        self.b.wait_recv()


def ffn_kernel(
    h2_ref,
    dy_ref,
    win_ref,
    wdn_ref,
    outp_ref,
    dh2_ref,
    gsum_ref,
    h2a,
    dya,
    pairs,
    win,
    wdn,
    hid,
    dbo,
    dpt,
    l1,
    l2,
    l3,
    l4,
    stage,
    gst,
    gland,
    send,
    recv,
    lsem,
    osem,
):
    units = wdn.shape[0]
    width = wdn.shape[1]
    copies = Copies(send, recv)
    weights = [
        pltpu.make_async_copy(win_ref.at[pl.ds(0, units // 2)], pairs, lsem.at[0]),
        pltpu.make_async_copy(win_ref.at[pl.ds(units // 2, units // 2)], pairs, lsem.at[4]),
        pltpu.make_async_copy(wdn_ref, wdn, lsem.at[1]),
    ]
    weights[0].start()
    weights[2].start()
    load = pltpu.make_async_copy(dy_ref, dya, lsem.at[2])
    load.start()
    barrier_with(("seq", "head"), core=True)
    gathers = [PlaneGather(copies, 0, half, h2_ref.at[half], h2a) for half in (0, 1)]
    for gather in gathers:
        gather.step1()
    for half in (0, 1):
        h2a[gathers[half].row(), gathers[half].i] = h2_ref[half]

    def split_pairs(first):
        win[first : first + units // 2] = pairs[:, 0, :]
        win[units + first : units + first + units // 2] = pairs[:, 1, :]

    weights[0].wait()
    split_pairs(0)
    weights[1].start()
    for gather in gathers:
        gather.step2()
    weights[1].wait()
    split_pairs(units // 2)
    weights[2].wait()
    load.wait()
    for gather in gathers:
        gather.step3()
    seq, head = lax.axis_index("seq"), lax.axis_index("head")

    def group(half, by):
        return 4 * half + lax.rem(seq + half * (head - seq) + by + 4, 4)

    def rows_of(ref, q):
        return ref[q].reshape(4 * BLOCK, width)

    def columns_of(q):
        return pl.ds(pl.multiple_of(q * 4 * BLOCK, 4 * BLOCK), 4 * BLOCK)

    def forward(q):
        both = nt(win[...], rows_of(h2a, q))
        d_hidden = nt(wdn[...], rows_of(dya, q))
        gate = both[:units]
        up = both[units:]
        sig = 1.0 / (1.0 + jnp.exp(-gate))
        act = gate * sig
        cols = columns_of(q)
        hid[:, cols] = (act * up).astype(bf16)
        dbo[:units, cols] = (d_hidden * up * (sig * (1.0 + gate * (1.0 - sig)))).astype(bf16)
        dbo[units:, cols] = (d_hidden * act).astype(bf16)

    def back(q):
        value = tn(dbo[:, columns_of(q)], win[...])
        dpt[q] = value.astype(bf16).reshape(4, BLOCK, width)

    @pl.loop(0, 2)
    def _(half):
        forward(group(half, 0))

    for gather in gathers:
        gather.step4()

    @pl.loop(0, 4)
    def _(k):
        forward(group(lax.div(k, 2), 1 - 2 * lax.rem(k, 2)))

    for gather in gathers:
        gather.finish()

    @pl.loop(0, 2)
    def _(half):
        forward(group(half, 2))
        back(group(half, 2))

    sums = [PlaneSum(copies, 16, half, dpt, l1, l2, l3, l4) for half in (0, 1)]
    for total in sums:
        total.step1()

    @pl.loop(0, 4)
    def _(k):
        back(group(lax.div(k, 2), 1 - 2 * lax.rem(k, 2)))

    for total in sums:
        total.step2()

    @pl.loop(0, 2)
    def _(half):
        back(group(half, 0))

    tile = gland.shape[2]
    half_rows = gland.shape[1]
    tokens = 8 * 4 * BLOCK
    core = lax.axis_index("dp_1")
    mine = pl.ds(pl.multiple_of(core * half_rows, 16), half_rows)
    theirs = pl.ds(pl.multiple_of((1 - core) * half_rows, 16), half_rows)
    swaps = []
    for n in range(gland.shape[0]):
        cols = pl.ds(n * tile, tile)
        gst[n, : 2 * units] = nn(dbo[...], h2a[:, :, :, cols].reshape(tokens, tile)).astype(bf16)
        gst[n, 2 * units :] = nn(hid[...], dya[:, :, :, cols].reshape(tokens, tile)).astype(bf16)
        swaps.append(
            copies.start_to_core(32 + n, gst.at[n, theirs], gland.at[n])
        )
    for total in sums:
        total.step3()

    def out_copy(q):
        slot = q % 2
        place = outp_ref.at[q, :, 0] if q < 4 else outp_ref.at[:, q - 4, 1]
        return pltpu.make_async_copy(stage.at[slot], place, osem.at[slot])

    def out_part(q):
        if q >= 2:
            out_copy(q - 2).wait()
        value = tn(hid[:, pl.ds(q * 4 * BLOCK, 4 * BLOCK)], wdn[...])
        stage[q % 2] = value.astype(bf16).reshape(4, BLOCK, width)
        out_copy(q).start()

    for q in range(4):
        out_part(q)
    for total in sums:
        total.step4()
    for q in range(4, 8):
        out_part(q)
    for half in (0, 1):
        dh2_ref[half] = sums[half].result()
    for n, swap in enumerate(swaps):
        swap.wait_recv()
        gland[n] = (gst[n, mine].astype(f32) + gland[n].astype(f32)).astype(bf16)
    keep = pltpu.make_async_copy(gland, gsum_ref, lsem.at[3])
    keep.start()
    out_copy(6).wait()
    out_copy(7).wait()
    keep.wait()
    copies.finish()


def ffn(h2, dy_all, w_in, w_down):
    units, width = w_down.shape
    tokens = 32 * BLOCK
    tile = 512
    any_spec = pl.BlockSpec(memory_space=pl.ANY)
    vmem_spec = pl.BlockSpec(memory_space=pltpu.VMEM)
    return pl.pallas_call(
        ffn_kernel,
        out_shape=(
            jax.ShapeDtypeStruct((4, 4, 2, BLOCK, width), bf16),
            jax.ShapeDtypeStruct((2, BLOCK, width), f32),
            jax.ShapeDtypeStruct((width // tile, 3 * units // 2, tile), bf16),
        ),
        in_specs=[vmem_spec, any_spec, any_spec, any_spec],
        out_specs=(any_spec, vmem_spec, any_spec),
        scratch_shapes=[
            pltpu.VMEM((8, 4, BLOCK, width), bf16),
            pltpu.VMEM((8, 4, BLOCK, width), bf16),
            pltpu.VMEM((units // 2, 2, width), bf16),
            pltpu.VMEM((2 * units, width), bf16),
            pltpu.VMEM((units, width), bf16),
            pltpu.VMEM((units, tokens), bf16),
            pltpu.VMEM((2 * units, tokens), bf16),
            pltpu.VMEM((8, 4, BLOCK, width), bf16),
            *sum_landings(width),
            pltpu.VMEM((2, 4, BLOCK, width), bf16),
            pltpu.VMEM((width // tile, 3 * units, tile), bf16),
            pltpu.VMEM((width // tile, 3 * units // 2, tile), bf16),
            pltpu.SemaphoreType.DMA((36,)),
            pltpu.SemaphoreType.DMA((36,)),
            pltpu.SemaphoreType.DMA((5,)),
            pltpu.SemaphoreType.DMA((2,)),
        ],
        compiler_params=pltpu.CompilerParams(
            collective_id=1, has_side_effects=True, vmem_limit_bytes=VMEM_BYTES
        ),
        name="ffn",
    )(h2, dy_all, w_in, w_down)


def mask_rows(starts_ref, row, transposed, mask_ref):
    seq, head = lax.axis_index("seq"), lax.axis_index("head")
    keys = 16 * BLOCK
    index = lax.broadcasted_iota(jnp.int32, (1, keys), 1)
    if transposed:
        group = lax.div(index, 4 * BLOCK)
        inner = lax.rem(lax.div(index, BLOCK), 4)
        k_pos = (inner * 4 + group) * BLOCK + lax.rem(index, BLOCK)
    else:
        k_pos = index
    first = (seq * 4 + head) * BLOCK
    q_pos = first + lax.broadcasted_iota(jnp.int32, (BLOCK, 1), 0)
    k_doc = jnp.zeros((1, keys), jnp.int32)
    q_doc = jnp.zeros((BLOCK, 1), jnp.int32)
    for d in range(starts_ref.shape[1]):
        start = starts_ref[row, d]
        k_doc += (start <= k_pos).astype(jnp.int32)
        q_doc += (start <= q_pos).astype(jnp.int32)
    seen = (k_pos <= q_pos) & (k_doc == q_doc)
    mask_ref[row] = seen.astype(f32)


LOG2E_SCALE = SCALE * math.log2(math.e)


def stacked(block, where):
    rows = jnp.concatenate([block[:, h * HD : (h + 1) * HD] for h in range(PER_GROUP)], 0)
    zero = jnp.zeros_like(rows)
    return jnp.concatenate([rows, zero] if where == 0 else [zero, rows], 1)


def unstacked(rows):
    return jnp.concatenate([rows[h * BLOCK : (h + 1) * BLOCK] for h in range(PER_GROUP)], 1)


def weights_of(q_rows, kv_rows, mask):
    scores = nt(q_rows, kv_rows)
    keys = kv_rows.shape[0]
    e = jnp.exp2(scores * LOG2E_SCALE).reshape(PER_GROUP, BLOCK, keys) * mask[None]
    return e.reshape(PER_GROUP * BLOCK, keys)


GROUP_COLS = PER_GROUP * HD
KV_COLS = 2 * HD


def head_means(columns=GROUP_COLS):
    a = lax.div(lax.broadcasted_iota(jnp.int32, (columns, columns), 0), HD)
    b = lax.div(lax.broadcasted_iota(jnp.int32, (columns, columns), 1), HD)
    return jnp.where(a == b, 1.0 / HD, 0.0).astype(f32)


def head_mean(v, means):
    return jnp.dot(v, means, precision=lax.Precision.HIGHEST, preferred_element_type=f32)


def swapped(v):
    columns = v.shape[1]
    lane = lax.rem(lax.broadcasted_iota(jnp.int32, v.shape, 1), HD)
    up = pltpu.roll(v, columns - HD // 2, 1)
    down = pltpu.roll(v, HD // 2, 1)
    return jnp.where(lane < HD // 2, up, down)


def turned(raw, gain, cosine, sine, means):
    normed = raw * lax.rsqrt(head_mean(raw * raw, means) + EPS)
    v = normed * gain
    return v * cosine + swapped(v) * sine


def turned_back(grad, raw, gain, cosine, sine, means):
    inverse = lax.rsqrt(head_mean(raw * raw, means) + EPS)
    normed = raw * inverse
    u = grad * cosine - swapped(grad) * sine
    gain_grad = jnp.sum(u * normed, axis=0, keepdims=True)
    e = u * gain
    return inverse * (e - normed * head_mean(e * normed, means)), gain_grad


def rms_parts(v):
    inverse = lax.rsqrt(jnp.mean(v * v, axis=-1, keepdims=True) + EPS)
    return (v * inverse, inverse)


def rms_back(grad, normed, inverse):
    return inverse * (grad - normed * jnp.mean(grad * normed, axis=-1, keepdims=True))


def front_kernel(
    starts_ref,
    x_ref,
    wqkv_ref,
    wout_ref,
    ga_ref,
    gf_ref,
    qg_ref,
    kg_ref,
    cos_ref,
    sin_ref,
    dy_ref,
    h1_ref,
    raw_ref,
    q_ref,
    kva_ref,
    mixed_ref,
    r1_ref,
    h2_ref,
    dya_ref,
    wq,
    wkv,
    wo,
    own,
    kva,
    dya,
    qst,
    mask,
    oacc,
    lacc,
    send,
    recv,
    lsem,
):
    count, width = x_ref.shape
    q_cols = HEADS * HD
    k_cols = KV * HD
    loads = [
        pltpu.make_async_copy(wqkv_ref.at[:, pl.ds(q_cols, 2 * k_cols)], wkv, lsem.at[0]),
        pltpu.make_async_copy(wqkv_ref.at[:, pl.ds(0, q_cols)], wq, lsem.at[1]),
        pltpu.make_async_copy(wout_ref, wo, lsem.at[2]),
    ]
    for load in loads:
        load.start()
    copies = Copies(send, recv)
    barrier_with(("seq", "head"))
    cotangents = [PlaneGather(copies, 16, half, dy_ref.at[half], dya) for half in (0, 1)]
    for gather in cotangents:
        gather.step1()
    for half in (0, 1):
        dya[cotangents[half].row(), cotangents[half].i] = dy_ref[half]
    means = head_means()
    cosine, sine = cos_ref[...], sin_ref[...]
    x = x_ref[...].astype(f32)
    h1_ref[...] = (rms_parts(x)[0] * ga_ref[...]).astype(bf16)
    loads[0].wait()
    kv = nn(h1_ref[...], wkv[...])
    raw_ref[:, q_cols:] = kv
    keys = jnp.concatenate(
        [
            turned(kv[:, c : c + GROUP_COLS], kg_ref[...], cosine, sine, means)
            for c in (0, GROUP_COLS)
        ],
        1,
    )
    for g in range(KV):
        k = keys[:, g * HD : (g + 1) * HD]
        v = kv[:, k_cols + g * HD : k_cols + (g + 1) * HD]
        own[:, :, g * KV_COLS : (g + 1) * KV_COLS] = (
            jnp.concatenate([k, v], 1).astype(bf16).reshape(2, BLOCK, KV_COLS)
        )
    gathers = [PlaneGather(copies, 0, half, own.at[half], kva) for half in (0, 1)]
    for gather in gathers:
        gather.step1()
    for half in (0, 1):
        kva[gathers[half].row(), gathers[half].i] = own[half]
    for gather in cotangents:
        gather.step2()
    loads[1].wait()

    def queries(g):
        cols = slice(g * GROUP_COLS, (g + 1) * GROUP_COLS)
        raw = nn(h1_ref[...], wq[:, cols])
        raw_ref[:, cols] = raw
        q = turned(raw, qg_ref[...], cosine, sine, means).astype(bf16)
        q_ref[:, cols] = q
        for row in (0, 1):
            qst[row * KV + g] = stacked(q[row * BLOCK : (row + 1) * BLOCK], 0)

    for g in range(3):
        queries(g)
    for gather in gathers:
        gather.step2()
    for g in range(3, KV):
        queries(g)
    for gather in gathers:
        gather.step3()
    mask_rows(starts_ref, 0, False, mask)
    mask_rows(starts_ref, 1, True, mask)
    seq, head = lax.axis_index("seq"), lax.axis_index("head")

    def scored(row, by, first):
        group = lax.rem(seq + row * (head - seq) + by + 4, 4)
        seen = mask[row, :, pl.ds(pl.multiple_of(group * 4 * BLOCK, 4 * BLOCK), 4 * BLOCK)]
        for g in range(KV):
            index = row * KV + g
            kv_rows = kva[
                4 * row + group, :, :, g * KV_COLS : (g + 1) * KV_COLS
            ].reshape(4 * BLOCK, KV_COLS)
            e = weights_of(qst[index], kv_rows, seen)
            total = e[:, : 2 * BLOCK] + e[:, 2 * BLOCK :]
            mixed = nn(e.astype(bf16), kv_rows)
            if first:
                lacc[index] = total
                oacc[index] = mixed
            else:
                lacc[index] += total
                oacc[index] += mixed

    @pl.loop(0, 2)
    def _(row):
        scored(row, 0, True)

    for gather in gathers:
        gather.step4()
    for gather in cotangents:
        gather.step3()

    @pl.loop(0, 4)
    def _(k):
        scored(lax.div(k, 2), 1 - 2 * lax.rem(k, 2), False)

    for gather in gathers:
        gather.finish()
    keep = pltpu.make_async_copy(kva, kva_ref, lsem.at[3])
    keep.start()

    @pl.loop(0, 2)
    def _(row):
        scored(row, 2, False)

    for row in (0, 1):
        for g in range(KV):
            index = row * KV + g
            mixed = oacc[index][:, HD:] / jnp.sum(lacc[index], axis=1, keepdims=True)
            mixed_ref[
                row * BLOCK : (row + 1) * BLOCK, g * GROUP_COLS : (g + 1) * GROUP_COLS
            ] = unstacked(mixed.astype(bf16))
    loads[2].wait()
    tile = 512
    for n in range(width // tile):
        cols = slice(n * tile, (n + 1) * tile)
        r1_ref[:, cols] = x_ref[:, cols].astype(f32) + nn(mixed_ref[...], wo[:, cols])
    for gather in cotangents:
        gather.step4()
    h2_ref[...] = (rms_parts(r1_ref[...])[0] * gf_ref[...]).astype(bf16)
    keep.wait()
    for gather in cotangents:
        gather.finish()
    keep = pltpu.make_async_copy(dya, dya_ref, lsem.at[4])
    keep.start()
    keep.wait()
    copies.finish()


def front(starts, x, w_qkv, w_out, g_attn, g_ffn, q_gain, k_gain, cosine, sine, dy):
    count, width = x.shape
    q_cols = HEADS * HD
    kv_cols = 2 * KV * HD
    vmem_spec = pl.BlockSpec(memory_space=pltpu.VMEM)
    any_spec = pl.BlockSpec(memory_space=pl.ANY)
    return pl.pallas_call(
        front_kernel,
        out_shape=(
            jax.ShapeDtypeStruct((count, width), bf16),
            jax.ShapeDtypeStruct((count, q_cols + kv_cols), f32),
            jax.ShapeDtypeStruct((count, q_cols), bf16),
            jax.ShapeDtypeStruct((8, 4, BLOCK, kv_cols), bf16),
            jax.ShapeDtypeStruct((count, q_cols), bf16),
            jax.ShapeDtypeStruct((count, width), f32),
            jax.ShapeDtypeStruct((count, width), bf16),
            jax.ShapeDtypeStruct((8, 4, BLOCK, width), bf16),
        ),
        in_specs=[
            pl.BlockSpec(memory_space=pltpu.SMEM),
            vmem_spec,
            any_spec,
            any_spec,
            *[vmem_spec] * 7,
        ],
        out_specs=(
            vmem_spec,
            vmem_spec,
            vmem_spec,
            any_spec,
            vmem_spec,
            vmem_spec,
            vmem_spec,
            any_spec,
        ),
        scratch_shapes=[
            pltpu.VMEM((width, q_cols), bf16),
            pltpu.VMEM((width, kv_cols), bf16),
            pltpu.VMEM((q_cols, width), bf16),
            pltpu.VMEM((2, BLOCK, kv_cols), bf16),
            pltpu.VMEM((8, 4, BLOCK, kv_cols), bf16),
            pltpu.VMEM((8, 4, BLOCK, width), bf16),
            pltpu.VMEM((2 * KV, PER_GROUP * BLOCK, KV_COLS), bf16),
            pltpu.VMEM((2, BLOCK, 16 * BLOCK), f32),
            pltpu.VMEM((2 * KV, PER_GROUP * BLOCK, KV_COLS), f32),
            pltpu.VMEM((2 * KV, PER_GROUP * BLOCK, 2 * BLOCK), f32),
            pltpu.SemaphoreType.DMA((32,)),
            pltpu.SemaphoreType.DMA((32,)),
            pltpu.SemaphoreType.DMA((5,)),
        ],
        compiler_params=pltpu.CompilerParams(
            collective_id=2, has_side_effects=True, vmem_limit_bytes=VMEM_BYTES
        ),
        name="front",
    )(starts, x, w_qkv, w_out, g_attn, g_ffn, q_gain, k_gain, cosine, sine, dy)


def rear_kernel(
    starts_ref,
    dh2_ref,
    r1_ref,
    dy_ref,
    x_ref,
    q_ref,
    raw_ref,
    kva_ref,
    wqkv_ref,
    wout_ref,
    gsum_ref,
    ga_ref,
    gf_ref,
    qg_ref,
    kg_ref,
    cos_ref,
    sin_ref,
    da_ref,
    dqkv_ref,
    gx_ref,
    gga_ref,
    ggf_ref,
    gq_ref,
    gk_ref,
    gall_ref,
    wqkv,
    wo,
    kva,
    gsum,
    gfull,
    gl1,
    gl2,
    part,
    mask,
    d_r1,
    d_o,
    dq,
    d_h1,
    l1,
    l2,
    l3,
    l4,
    send,
    recv,
    lsem,
):
    count, width = x_ref.shape
    q_cols = HEADS * HD
    k_cols = KV * HD
    loads = [
        pltpu.make_async_copy(wout_ref, wo, lsem.at[0]),
        pltpu.make_async_copy(kva_ref, kva, lsem.at[1]),
        pltpu.make_async_copy(wqkv_ref, wqkv, lsem.at[2]),
        pltpu.make_async_copy(gsum_ref, gsum, lsem.at[3]),
    ]
    for load in loads:
        load.start()
    copies = Copies(send, recv)
    barrier_with(("dp_0", "seq", "head"))
    gring = RingSum(copies, 16, "dp_0", gsum, gl1, gl2)
    gback = RingGather(copies, 20, "dp_0", gfull)
    loads[3].wait()
    gring.step1()
    n2, inv2 = rms_parts(r1_ref[...])
    d_h2 = dh2_ref[...]
    ggf_ref[...] = jnp.sum(d_h2 * n2, axis=0, keepdims=True)
    d_r1[...] = dy_ref[...].astype(f32) + rms_back(d_h2 * gf_ref[...], n2, inv2)
    da_ref[...] = d_r1[...].astype(bf16)
    mask_rows(starts_ref, 0, False, mask)
    mask_rows(starts_ref, 1, True, mask)
    loads[0].wait()
    for g in range(KV):
        cols = slice(g * GROUP_COLS, (g + 1) * GROUP_COLS)
        d_o[:, cols] = nt(da_ref[...], wo[cols]).astype(bf16)
    loads[1].wait()
    gring.step2()
    sums = [PlaneSum(copies, 0, half, part, l1, l2, l3, l4) for half in (0, 1)]
    for row in (0, 1):
        rows = slice(row * BLOCK, (row + 1) * BLOCK)
        for g in range(KV):
            cols = slice(g * GROUP_COLS, (g + 1) * GROUP_COLS)
            lanes = slice(g * KV_COLS, (g + 1) * KV_COLS)
            q_rows = stacked(q_ref[rows, cols], 0)
            do_rows = stacked(d_o[rows, cols], 1)
            kv_rows = kva[4 * row : 4 * row + 4, :, :, lanes].reshape(16 * BLOCK, KV_COLS)
            e = weights_of(q_rows, kv_rows, mask[row])
            probs = e * (1.0 / jnp.sum(e, axis=1, keepdims=True))
            d_probs = nt(do_rows, kv_rows)
            delta = jnp.sum(probs * d_probs, axis=1, keepdims=True)
            d_scores = (probs * (d_probs - delta)).astype(bf16)
            dq_rows = nn(d_scores, kv_rows)[:, :HD] * SCALE
            dq[rows, cols] = unstacked(dq_rows.astype(bf16))
            dkv = tn(d_scores, q_rows * jnp.asarray(SCALE, bf16)) + tn(probs.astype(bf16), do_rows)
            part[4 * row : 4 * row + 4, :, :, lanes] = dkv.astype(bf16).reshape(
                4, 4, BLOCK, KV_COLS
            )
        sums[row].step1()
        if row == 0:
            gfull[gring.i] = gring.finish()[...]
            gback.step1()
    means = head_means()
    cosine, sine = cos_ref[...], sin_ref[...]

    def queries(g):
        cols = slice(g * GROUP_COLS, (g + 1) * GROUP_COLS)
        value, gain = turned_back(
            dq[:, cols].astype(f32), raw_ref[:, cols], qg_ref[...], cosine, sine, means
        )
        dqkv_ref[:, cols] = value.astype(bf16)
        return gain

    gain = queries(0)
    for g in range(1, KV):
        gain += queries(g)
    gq_ref[...] = gain
    for total in sums:
        total.step2()
    gback.step2()
    loads[2].wait()
    tile = 512
    for n in range(width // tile):
        cols = slice(n * tile, (n + 1) * tile)
        d_h1[:, cols] = nt(dqkv_ref[:, :q_cols], wqkv[cols, :q_cols])
    for total in sums:
        total.step3()
    for total in sums:
        total.step4()
    gback.finish()
    keep = pltpu.make_async_copy(gfull, gall_ref, lsem.at[4])
    keep.start()
    d_kv = jnp.concatenate([total.result().astype(bf16) for total in sums], 0)
    pieces = [d_kv[:, g * KV_COLS : g * KV_COLS + HD] for g in range(KV)]
    pieces += [d_kv[:, g * KV_COLS + HD : (g + 1) * KV_COLS] for g in range(KV)]
    d_kv = jnp.concatenate(pieces, 1)
    first, gain1 = turned_back(
        d_kv[:, :GROUP_COLS].astype(f32),
        raw_ref[:, q_cols : q_cols + GROUP_COLS],
        kg_ref[...],
        cosine,
        sine,
        means,
    )
    second, gain2 = turned_back(
        d_kv[:, GROUP_COLS : 2 * GROUP_COLS].astype(f32),
        raw_ref[:, q_cols + GROUP_COLS : q_cols + 2 * GROUP_COLS],
        kg_ref[...],
        cosine,
        sine,
        means,
    )
    lane = lax.broadcasted_iota(jnp.int32, gain2.shape, 1)
    gk_ref[...] = gain1 + jnp.where(lane < k_cols - GROUP_COLS, gain2, 0.0)
    dqkv_ref[:, q_cols : q_cols + GROUP_COLS] = first.astype(bf16)
    lane = lax.broadcasted_iota(jnp.int32, second.shape, 1)
    dqkv_ref[:, q_cols + GROUP_COLS : q_cols + 2 * GROUP_COLS] = jnp.where(
        lane < k_cols - GROUP_COLS,
        second.astype(bf16),
        d_kv[:, GROUP_COLS : 2 * GROUP_COLS],
    )
    dqkv_ref[:, q_cols + 2 * GROUP_COLS :] = d_kv[:, 2 * GROUP_COLS :]
    for n in range(width // tile):
        cols = slice(n * tile, (n + 1) * tile)
        d_h1[:, cols] += nt(dqkv_ref[:, q_cols:], wqkv[cols, q_cols:])
    n1, inv1 = rms_parts(x_ref[...].astype(f32))
    gga_ref[...] = jnp.sum(d_h1[...] * n1, axis=0, keepdims=True)
    gx_ref[...] = (d_r1[...] + rms_back(d_h1[...] * ga_ref[...], n1, inv1)).astype(bf16)
    keep.wait()
    copies.finish()


def rear(
    starts,
    d_h2,
    r1,
    dy,
    x,
    q,
    raw,
    kva,
    w_qkv,
    w_out,
    gsum,
    g_attn,
    g_ffn,
    q_gain,
    k_gain,
    cosine,
    sine,
):
    count, width = x.shape
    q_cols = HEADS * HD
    kv_cols = 2 * KV * HD
    vmem_spec = pl.BlockSpec(memory_space=pltpu.VMEM)
    any_spec = pl.BlockSpec(memory_space=pl.ANY)
    return pl.pallas_call(
        rear_kernel,
        out_shape=(
            jax.ShapeDtypeStruct((count, width), bf16),
            jax.ShapeDtypeStruct((count, q_cols + kv_cols), bf16),
            jax.ShapeDtypeStruct((count, width), bf16),
            jax.ShapeDtypeStruct((1, width), f32),
            jax.ShapeDtypeStruct((1, width), f32),
            jax.ShapeDtypeStruct((1, GROUP_COLS), f32),
            jax.ShapeDtypeStruct((1, GROUP_COLS), f32),
            jax.ShapeDtypeStruct(gsum.shape, bf16),
        ),
        in_specs=[
            pl.BlockSpec(memory_space=pltpu.SMEM),
            *[vmem_spec] * 6,
            *[any_spec] * 4,
            *[vmem_spec] * 6,
        ],
        out_specs=(*[vmem_spec] * 7, any_spec),
        scratch_shapes=[
            pltpu.VMEM((width, q_cols + kv_cols), bf16),
            pltpu.VMEM((q_cols, width), bf16),
            pltpu.VMEM((8, 4, BLOCK, kv_cols), bf16),
            pltpu.VMEM(gsum.shape, bf16),
            pltpu.VMEM(gsum.shape, bf16),
            pltpu.VMEM((2, gsum.shape[1] // 2, gsum.shape[2]), bf16),
            pltpu.VMEM((2, *gsum.shape[1:]), bf16),
            pltpu.VMEM((8, 4, BLOCK, kv_cols), bf16),
            pltpu.VMEM((2, BLOCK, 16 * BLOCK), f32),
            pltpu.VMEM((count, width), f32),
            pltpu.VMEM((count, q_cols), bf16),
            pltpu.VMEM((count, q_cols), bf16),
            pltpu.VMEM((count, width), f32),
            *sum_landings(kv_cols),
            pltpu.SemaphoreType.DMA((24,)),
            pltpu.SemaphoreType.DMA((24,)),
            pltpu.SemaphoreType.DMA((5,)),
        ],
        compiler_params=pltpu.CompilerParams(
            collective_id=3, has_side_effects=True, vmem_limit_bytes=VMEM_BYTES
        ),
        name="rear",
    )(
        starts,
        d_h2,
        r1,
        dy,
        x,
        q,
        raw,
        kva,
        w_qkv,
        w_out,
        gsum,
        g_attn,
        g_ffn,
        q_gain,
        k_gain,
        cosine,
        sine,
    )


AXIS_ORDERS = (("dp_0", "seq", "head"), ("seq", "head", "dp_0"), ("head", "dp_0", "seq"))
CHIP_AXES = ("dp_0", "seq", "head")


def projections_kernel(
    h1_ref,
    da_ref,
    dqkv_ref,
    mix_ref,
    gain_ref,
    gall_ref,
    left_ref,
    right_ref,
    gain_out,
    gboth_ref,
    *scratch,
):
    (h1c, dac, dqc, mxc, gsum, gboth) = scratch[:6]
    parts = scratch[6:9]
    half1, full1, half2, full2, last = (scratch[9 + 3 * k : 12 + 3 * k] for k in range(5))
    send, recv, lsem = scratch[24:]
    tokens = h1_ref.shape[0]
    copies = Copies(send, recv)
    barrier = pltpu.get_barrier_semaphore()
    core = lax.axis_index("dp_1")
    other = 1 - core
    for axis in CHIP_AXES:
        for by in (1, 2, 3):
            pl.semaphore_signal(
                barrier,
                inc=1,
                device_id={axis: shift(lax.axis_index(axis), by)},
                device_id_type=MESH,
            )
    pl.semaphore_signal(barrier, inc=1, device_id={"dp_1": other}, device_id_type=MESH)
    pl.semaphore_wait(barrier, 10)

    to_other = copies.start_to_core
    mine, theirs = pl.ds(0, tokens), pl.ds(tokens, tokens)

    def piece(z, which):
        return pl.ds(pl.multiple_of(z * 512 + which * 256, 256), 256)

    moves = [
        to_other(0, dqkv_ref, dqc.at[theirs]),
        to_other(1, mix_ref, mxc.at[theirs]),
    ]
    for z in range(4):
        cols = pl.ds(z * 256, 256)
        moves.append(to_other(2 + 2 * z, h1_ref.at[:, piece(z, other)], h1c.at[theirs, cols]))
        moves.append(to_other(3 + 2 * z, da_ref.at[:, piece(z, other)], dac.at[theirs, cols]))
    gain_move = to_other(10, gain_ref, gsum.at[3, core])
    grows = gall_ref.shape[1]
    place = gboth.at[:, pl.ds(pl.multiple_of(core * grows, 16), grows)]
    gmove = to_other(53, gall_ref, place)
    gload = pltpu.make_async_copy(gall_ref, place, lsem.at[0])
    gload.start()
    for z in range(4):
        cols = pl.ds(z * 256, 256)
        h1c[mine, cols] = h1_ref[:, piece(z, core)]
        dac[mine, cols] = da_ref[:, piece(z, core)]
    dqc[mine] = dqkv_ref[...]
    mxc[mine] = mix_ref[...]
    for move in moves:
        move.wait_recv()

    widths = [part.shape[4] for part in parts]
    qkv_width = dqkv_ref.shape[1]
    columns = qkv_width + mix_ref.shape[1]
    split = qkv_width - widths[0]
    sources = (
        ((h1c, dqc, 0, widths[0], 0),),
        ((h1c, dqc, widths[0], split, 0), (dac, mxc, 0, widths[1] - split, split)),
        ((dac, mxc, widths[1] - split, widths[2], 0),),
    )

    @pl.loop(0, 4)
    def _(z):
        cols = pl.ds(pl.multiple_of(z * 256, 256), 256)
        for k in range(3):
            for lhs, rhs, first, width, place in sources[k]:
                value = tn(lhs[:, cols], rhs[:, first : first + width]).astype(bf16)
                value = value.reshape(4, 4, 16, width)
                to = slice(place, place + width)
                if k == 0:
                    parts[0][z, :, :, :, to] = value
                elif k == 1:
                    parts[1][:, :, z, :, to] = value
                else:
                    for y in range(4):
                        parts[2][:, z, y, :, to] = value[y]

    def gain_step(k, axis, value):
        i = lax.axis_index(axis)
        gsum[k, i] = value
        out = []
        for n, by in enumerate((1, 2, 3)):
            src = gsum.at[k, i]
            out.append(copies.start(11 + 3 * k + n, src, src, axis, by))
        return out

    def gain_total(k, moves):
        for move in moves:
            move.wait_recv()
        return gsum[k, 0] + gsum[k, 1] + gsum[k, 2] + gsum[k, 3]

    base = 20
    rings = [
        RingSum(copies, base + 4 * k, AXIS_ORDERS[k][0], parts[k], half1[k], full1[k])
        for k in range(3)
    ]
    for ring in rings:
        ring.step1()
    gmove.wait_recv()
    gload.wait()
    gkeep = pltpu.make_async_copy(gboth, gboth_ref, lsem.at[1])
    gkeep.start()
    gain_move.wait_recv()
    gsum[3, core] = gain_ref[...]
    total = gsum[3, 0] + gsum[3, 1]
    gmoves = gain_step(0, CHIP_AXES[0], total)
    for ring in rings:
        ring.step2()
    gmoves = gain_step(1, CHIP_AXES[1], gain_total(0, gmoves))
    owns = [ring.finish() for ring in rings]
    rings = [
        RingSum(copies, base + 12 + 4 * k, AXIS_ORDERS[k][1], owns[k], half2[k], full2[k])
        for k in range(3)
    ]
    for ring in rings:
        ring.step1()
    gmoves = gain_step(2, CHIP_AXES[2], gain_total(1, gmoves))
    for ring in rings:
        ring.step2()
    gain_out[...] = gain_total(2, gmoves)
    owns = [ring.finish() for ring in rings]
    ends = []
    for k in range(3):
        axis = AXIS_ORDERS[k][2]
        i = lax.axis_index(axis)
        for n, by in enumerate((1, 2, 3)):
            ends.append(
                copies.start(
                    base + 24 + 3 * k + n, owns[k].at[shift(i, by)], last[k].at[n], axis, by
                )
            )
    for end in ends:
        end.wait_recv()
    place = 0
    for k in range(3):
        i = lax.axis_index(AXIS_ORDERS[k][2])
        value = owns[k][i].astype(f32)
        for n in range(3):
            value = value + last[k][n].astype(f32)
        for ref, first, last_col in ((left_ref, 0, qkv_width), (right_ref, qkv_width, columns)):
            low, high = max(first, place), min(last_col, place + widths[k])
            if low < high:
                ref[:, low - first : high - first] = value[:, low - place : high - place]
        place += widths[k]
    gkeep.wait()
    copies.finish()


def projections(h1, d_attn, d_qkv, mixed, gains, gall):
    tokens, qkv_width = d_qkv.shape
    columns = qkv_width + mixed.shape[1]
    widths = (1536, 1536, columns - 3072)
    any_spec = pl.BlockSpec(memory_space=pl.ANY)
    vmem_spec = pl.BlockSpec(memory_space=pltpu.VMEM)
    rows = h1.shape[1] // 2

    def each(make):
        return [pltpu.VMEM(make(width), bf16) for width in widths]

    return pl.pallas_call(
        projections_kernel,
        out_shape=(
            jax.ShapeDtypeStruct((16, qkv_width), f32),
            jax.ShapeDtypeStruct((16, mixed.shape[1]), f32),
            jax.ShapeDtypeStruct(gains.shape, f32),
            jax.ShapeDtypeStruct((gall.shape[0], 2 * gall.shape[1], gall.shape[2]), bf16),
        ),
        in_specs=[*[vmem_spec] * 5, any_spec],
        out_specs=(vmem_spec, vmem_spec, vmem_spec, any_spec),
        scratch_shapes=[
            pltpu.VMEM((2 * tokens, rows), bf16),
            pltpu.VMEM((2 * tokens, rows), bf16),
            pltpu.VMEM((2 * tokens, qkv_width), bf16),
            pltpu.VMEM((2 * tokens, mixed.shape[1]), bf16),
            pltpu.VMEM((4, 4, *gains.shape), f32),
            pltpu.VMEM((gall.shape[0], 2 * gall.shape[1], gall.shape[2]), bf16),
            *each(lambda w: (4, 4, 4, 16, w)),
            *each(lambda w: (2, 2, 4, 16, w)),
            *each(lambda w: (2, 4, 4, 16, w)),
            *each(lambda w: (2, 2, 16, w)),
            *each(lambda w: (2, 4, 16, w)),
            *each(lambda w: (3, 16, w)),
            pltpu.SemaphoreType.DMA((54,)),
            pltpu.SemaphoreType.DMA((54,)),
            pltpu.SemaphoreType.DMA((2,)),
        ],
        compiler_params=pltpu.CompilerParams(
            collective_id=4, has_side_effects=True, vmem_limit_bytes=VMEM_BYTES
        ),
        name="projections",
    )(h1, d_attn, d_qkv, mixed, gains, gall)


def widen_kernel(g_ref, gin_ref, gdn_ref):
    units = gdn_ref.shape[0]
    gin_ref[:, 0, :] = g_ref[:units].astype(f32)
    gin_ref[:, 1, :] = g_ref[units : 2 * units].astype(f32)
    gdn_ref[...] = g_ref[2 * units :].astype(f32)


def widen(g, units):
    tiles, _, tile = g.shape
    return pl.pallas_call(
        widen_kernel,
        grid=(tiles,),
        out_shape=(
            jax.ShapeDtypeStruct((units, 2, tiles * tile), f32),
            jax.ShapeDtypeStruct((units, tiles * tile), f32),
        ),
        in_specs=[pl.BlockSpec((None, 3 * units, tile), lambda n: (n, 0, 0))],
        out_specs=(
            pl.BlockSpec((units, 2, tile), lambda n: (0, 0, n)),
            pl.BlockSpec((units, tile), lambda n: (0, n)),
        ),
        compiler_params=pltpu.CompilerParams(vmem_limit_bytes=VMEM_BYTES),
        name="widen",
    )(g)


def angle_tables(positions, columns):
    lane = jnp.arange(columns)
    freq = jnp.exp((lane % (HD // 2)).astype(f32) * (-2.0 * math.log(10000.0) / HD))
    angle = positions.astype(f32)[:, None] * freq[None, :]
    sign = jnp.where(lane % HD < HD // 2, -1.0, 1.0)
    return (jnp.cos(angle), jnp.sin(angle) * sign[None, :])


def body(
    tokens, w_qkv, w_out, w_ffn_in, w_ffn_out, g_attn, g_ffn, q_gain, k_gain, doc_starts, d_out
):
    rows, tok, width = tokens.shape
    count = rows * tok
    n_seq = lax.axis_size("seq")
    n_head = lax.axis_size("head")
    first = (lax.axis_index("seq") * n_head + lax.axis_index("head")) * tok
    cosine, sine = angle_tables(first + jnp.arange(count) % tok, GROUP_COLS)
    x = tokens.reshape(count, width)
    dy = d_out.reshape(count, width)
    ga = g_attn[None]
    gf = g_ffn[None]
    qg = jnp.tile(q_gain, PER_GROUP)[None]
    kg = jnp.tile(k_gain, PER_GROUP)[None]
    h1, raw, q, kva, mixed, r1, h2, dy_all = front(
        doc_starts, x, w_qkv, w_out, ga, gf, qg, kg, cosine, sine, d_out
    )
    outp, d_h2, gsum = ffn(h2.reshape(rows, tok, width), dy_all, w_ffn_in, w_ffn_out)
    ffn_sum = lax.psum_scatter(
        outp.reshape(n_seq * n_head * count, width), ("seq", "head"), scatter_dimension=0, tiled=True
    )
    d_attn, d_qkv, grad_x, grad_gattn, grad_gffn, grad_qgain, grad_kgain, gall = rear(
        doc_starts,
        d_h2.reshape(count, width),
        r1,
        dy,
        x,
        q,
        raw,
        kva,
        w_qkv,
        w_out,
        gsum,
        ga,
        gf,
        qg,
        kg,
        cosine,
        sine,
    )
    gains = jnp.concatenate([grad_gattn, grad_gffn, grad_qgain, grad_kgain], 1)[0]
    gains = jnp.pad(gains, (0, 40 * 128 - gains.shape[0])).reshape(40, 128)
    grad_qkv, grad_out, gains, gboth = projections(h1, d_attn, d_qkv, mixed, gains, gall)
    grad_in, grad_down = widen(gboth, w_ffn_out.shape[0])
    gains = gains.reshape(-1)
    output = (r1 + ffn_sum.astype(f32)).astype(bf16)
    heads = gains[2 * width : 2 * width + 2 * GROUP_COLS].reshape(2, PER_GROUP, HD).sum(1)
    return (
        output.reshape(rows, tok, width),
        grad_x.reshape(rows, tok, width),
        grad_qkv,
        grad_out.T,
        grad_in,
        grad_down,
        gains[:width],
        gains[width : 2 * width],
        heads[0],
        heads[1],
    )


def solution(mesh):
    split = Mesh(
        mesh.devices.reshape(4, 2, mesh.shape["seq"], mesh.shape["head"]),
        ("dp_0", "dp_1", "seq", "head"),
    )
    return jax.shard_map(
        body,
        mesh=split,
        in_specs=(
            P(DP, ("seq", "head"), None),
            P(),
            P(),
            P(("seq", "head"), None, None),
            P(("seq", "head"), None),
            P(),
            P(),
            P(),
            P(),
            P(DP, None),
            P(DP, ("seq", "head"), None),
        ),
        out_specs=(
            P(DP, ("seq", "head"), None),
            P(DP, ("seq", "head"), None),
            P(DP_SEQ_HEAD, None),
            P(None, DP_SEQ_HEAD),
            P(("seq", "head"), None, None),
            P(("seq", "head"), None),
            P(),
            P(),
            P(),
            P(),
        ),
        check_vma=False,
    )
```

```python
import functools
import math

import jax
import jax.numpy as jnp
from jax import lax
from jax.experimental import pallas as pl
from jax.experimental.pallas import tpu as pltpu
from jax.sharding import Mesh
from jax.sharding import PartitionSpec as P

HEADS = 28
KV = 7
HD = 64
PER_GROUP = HEADS // KV
DP_SEQ_HEAD = ("dp_0", "dp_1", "seq", "head")
DP = ("dp_0", "dp_1")
RING = 4
BLOCK = 64
MESH = pl.DeviceIdType.MESH
EPS = 1e-06
SCALE = 0.125
f32 = jnp.float32
bf16 = jnp.bfloat16
VMEM_BYTES = 62 * 2**20


def nt(a, b):
    return lax.dot_general(a, b, (((1,), (1,)), ((), ())), preferred_element_type=f32)


def nn(a, b):
    return lax.dot_general(a, b, (((1,), (0,)), ((), ())), preferred_element_type=f32)


def tn(a, b):
    return lax.dot_general(a, b, (((0,), (0,)), ((), ())), preferred_element_type=f32)


def shift(index, by):
    return lax.rem(index + (by + RING), RING)


def barrier_with(axes, core=False):
    barrier = pltpu.get_barrier_semaphore()
    for axis in axes:
        index = lax.axis_index(axis)
        for by in (1, -1):
            pl.semaphore_signal(
                barrier, inc=1, device_id={axis: shift(index, by)}, device_id_type=MESH
            )
    if core:
        other = 1 - lax.axis_index("dp_1")
        pl.semaphore_signal(barrier, inc=1, device_id={"dp_1": other}, device_id_type=MESH)
    pl.semaphore_wait(barrier, 2 * len(axes) + int(core))


class Copies:
    def __init__(self, send, recv):
        self.send = send
        self.recv = recv
        self.started = []

    def start(self, slot, src, dst, axis, by):
        copy = pltpu.make_async_remote_copy(
            src_ref=src,
            dst_ref=dst,
            send_sem=self.send.at[slot],
            recv_sem=self.recv.at[slot],
            device_id={axis: shift(lax.axis_index(axis), by)},
            device_id_type=MESH,
        )
        copy.start()
        self.started.append(copy)
        return copy

    def start_to_core(self, slot, src, dst):
        copy = pltpu.make_async_remote_copy(
            src_ref=src,
            dst_ref=dst,
            send_sem=self.send.at[slot],
            recv_sem=self.recv.at[slot],
            device_id={"dp_1": 1 - lax.axis_index("dp_1")},
            device_id_type=MESH,
        )
        copy.start()
        self.started.append(copy)
        return copy

    def finish(self):
        for copy in self.started:
            copy.wait_send()


INNER = ("head", "seq")
GROUP = ("seq", "head")


class PlaneGather:
    def __init__(self, copies, base, half, own, buf):
        self.c = copies
        self.base = base + 8 * half
        self.half = half
        self.own = own
        self.buf = buf
        self.i = lax.axis_index(INNER[half])
        self.g = lax.axis_index(GROUP[half])

    def row(self, by=0):
        return 4 * self.half + shift(self.g, by)

    def step1(self):
        ax = INNER[self.half]
        dst = self.buf.at[self.row(), self.i]
        self.a = self.c.start(self.base, self.own, dst, ax, 1)
        self.b = self.c.start(self.base + 1, self.own, dst, ax, -1)

    def step2(self):
        ax = INNER[self.half]
        n = self.buf.shape[2] // 2
        self.a.wait_recv()
        left = self.buf.at[self.row(), shift(self.i, -1), pl.ds(0, n)]
        self.a = self.c.start(self.base + 2, left, left, ax, 1)
        self.b.wait_recv()
        right = self.buf.at[self.row(), shift(self.i, 1), pl.ds(n, n)]
        self.b = self.c.start(self.base + 3, right, right, ax, -1)

    def step3(self):
        ax = GROUP[self.half]
        self.a.wait_recv()
        self.b.wait_recv()
        rows = self.buf.at[self.row()]
        self.a = self.c.start(self.base + 4, rows, rows, ax, 1)
        self.b = self.c.start(self.base + 5, rows, rows, ax, -1)

    def step4(self):
        ax = GROUP[self.half]
        self.a.wait_recv()
        left = self.buf.at[self.row(-1), pl.ds(0, 2)]
        self.a = self.c.start(self.base + 6, left, left, ax, 1)
        self.b.wait_recv()
        right = self.buf.at[self.row(1), pl.ds(2, 2)]
        self.b = self.c.start(self.base + 7, right, right, ax, -1)

    def finish(self):
        self.a.wait_recv()
        self.b.wait_recv()


class PlaneSum:
    def __init__(self, copies, base, half, part, land1, land2, land3, land4):
        self.c = copies
        self.base = base + 12 * half
        self.half = half
        self.part = part
        self.l1, self.l2, self.l3, self.l4 = (
            ref.at[half] for ref in (land1, land2, land3, land4)
        )
        self.i = lax.axis_index(INNER[half])
        self.g = lax.axis_index(GROUP[half])

    def row(self, by=0):
        return 4 * self.half + shift(self.g, by)

    def add(self, ref, other):
        ref[...] = (ref[...].astype(f32) + other[...].astype(f32)).astype(ref.dtype)

    def far(self):
        ax = GROUP[self.half]
        row = self.row(2)
        self.a = self.c.start(self.base, self.part.at[row, pl.ds(0, 2)], self.l1.at[0], ax, 1)
        self.b = self.c.start(self.base + 1, self.part.at[row, pl.ds(2, 2)], self.l1.at[1], ax, -1)

    def early(self):
        ax = GROUP[self.half]
        one, two = pl.ds(0, 2), pl.ds(2, 2)
        right, left = self.part.at[self.row(1)], self.part.at[self.row(-1)]
        self.ea = self.c.start(self.base + 2, right.at[two], self.l2.at[0, two], ax, 1)
        self.eb = self.c.start(self.base + 3, left.at[one], self.l2.at[1, one], ax, -1)

    def late(self):
        ax = GROUP[self.half]
        one, two = pl.ds(0, 2), pl.ds(2, 2)
        right, left = self.part.at[self.row(1), one], self.part.at[self.row(-1), two]
        self.a.wait_recv()
        self.add(right, self.l1.at[0])
        self.a = self.c.start(self.base + 4, right, self.l2.at[0, one], ax, 1)
        self.b.wait_recv()
        self.add(left, self.l1.at[1])
        self.b = self.c.start(self.base + 5, left, self.l2.at[1, two], ax, -1)

    def inner_start(self):
        ax = INNER[self.half]
        n = self.part.shape[2] // 2
        one, two = pl.ds(0, n), pl.ds(n, n)
        for copy in (self.ea, self.eb, self.a, self.b):
            copy.wait_recv()
        rows = self.part.at[self.row()]

        def sum_of(k):
            rows[k] = (
                rows[k].astype(f32) + self.l2[0, k].astype(f32) + self.l2[1, k].astype(f32)
            ).astype(rows.dtype)

        sum_of(shift(self.i, 2))
        block = rows.at[shift(self.i, 2)]
        self.a = self.c.start(self.base + 6, block.at[one], self.l3.at[0], ax, 1)
        self.b = self.c.start(self.base + 7, block.at[two], self.l3.at[1], ax, -1)
        sum_of(shift(self.i, 1))
        sum_of(shift(self.i, -1))
        right, left = rows.at[shift(self.i, 1)], rows.at[shift(self.i, -1)]
        self.ea = self.c.start(self.base + 8, right.at[two], self.l4.at[0, two], ax, 1)
        self.eb = self.c.start(self.base + 9, left.at[one], self.l4.at[1, one], ax, -1)
        sum_of(self.i)

    def inner_late(self):
        ax = INNER[self.half]
        n = self.part.shape[2] // 2
        one, two = pl.ds(0, n), pl.ds(n, n)
        right = self.part.at[self.row(), shift(self.i, 1), one]
        left = self.part.at[self.row(), shift(self.i, -1), two]
        self.a.wait_recv()
        self.add(right, self.l3.at[0])
        self.a = self.c.start(self.base + 10, right, self.l4.at[0, one], ax, 1)
        self.b.wait_recv()
        self.add(left, self.l3.at[1])
        self.b = self.c.start(self.base + 11, left, self.l4.at[1, two], ax, -1)

    def result(self):
        for copy in (self.ea, self.eb, self.a, self.b):
            copy.wait_recv()
        own = self.part[self.row(), self.i].astype(f32)
        return own + self.l4[0].astype(f32) + self.l4[1].astype(f32)


def sum_landings(columns):
    return [
        pltpu.VMEM((2, 2, 2, BLOCK, columns), bf16),
        pltpu.VMEM((2, 2, 4, BLOCK, columns), bf16),
        pltpu.VMEM((2, 2, BLOCK // 2, columns), bf16),
        pltpu.VMEM((2, 2, BLOCK, columns), bf16),
    ]


class RingSum:
    def __init__(self, copies, base, axis, part, half_land, full_land):
        self.c = copies
        self.base = base
        self.axis = axis
        self.part = part
        self.hl = half_land
        self.fl = full_land
        self.i = lax.axis_index(axis)
        n = part.shape[1] // 2
        self.one, self.two = pl.ds(0, n), pl.ds(n, n)

    def start(self):
        far = self.part.at[shift(self.i, 2)]
        right, left = self.part.at[shift(self.i, 1)], self.part.at[shift(self.i, -1)]
        one, two, ax = self.one, self.two, self.axis
        self.a = self.c.start(self.base, far.at[one], self.hl.at[0], ax, 1)
        self.b = self.c.start(self.base + 1, far.at[two], self.hl.at[1], ax, -1)
        self.ea = self.c.start(self.base + 2, right.at[two], self.fl.at[0, two], ax, 1)
        self.eb = self.c.start(self.base + 3, left.at[one], self.fl.at[1, one], ax, -1)

    def late(self):
        right = self.part.at[shift(self.i, 1), self.one]
        left = self.part.at[shift(self.i, -1), self.two]
        self.a.wait_recv()
        right[...] = (right[...].astype(f32) + self.hl[0].astype(f32)).astype(bf16)
        self.a = self.c.start(self.base + 4, right, self.fl.at[0, self.one], self.axis, 1)
        self.b.wait_recv()
        left[...] = (left[...].astype(f32) + self.hl[1].astype(f32)).astype(bf16)
        self.b = self.c.start(self.base + 5, left, self.fl.at[1, self.two], self.axis, -1)

    def finish(self):
        for copy in (self.ea, self.eb, self.a, self.b):
            copy.wait_recv()
        own = self.part.at[self.i]
        own[...] = (
            own[...].astype(f32) + self.fl[0].astype(f32) + self.fl[1].astype(f32)
        ).astype(bf16)
        return own


class RingGather:
    def __init__(self, copies, base, axis, full):
        self.c = copies
        self.base = base
        self.axis = axis
        self.full = full
        self.i = lax.axis_index(axis)

    def step1(self):
        own = self.full.at[self.i]
        self.a = self.c.start(self.base, own, own, self.axis, 1)
        self.b = self.c.start(self.base + 1, own, own, self.axis, -1)

    def step2(self):
        n = self.full.shape[1] // 2
        self.a.wait_recv()
        left = self.full.at[shift(self.i, -1), pl.ds(0, n)]
        self.a = self.c.start(self.base + 2, left, left, self.axis, 1)
        self.b.wait_recv()
        right = self.full.at[shift(self.i, 1), pl.ds(n, n)]
        self.b = self.c.start(self.base + 3, right, right, self.axis, -1)

    def finish(self):
        self.a.wait_recv()
        self.b.wait_recv()


def ffn_kernel(
    h2_ref,
    dy_ref,
    win_ref,
    wdn_ref,
    outp_ref,
    dh2_ref,
    gsum_ref,
    h2a,
    dya,
    pairs,
    win,
    wdn,
    hid,
    dbo,
    dpt,
    l1,
    l2,
    l3,
    l4,
    stage,
    gst,
    gland,
    send,
    recv,
    lsem,
    osem,
):
    units = wdn.shape[0]
    width = wdn.shape[1]
    copies = Copies(send, recv)
    weights = [
        pltpu.make_async_copy(win_ref.at[pl.ds(0, units // 2)], pairs, lsem.at[0]),
        pltpu.make_async_copy(win_ref.at[pl.ds(units // 2, units // 2)], pairs, lsem.at[4]),
        pltpu.make_async_copy(wdn_ref, wdn, lsem.at[1]),
    ]
    weights[0].start()
    weights[2].start()
    load = pltpu.make_async_copy(dy_ref, dya, lsem.at[2])
    load.start()
    barrier_with(("seq", "head"), core=True)
    gathers = [PlaneGather(copies, 0, half, h2_ref.at[half], h2a) for half in (0, 1)]
    for gather in gathers:
        gather.step1()
    for half in (0, 1):
        h2a[gathers[half].row(), gathers[half].i] = h2_ref[half]

    def split_pairs(first):
        win[first : first + units // 2] = pairs[:, 0, :]
        win[units + first : units + first + units // 2] = pairs[:, 1, :]

    weights[0].wait()
    split_pairs(0)
    weights[1].start()
    for gather in gathers:
        gather.step2()
    weights[1].wait()
    split_pairs(units // 2)
    weights[2].wait()
    load.wait()
    for gather in gathers:
        gather.step3()
    seq, head = lax.axis_index("seq"), lax.axis_index("head")

    def group(half, by):
        return 4 * half + lax.rem(seq + half * (head - seq) + by + 4, 4)

    def rows_of(ref, q):
        return ref[q].reshape(4 * BLOCK, width)

    def columns_of(q):
        return pl.ds(pl.multiple_of(q * 4 * BLOCK, 4 * BLOCK), 4 * BLOCK)

    def forward(q):
        both = nt(win[...], rows_of(h2a, q))
        d_hidden = nt(wdn[...], rows_of(dya, q))
        gate = both[:units]
        up = both[units:]
        sig = 1.0 / (1.0 + jnp.exp(-gate))
        act = gate * sig
        cols = columns_of(q)
        hid[:, cols] = (act * up).astype(bf16)
        dbo[:units, cols] = (d_hidden * up * (sig * (1.0 + gate * (1.0 - sig)))).astype(bf16)
        dbo[units:, cols] = (d_hidden * act).astype(bf16)

    def back(q):
        value = tn(dbo[:, columns_of(q)], win[...])
        dpt[q] = value.astype(bf16).reshape(4, BLOCK, width)

    @pl.loop(0, 2)
    def _(half):
        forward(group(half, 0))

    for gather in gathers:
        gather.step4()

    @pl.loop(0, 4)
    def _(k):
        q = group(lax.div(k, 2), 1 - 2 * lax.rem(k, 2))
        forward(q)
        back(q)

    for gather in gathers:
        gather.finish()
    sums = [PlaneSum(copies, 16, half, dpt, l1, l2, l3, l4) for half in (0, 1)]
    for total in sums:
        total.early()

    @pl.loop(0, 2)
    def _(half):
        forward(group(half, 2))
        back(group(half, 2))

    for total in sums:
        total.far()

    @pl.loop(0, 2)
    def _(half):
        back(group(half, 0))

    tile = gland.shape[2]
    half_rows = gland.shape[1]
    tokens = 8 * 4 * BLOCK
    core = lax.axis_index("dp_1")
    mine = pl.ds(pl.multiple_of(core * half_rows, 16), half_rows)
    theirs = pl.ds(pl.multiple_of((1 - core) * half_rows, 16), half_rows)
    swaps = []
    for n in range(gland.shape[0]):
        cols = pl.ds(n * tile, tile)
        gst[n, : 2 * units] = nn(dbo[...], h2a[:, :, :, cols].reshape(tokens, tile)).astype(bf16)
        gst[n, 2 * units :] = nn(hid[...], dya[:, :, :, cols].reshape(tokens, tile)).astype(bf16)
        swaps.append(copies.start_to_core(40 + n, gst.at[n, theirs], gland.at[n]))
        if n == 2:
            for total in sums:
                total.late()

    def out_copy(q):
        return pltpu.make_async_copy(stage.at[q % 2], outp_ref.at[q], osem.at[q % 2])

    def out_part(q):
        if q >= 2:
            out_copy(q - 2).wait()
        value = tn(hid[:, pl.ds(q * 4 * BLOCK, 4 * BLOCK)], wdn[...])
        stage[q % 2] = value.astype(bf16).reshape(4, BLOCK, width)
        out_copy(q).start()

    for q in range(6):
        out_part(q)
    for total in sums:
        total.inner_start()
    for q in range(6, 8):
        out_part(q)
    for total in sums:
        total.inner_late()
    for half in (0, 1):
        dh2_ref[half] = sums[half].result()
    for n, swap in enumerate(swaps):
        swap.wait_recv()
        gland[n] = (gst[n, mine].astype(f32) + gland[n].astype(f32)).astype(bf16)
    keep = pltpu.make_async_copy(gland, gsum_ref, lsem.at[3])
    keep.start()
    out_copy(6).wait()
    out_copy(7).wait()
    keep.wait()
    copies.finish()


def ffn(h2, dy_all, w_in, w_down):
    units, width = w_down.shape
    tokens = 32 * BLOCK
    tile = 512
    any_spec = pl.BlockSpec(memory_space=pl.ANY)
    vmem_spec = pl.BlockSpec(memory_space=pltpu.VMEM)
    return pl.pallas_call(
        ffn_kernel,
        out_shape=(
            jax.ShapeDtypeStruct((8, 4, BLOCK, width), bf16),
            jax.ShapeDtypeStruct((2, BLOCK, width), f32),
            jax.ShapeDtypeStruct((width // tile, 3 * units // 2, tile), bf16),
        ),
        in_specs=[vmem_spec, any_spec, any_spec, any_spec],
        out_specs=(any_spec, vmem_spec, any_spec),
        scratch_shapes=[
            pltpu.VMEM((8, 4, BLOCK, width), bf16),
            pltpu.VMEM((8, 4, BLOCK, width), bf16),
            pltpu.VMEM((units // 2, 2, width), bf16),
            pltpu.VMEM((2 * units, width), bf16),
            pltpu.VMEM((units, width), bf16),
            pltpu.VMEM((units, tokens), bf16),
            pltpu.VMEM((2 * units, tokens), bf16),
            pltpu.VMEM((8, 4, BLOCK, width), bf16),
            *sum_landings(width),
            pltpu.VMEM((2, 4, BLOCK, width), bf16),
            pltpu.VMEM((width // tile, 3 * units, tile), bf16),
            pltpu.VMEM((width // tile, 3 * units // 2, tile), bf16),
            pltpu.SemaphoreType.DMA((44,)),
            pltpu.SemaphoreType.DMA((44,)),
            pltpu.SemaphoreType.DMA((5,)),
            pltpu.SemaphoreType.DMA((2,)),
        ],
        compiler_params=pltpu.CompilerParams(
            collective_id=1, has_side_effects=True, vmem_limit_bytes=VMEM_BYTES
        ),
        name="ffn",
    )(h2, dy_all, w_in, w_down)


def mask_rows(starts_ref, row, transposed, mask_ref):
    seq, head = lax.axis_index("seq"), lax.axis_index("head")
    keys = 16 * BLOCK
    index = lax.broadcasted_iota(jnp.int32, (1, keys), 1)
    if transposed:
        group = lax.div(index, 4 * BLOCK)
        inner = lax.rem(lax.div(index, BLOCK), 4)
        k_pos = (inner * 4 + group) * BLOCK + lax.rem(index, BLOCK)
    else:
        k_pos = index
    first = (seq * 4 + head) * BLOCK
    q_pos = first + lax.broadcasted_iota(jnp.int32, (BLOCK, 1), 0)
    k_doc = jnp.zeros((1, keys), jnp.int32)
    q_doc = jnp.zeros((BLOCK, 1), jnp.int32)
    for d in range(starts_ref.shape[1]):
        start = starts_ref[row, d]
        k_doc += (start <= k_pos).astype(jnp.int32)
        q_doc += (start <= q_pos).astype(jnp.int32)
    seen = (k_pos <= q_pos) & (k_doc == q_doc)
    mask_ref[row] = seen.astype(f32)


LOG2E_SCALE = SCALE * math.log2(math.e)


def stacked(block, where):
    rows = jnp.concatenate([block[:, h * HD : (h + 1) * HD] for h in range(PER_GROUP)], 0)
    zero = jnp.zeros_like(rows)
    return jnp.concatenate([rows, zero] if where == 0 else [zero, rows], 1)


def unstacked(rows):
    return jnp.concatenate([rows[h * BLOCK : (h + 1) * BLOCK] for h in range(PER_GROUP)], 1)


def weights_of(q_rows, kv_rows, mask):
    scores = nt(q_rows, kv_rows)
    keys = kv_rows.shape[0]
    e = jnp.exp2(scores * LOG2E_SCALE).reshape(PER_GROUP, BLOCK, keys) * mask[None]
    return e.reshape(PER_GROUP * BLOCK, keys)


GROUP_COLS = PER_GROUP * HD
KV_COLS = 2 * HD


def head_means(columns=GROUP_COLS):
    a = lax.div(lax.broadcasted_iota(jnp.int32, (columns, columns), 0), HD)
    b = lax.div(lax.broadcasted_iota(jnp.int32, (columns, columns), 1), HD)
    return jnp.where(a == b, 1.0 / HD, 0.0).astype(f32)


def head_mean(v, means):
    return jnp.dot(v, means, precision=lax.Precision.HIGHEST, preferred_element_type=f32)


def swapped(v):
    columns = v.shape[1]
    lane = lax.rem(lax.broadcasted_iota(jnp.int32, v.shape, 1), HD)
    up = pltpu.roll(v, columns - HD // 2, 1)
    down = pltpu.roll(v, HD // 2, 1)
    return jnp.where(lane < HD // 2, up, down)


def turned(raw, gain, cosine, sine, means):
    normed = raw * lax.rsqrt(head_mean(raw * raw, means) + EPS)
    v = normed * gain
    return v * cosine + swapped(v) * sine


def turned_back(grad, raw, gain, cosine, sine, means):
    inverse = lax.rsqrt(head_mean(raw * raw, means) + EPS)
    normed = raw * inverse
    u = grad * cosine - swapped(grad) * sine
    gain_grad = jnp.sum(u * normed, axis=0, keepdims=True)
    e = u * gain
    return inverse * (e - normed * head_mean(e * normed, means)), gain_grad


def rms_parts(v):
    inverse = lax.rsqrt(jnp.mean(v * v, axis=-1, keepdims=True) + EPS)
    return (v * inverse, inverse)


def rms_back(grad, normed, inverse):
    return inverse * (grad - normed * jnp.mean(grad * normed, axis=-1, keepdims=True))


def front_kernel(
    starts_ref,
    x_ref,
    wqkv_ref,
    wout_ref,
    ga_ref,
    gf_ref,
    qg_ref,
    kg_ref,
    cos_ref,
    sin_ref,
    dy_ref,
    h1_ref,
    raw_ref,
    q_ref,
    kva_ref,
    mixed_ref,
    r1_ref,
    h2_ref,
    dya_ref,
    wq,
    wkv,
    wo,
    own,
    kva,
    dya,
    qst,
    mask,
    oacc,
    lacc,
    send,
    recv,
    lsem,
):
    count, width = x_ref.shape
    q_cols = HEADS * HD
    k_cols = KV * HD
    loads = [
        pltpu.make_async_copy(wqkv_ref.at[:, pl.ds(q_cols, 2 * k_cols)], wkv, lsem.at[0]),
        pltpu.make_async_copy(wqkv_ref.at[:, pl.ds(0, q_cols)], wq, lsem.at[1]),
        pltpu.make_async_copy(wout_ref, wo, lsem.at[2]),
    ]
    for load in loads:
        load.start()
    copies = Copies(send, recv)
    barrier_with(("seq", "head"))
    cotangents = [PlaneGather(copies, 16, half, dy_ref.at[half], dya) for half in (0, 1)]
    for gather in cotangents:
        gather.step1()
    for half in (0, 1):
        dya[cotangents[half].row(), cotangents[half].i] = dy_ref[half]
    means = head_means()
    cosine, sine = cos_ref[...], sin_ref[...]
    x = x_ref[...].astype(f32)
    h1_ref[...] = (rms_parts(x)[0] * ga_ref[...]).astype(bf16)
    loads[0].wait()
    kv = nn(h1_ref[...], wkv[...])
    raw_ref[:, q_cols:] = kv
    keys = jnp.concatenate(
        [
            turned(kv[:, c : c + GROUP_COLS], kg_ref[...], cosine, sine, means)
            for c in (0, GROUP_COLS)
        ],
        1,
    )
    for g in range(KV):
        k = keys[:, g * HD : (g + 1) * HD]
        v = kv[:, k_cols + g * HD : k_cols + (g + 1) * HD]
        own[:, :, g * KV_COLS : (g + 1) * KV_COLS] = (
            jnp.concatenate([k, v], 1).astype(bf16).reshape(2, BLOCK, KV_COLS)
        )
    gathers = [PlaneGather(copies, 0, half, own.at[half], kva) for half in (0, 1)]
    for gather in gathers:
        gather.step1()
    for half in (0, 1):
        kva[gathers[half].row(), gathers[half].i] = own[half]
    for gather in cotangents:
        gather.step2()
    loads[1].wait()

    def queries(g):
        cols = slice(g * GROUP_COLS, (g + 1) * GROUP_COLS)
        raw = nn(h1_ref[...], wq[:, cols])
        raw_ref[:, cols] = raw
        q = turned(raw, qg_ref[...], cosine, sine, means).astype(bf16)
        q_ref[:, cols] = q
        for row in (0, 1):
            qst[row * KV + g] = stacked(q[row * BLOCK : (row + 1) * BLOCK], 0)

    for g in range(3):
        queries(g)
    for gather in gathers:
        gather.step2()
    for g in range(3, KV):
        queries(g)
    for gather in gathers:
        gather.step3()
    mask_rows(starts_ref, 0, False, mask)
    mask_rows(starts_ref, 1, True, mask)
    seq, head = lax.axis_index("seq"), lax.axis_index("head")

    def scored(row, by, first):
        group = lax.rem(seq + row * (head - seq) + by + 4, 4)
        seen = mask[row, :, pl.ds(pl.multiple_of(group * 4 * BLOCK, 4 * BLOCK), 4 * BLOCK)]
        for g in range(KV):
            index = row * KV + g
            kv_rows = kva[
                4 * row + group, :, :, g * KV_COLS : (g + 1) * KV_COLS
            ].reshape(4 * BLOCK, KV_COLS)
            e = weights_of(qst[index], kv_rows, seen)
            total = e[:, : 2 * BLOCK] + e[:, 2 * BLOCK :]
            mixed = nn(e.astype(bf16), kv_rows)
            if first:
                lacc[index] = total
                oacc[index] = mixed
            else:
                lacc[index] += total
                oacc[index] += mixed

    @pl.loop(0, 2)
    def _(row):
        scored(row, 0, True)

    for gather in gathers:
        gather.step4()
    for gather in cotangents:
        gather.step3()

    @pl.loop(0, 4)
    def _(k):
        scored(lax.div(k, 2), 1 - 2 * lax.rem(k, 2), False)

    for gather in gathers:
        gather.finish()
    keep = pltpu.make_async_copy(kva, kva_ref, lsem.at[3])
    keep.start()

    @pl.loop(0, 2)
    def _(row):
        scored(row, 2, False)

    for row in (0, 1):
        for g in range(KV):
            index = row * KV + g
            mixed = oacc[index][:, HD:] / jnp.sum(lacc[index], axis=1, keepdims=True)
            mixed_ref[
                row * BLOCK : (row + 1) * BLOCK, g * GROUP_COLS : (g + 1) * GROUP_COLS
            ] = unstacked(mixed.astype(bf16))
    loads[2].wait()
    tile = 512
    for n in range(width // tile):
        cols = slice(n * tile, (n + 1) * tile)
        r1_ref[:, cols] = x_ref[:, cols].astype(f32) + nn(mixed_ref[...], wo[:, cols])
    for gather in cotangents:
        gather.step4()
    h2_ref[...] = (rms_parts(r1_ref[...])[0] * gf_ref[...]).astype(bf16)
    keep.wait()
    for gather in cotangents:
        gather.finish()
    keep = pltpu.make_async_copy(dya, dya_ref, lsem.at[4])
    keep.start()
    keep.wait()
    copies.finish()


def front(starts, x, w_qkv, w_out, g_attn, g_ffn, q_gain, k_gain, cosine, sine, dy):
    count, width = x.shape
    q_cols = HEADS * HD
    kv_cols = 2 * KV * HD
    vmem_spec = pl.BlockSpec(memory_space=pltpu.VMEM)
    any_spec = pl.BlockSpec(memory_space=pl.ANY)
    return pl.pallas_call(
        front_kernel,
        out_shape=(
            jax.ShapeDtypeStruct((count, width), bf16),
            jax.ShapeDtypeStruct((count, q_cols + kv_cols), f32),
            jax.ShapeDtypeStruct((count, q_cols), bf16),
            jax.ShapeDtypeStruct((8, 4, BLOCK, kv_cols), bf16),
            jax.ShapeDtypeStruct((count, q_cols), bf16),
            jax.ShapeDtypeStruct((count, width), f32),
            jax.ShapeDtypeStruct((count, width), bf16),
            jax.ShapeDtypeStruct((8, 4, BLOCK, width), bf16),
        ),
        in_specs=[
            pl.BlockSpec(memory_space=pltpu.SMEM),
            vmem_spec,
            any_spec,
            any_spec,
            *[vmem_spec] * 7,
        ],
        out_specs=(
            vmem_spec,
            vmem_spec,
            vmem_spec,
            any_spec,
            vmem_spec,
            vmem_spec,
            vmem_spec,
            any_spec,
        ),
        scratch_shapes=[
            pltpu.VMEM((width, q_cols), bf16),
            pltpu.VMEM((width, kv_cols), bf16),
            pltpu.VMEM((q_cols, width), bf16),
            pltpu.VMEM((2, BLOCK, kv_cols), bf16),
            pltpu.VMEM((8, 4, BLOCK, kv_cols), bf16),
            pltpu.VMEM((8, 4, BLOCK, width), bf16),
            pltpu.VMEM((2 * KV, PER_GROUP * BLOCK, KV_COLS), bf16),
            pltpu.VMEM((2, BLOCK, 16 * BLOCK), f32),
            pltpu.VMEM((2 * KV, PER_GROUP * BLOCK, KV_COLS), f32),
            pltpu.VMEM((2 * KV, PER_GROUP * BLOCK, 2 * BLOCK), f32),
            pltpu.SemaphoreType.DMA((32,)),
            pltpu.SemaphoreType.DMA((32,)),
            pltpu.SemaphoreType.DMA((5,)),
        ],
        compiler_params=pltpu.CompilerParams(
            collective_id=2, has_side_effects=True, vmem_limit_bytes=VMEM_BYTES
        ),
        name="front",
    )(starts, x, w_qkv, w_out, g_attn, g_ffn, q_gain, k_gain, cosine, sine, dy)


def rear_kernel(
    starts_ref,
    dh2_ref,
    r1_ref,
    dy_ref,
    x_ref,
    q_ref,
    raw_ref,
    h1_ref,
    mix_ref,
    kva_ref,
    wqkv_ref,
    wout_ref,
    gsum_ref,
    outp_ref,
    ga_ref,
    gf_ref,
    qg_ref,
    kg_ref,
    cos_ref,
    sin_ref,
    y_ref,
    gx_ref,
    gga_ref,
    ggf_ref,
    gq_ref,
    gk_ref,
    gall_ref,
    h1_out,
    da_out,
    dq_out,
    mx_out,
    wbuf,
    wkv,
    kva,
    gsum,
    gl1,
    gl2,
    gboth,
    outp,
    mask,
    d_r1,
    d_o,
    dq,
    d_h1,
    da,
    h1c,
    dac,
    dqc,
    mxc,
    *scratch,
):
    landings, out_landings = scratch[:4], scratch[4:8]
    send, recv, lsem = scratch[8:]
    count, width = x_ref.shape
    q_cols = HEADS * HD
    k_cols = KV * HD
    seq, head = lax.axis_index("seq"), lax.axis_index("head")
    far_rows = (shift(seq, 2), 4 + shift(head, 2))
    loads = [
        pltpu.make_async_copy(outp_ref.at[far_rows[0]], outp.at[far_rows[0]], lsem.at[5]),
        pltpu.make_async_copy(outp_ref.at[far_rows[1]], outp.at[far_rows[1]], lsem.at[6]),
        pltpu.make_async_copy(gsum_ref, gsum, lsem.at[3]),
    ]
    for half in (0, 1):
        for by in (1, 3, 0):
            row = 4 * half + shift(head if half else seq, by)
            loads.append(
                pltpu.make_async_copy(outp_ref.at[row], outp.at[row], lsem.at[7 + 4 * half + by])
            )
    loads += [
        pltpu.make_async_copy(wout_ref, wbuf.at[pl.ds(0, q_cols)], lsem.at[0]),
        pltpu.make_async_copy(kva_ref, kva, lsem.at[1]),
        pltpu.make_async_copy(wqkv_ref.at[:, pl.ds(q_cols, 2 * k_cols)], wkv, lsem.at[2]),
    ]
    for load in loads:
        load.start()
    load_wo, load_kva, load_wkv = loads[-3:]
    load_wq = pltpu.make_async_copy(
        wqkv_ref.at[:, pl.ds(0, q_cols)], wbuf.at[:, pl.ds(0, q_cols)], lsem.at[5]
    )
    copies = Copies(send, recv)
    core = lax.axis_index("dp_1")
    mine, theirs = pl.ds(0, count), pl.ds(count, count)

    def piece(z, which):
        return pl.ds(pl.multiple_of(z * 512 + which * 256, 256), 256)

    barrier_with(("dp_0", "seq", "head"), core=True)
    outs = [PlaneSum(copies, 24, half, outp, *out_landings) for half in (0, 1)]
    loads[0].wait()
    outs[0].far()
    loads[1].wait()
    outs[1].far()
    gring = RingSum(copies, 48, "dp_0", gsum, gl1, gl2)
    grows = gsum.shape[1]
    place = pl.ds(pl.multiple_of(core * grows, 16), grows)
    gfull = gboth.at[:, place]
    gback = RingGather(copies, 54, "dp_0", gfull)
    loads[2].wait()
    gring.start()
    for load in loads[3:9]:
        load.wait()
    for total in outs:
        total.early()
    n2, inv2 = rms_parts(r1_ref[...])
    d_h2 = dh2_ref[...]
    ggf_ref[...] = jnp.sum(d_h2 * n2, axis=0, keepdims=True)
    d_r1[...] = dy_ref[...].astype(f32) + rms_back(d_h2 * gf_ref[...], n2, inv2)
    da[...] = d_r1[...].astype(bf16)
    swaps = [copies.start_to_core(58, mix_ref, mxc.at[theirs])]
    for z in range(4):
        cols = pl.ds(z * 256, 256)
        h1c[mine, cols] = h1_ref[:, piece(z, core)]
        dac[mine, cols] = da[:, piece(z, core)]
        swaps.append(
            copies.start_to_core(60 + 2 * z, h1_ref.at[:, piece(z, 1 - core)], h1c.at[theirs, cols])
        )
        swaps.append(
            copies.start_to_core(61 + 2 * z, da.at[:, piece(z, 1 - core)], dac.at[theirs, cols])
        )
    mxc[mine] = mix_ref[...]
    mask_rows(starts_ref, 0, False, mask)
    mask_rows(starts_ref, 1, True, mask)
    load_wo.wait()
    for g in range(KV):
        cols = slice(g * GROUP_COLS, (g + 1) * GROUP_COLS)
        d_o[:, cols] = nt(da[...], wbuf[cols]).astype(bf16)
    load_wq.start()
    load_kva.wait()
    sums = [PlaneSum(copies, 0, half, kva, *landings) for half in (0, 1)]
    for row in (0, 1):
        rows = slice(row * BLOCK, (row + 1) * BLOCK)
        for g in range(KV):
            cols = slice(g * GROUP_COLS, (g + 1) * GROUP_COLS)
            lanes = slice(g * KV_COLS, (g + 1) * KV_COLS)
            q_rows = stacked(q_ref[rows, cols], 0)
            do_rows = stacked(d_o[rows, cols], 1)
            kv_rows = kva[4 * row : 4 * row + 4, :, :, lanes].reshape(16 * BLOCK, KV_COLS)
            e = weights_of(q_rows, kv_rows, mask[row])
            probs = e * (1.0 / jnp.sum(e, axis=1, keepdims=True))
            d_probs = nt(do_rows, kv_rows)
            delta = jnp.sum(probs * d_probs, axis=1, keepdims=True)
            d_scores = (probs * (d_probs - delta)).astype(bf16)
            dq_rows = nn(d_scores, kv_rows)[:, :HD] * SCALE
            dq[rows, cols] = unstacked(dq_rows.astype(bf16))
            dkv = tn(d_scores, q_rows * jnp.asarray(SCALE, bf16)) + tn(probs.astype(bf16), do_rows)
            kva[4 * row : 4 * row + 4, :, :, lanes] = dkv.astype(bf16).reshape(
                4, 4, BLOCK, KV_COLS
            )
        sums[row].far()
        sums[row].early()
        if row == 0:
            gring.late()
    means = head_means()
    cosine, sine = cos_ref[...], sin_ref[...]

    def queries(g):
        cols = slice(g * GROUP_COLS, (g + 1) * GROUP_COLS)
        value, gain = turned_back(
            dq[:, cols].astype(f32), raw_ref[:, cols], qg_ref[...], cosine, sine, means
        )
        dqc[mine, cols] = value.astype(bf16)
        return gain

    gain = queries(0)
    for g in range(1, KV):
        gain += queries(g)
    gq_ref[...] = gain
    swaps.append(
        copies.start_to_core(
            68, dqc.at[mine, pl.ds(0, q_cols)], dqc.at[theirs, pl.ds(0, q_cols)]
        )
    )
    for total in sums:
        total.late()
    gboth[gring.i, place] = gring.finish()[...]
    gback.step1()
    for total in outs:
        total.late()
    load_wq.wait()
    load_wkv.wait()
    tile = 512
    for n in range(width // tile):
        cols = slice(n * tile, (n + 1) * tile)
        d_h1[:, cols] = nt(dqc[mine, :q_cols], wbuf[cols, :q_cols])
    for total in sums:
        total.inner_start()
    gback.step2()
    for total in sums:
        total.inner_late()
    for total in outs:
        total.inner_start()
    d_kv = jnp.concatenate([total.result().astype(bf16) for total in sums], 0)
    pieces = [d_kv[:, g * KV_COLS : g * KV_COLS + HD] for g in range(KV)]
    pieces += [d_kv[:, g * KV_COLS + HD : (g + 1) * KV_COLS] for g in range(KV)]
    d_kv = jnp.concatenate(pieces, 1)
    first, gain1 = turned_back(
        d_kv[:, :GROUP_COLS].astype(f32),
        raw_ref[:, q_cols : q_cols + GROUP_COLS],
        kg_ref[...],
        cosine,
        sine,
        means,
    )
    second, gain2 = turned_back(
        d_kv[:, GROUP_COLS : 2 * GROUP_COLS].astype(f32),
        raw_ref[:, q_cols + GROUP_COLS : q_cols + 2 * GROUP_COLS],
        kg_ref[...],
        cosine,
        sine,
        means,
    )
    lane = lax.broadcasted_iota(jnp.int32, gain2.shape, 1)
    gk_ref[...] = gain1 + jnp.where(lane < k_cols - GROUP_COLS, gain2, 0.0)
    dqc[mine, q_cols : q_cols + GROUP_COLS] = first.astype(bf16)
    lane = lax.broadcasted_iota(jnp.int32, second.shape, 1)
    dqc[mine, q_cols + GROUP_COLS : q_cols + 2 * GROUP_COLS] = jnp.where(
        lane < k_cols - GROUP_COLS,
        second.astype(bf16),
        d_kv[:, GROUP_COLS : 2 * GROUP_COLS],
    )
    dqc[mine, q_cols + 2 * GROUP_COLS :] = d_kv[:, 2 * GROUP_COLS :]
    kv_part = pl.ds(q_cols, 2 * k_cols)
    swaps.append(copies.start_to_core(69, dqc.at[mine, kv_part], dqc.at[theirs, kv_part]))
    gback.finish()
    gswap = copies.start_to_core(59, gfull, gfull)
    for total in outs:
        total.inner_late()
    for n in range(width // tile):
        cols = slice(n * tile, (n + 1) * tile)
        d_h1[:, cols] += nt(dqc[mine, q_cols:], wkv[cols])
    n1, inv1 = rms_parts(x_ref[...].astype(f32))
    gga_ref[...] = jnp.sum(d_h1[...] * n1, axis=0, keepdims=True)
    gx_ref[...] = (d_r1[...] + rms_back(d_h1[...] * ga_ref[...], n1, inv1)).astype(bf16)
    for half in (0, 1):
        rows = slice(half * BLOCK, (half + 1) * BLOCK)
        y_ref[rows] = (r1_ref[rows] + outs[half].result()).astype(bf16)
    gswap.wait_recv()
    for swap in swaps:
        swap.wait_recv()
    keeps = [
        pltpu.make_async_copy(gboth, gall_ref, lsem.at[4]),
        pltpu.make_async_copy(h1c, h1_out, lsem.at[0]),
        pltpu.make_async_copy(dac, da_out, lsem.at[1]),
        pltpu.make_async_copy(dqc, dq_out, lsem.at[2]),
        pltpu.make_async_copy(mxc, mx_out, lsem.at[3]),
    ]
    for keep in keeps:
        keep.start()
    for keep in keeps:
        keep.wait()
    copies.finish()


def rear(
    starts,
    d_h2,
    r1,
    dy,
    x,
    q,
    raw,
    h1,
    mixed,
    kva,
    w_qkv,
    w_out,
    gsum,
    outp,
    g_attn,
    g_ffn,
    q_gain,
    k_gain,
    cosine,
    sine,
):
    count, width = x.shape
    q_cols = HEADS * HD
    kv_cols = 2 * KV * HD
    vmem_spec = pl.BlockSpec(memory_space=pltpu.VMEM)
    any_spec = pl.BlockSpec(memory_space=pl.ANY)
    both = (gsum.shape[0], 2 * gsum.shape[1], gsum.shape[2])
    pair_shapes = [
        (2 * count, width // 2),
        (2 * count, width // 2),
        (2 * count, q_cols + kv_cols),
        (2 * count, q_cols),
    ]
    return pl.pallas_call(
        rear_kernel,
        out_shape=(
            jax.ShapeDtypeStruct((count, width), bf16),
            jax.ShapeDtypeStruct((count, width), bf16),
            jax.ShapeDtypeStruct((1, width), f32),
            jax.ShapeDtypeStruct((1, width), f32),
            jax.ShapeDtypeStruct((1, GROUP_COLS), f32),
            jax.ShapeDtypeStruct((1, GROUP_COLS), f32),
            jax.ShapeDtypeStruct(both, bf16),
            *[jax.ShapeDtypeStruct(shape, bf16) for shape in pair_shapes],
        ),
        in_specs=[
            pl.BlockSpec(memory_space=pltpu.SMEM),
            *[vmem_spec] * 8,
            *[any_spec] * 5,
            *[vmem_spec] * 6,
        ],
        out_specs=(*[vmem_spec] * 6, *[any_spec] * 5),
        scratch_shapes=[
            pltpu.VMEM((width, width), bf16),
            pltpu.VMEM((width, kv_cols), bf16),
            pltpu.VMEM((8, 4, BLOCK, kv_cols), bf16),
            pltpu.VMEM(gsum.shape, bf16),
            pltpu.VMEM((2, gsum.shape[1] // 2, gsum.shape[2]), bf16),
            pltpu.VMEM((2, *gsum.shape[1:]), bf16),
            pltpu.VMEM(both, bf16),
            pltpu.VMEM((8, 4, BLOCK, width), bf16),
            pltpu.VMEM((2, BLOCK, 16 * BLOCK), f32),
            pltpu.VMEM((count, width), f32),
            pltpu.VMEM((count, q_cols), bf16),
            pltpu.VMEM((count, q_cols), bf16),
            pltpu.VMEM((count, width), f32),
            pltpu.VMEM((count, width), bf16),
            *[pltpu.VMEM(shape, bf16) for shape in pair_shapes],
            *sum_landings(kv_cols),
            *sum_landings(width),
            pltpu.SemaphoreType.DMA((70,)),
            pltpu.SemaphoreType.DMA((70,)),
            pltpu.SemaphoreType.DMA((15,)),
        ],
        compiler_params=pltpu.CompilerParams(
            collective_id=3, has_side_effects=True, vmem_limit_bytes=VMEM_BYTES
        ),
        name="rear",
    )(
        starts,
        d_h2,
        r1,
        dy,
        x,
        q,
        raw,
        h1,
        mixed,
        kva,
        w_qkv,
        w_out,
        gsum,
        outp,
        g_attn,
        g_ffn,
        q_gain,
        k_gain,
        cosine,
        sine,
    )


AXIS_ORDERS = (("dp_0", "seq", "head"), ("seq", "head", "dp_0"), ("head", "dp_0", "seq"))
CHIP_AXES = ("dp_0", "seq", "head")


def projections_kernel(
    h1_ref, da_ref, dq_ref, mix_ref, gain_ref, left_ref, right_ref, gain_out, *scratch
):
    gsum = scratch[0]
    parts = scratch[1:4]
    half1, full1, half2, full2, last = (scratch[4 + 3 * k : 7 + 3 * k] for k in range(5))
    send, recv = scratch[19:]
    copies = Copies(send, recv)
    barrier = pltpu.get_barrier_semaphore()
    core = lax.axis_index("dp_1")
    for axis in CHIP_AXES:
        for by in (1, 2, 3):
            pl.semaphore_signal(
                barrier,
                inc=1,
                device_id={axis: shift(lax.axis_index(axis), by)},
                device_id_type=MESH,
            )
    pl.semaphore_signal(barrier, inc=1, device_id={"dp_1": 1 - core}, device_id_type=MESH)
    pl.semaphore_wait(barrier, 10)
    gain_move = copies.start_to_core(0, gain_ref, gsum.at[3, core])
    widths = [part.shape[4] for part in parts]
    qkv_width = dq_ref.shape[1]
    columns = qkv_width + mix_ref.shape[1]
    split = qkv_width - widths[0]
    sources = (
        ((h1_ref, dq_ref, 0, widths[0], 0),),
        ((h1_ref, dq_ref, widths[0], split, 0), (da_ref, mix_ref, 0, widths[1] - split, split)),
        ((da_ref, mix_ref, widths[1] - split, widths[2], 0),),
    )
    base = 10
    rings = [
        RingSum(copies, base + 6 * k, AXIS_ORDERS[k][0], parts[k], half1[k], full1[k])
        for k in range(3)
    ]
    for k in (2, 1, 0):

        @pl.loop(0, 4)
        def _(z, k=k):
            cols = pl.ds(pl.multiple_of(z * 256, 256), 256)
            for lhs, rhs, first, width, place in sources[k]:
                value = tn(lhs[:, cols], rhs[:, first : first + width]).astype(bf16)
                value = value.reshape(4, 4, 16, width)
                to = slice(place, place + width)
                if k == 0:
                    parts[0][z, :, :, :, to] = value
                elif k == 1:
                    parts[1][:, :, z, :, to] = value
                else:
                    for y in range(4):
                        parts[2][:, z, y, :, to] = value[y]

        rings[k].start()

    def gain_step(k, axis, value):
        i = lax.axis_index(axis)
        gsum[k, i] = value
        out = []
        for n, by in enumerate((1, 2, 3)):
            src = gsum.at[k, i]
            out.append(copies.start(1 + 3 * k + n, src, src, axis, by))
        return out

    def gain_total(k, moves):
        for move in moves:
            move.wait_recv()
        return gsum[k, 0] + gsum[k, 1] + gsum[k, 2] + gsum[k, 3]

    gain_move.wait_recv()
    gsum[3, core] = gain_ref[...]
    total = gsum[3, 0] + gsum[3, 1]
    gmoves = gain_step(0, CHIP_AXES[0], total)
    for k in (2, 1, 0):
        rings[k].late()
    gmoves = gain_step(1, CHIP_AXES[1], gain_total(0, gmoves))
    owns = [None] * 3
    rings2 = [None] * 3
    for k in (2, 1, 0):
        owns[k] = rings[k].finish()
        rings2[k] = RingSum(
            copies, base + 18 + 6 * k, AXIS_ORDERS[k][1], owns[k], half2[k], full2[k]
        )
        rings2[k].start()
    gmoves = gain_step(2, CHIP_AXES[2], gain_total(1, gmoves))
    for k in (2, 1, 0):
        rings2[k].late()
    gain_out[...] = gain_total(2, gmoves)
    ends = [None] * 3
    for k in (2, 1, 0):
        owns[k] = rings2[k].finish()
        axis = AXIS_ORDERS[k][2]
        i = lax.axis_index(axis)
        ends[k] = [
            copies.start(base + 36 + 3 * k + n, owns[k].at[shift(i, by)], last[k].at[n], axis, by)
            for n, by in enumerate((1, 2, 3))
        ]
    starts = (0, widths[0], widths[0] + widths[1])
    for k in (2, 1, 0):
        i = lax.axis_index(AXIS_ORDERS[k][2])
        for end in ends[k]:
            end.wait_recv()
        value = owns[k][i].astype(f32)
        for n in range(3):
            value = value + last[k][n].astype(f32)
        place = starts[k]
        for ref, first, last_col in ((left_ref, 0, qkv_width), (right_ref, qkv_width, columns)):
            low, high = max(first, place), min(last_col, place + widths[k])
            if low < high:
                ref[:, low - first : high - first] = value[:, low - place : high - place]
    copies.finish()


def projections(h1, d_attn, d_qkv, mixed, gains):
    qkv_width = d_qkv.shape[1]
    columns = qkv_width + mixed.shape[1]
    widths = (1536, 1536, columns - 3072)
    vmem_spec = pl.BlockSpec(memory_space=pltpu.VMEM)

    def each(make):
        return [pltpu.VMEM(make(width), bf16) for width in widths]

    return pl.pallas_call(
        projections_kernel,
        out_shape=(
            jax.ShapeDtypeStruct((16, qkv_width), f32),
            jax.ShapeDtypeStruct((16, mixed.shape[1]), f32),
            jax.ShapeDtypeStruct(gains.shape, f32),
        ),
        in_specs=[vmem_spec] * 5,
        out_specs=(vmem_spec,) * 3,
        scratch_shapes=[
            pltpu.VMEM((4, 4, *gains.shape), f32),
            *each(lambda w: (4, 4, 4, 16, w)),
            *each(lambda w: (2, 2, 4, 16, w)),
            *each(lambda w: (2, 4, 4, 16, w)),
            *each(lambda w: (2, 2, 16, w)),
            *each(lambda w: (2, 4, 16, w)),
            *each(lambda w: (3, 16, w)),
            pltpu.SemaphoreType.DMA((55,)),
            pltpu.SemaphoreType.DMA((55,)),
        ],
        compiler_params=pltpu.CompilerParams(
            collective_id=4, has_side_effects=True, vmem_limit_bytes=VMEM_BYTES
        ),
        name="projections",
    )(h1, d_attn, d_qkv, mixed, gains)


def widen_kernel(g_ref, gin_ref, gdn_ref):
    units = gdn_ref.shape[0]
    gin_ref[:, 0, :] = g_ref[:units].astype(f32)
    gin_ref[:, 1, :] = g_ref[units : 2 * units].astype(f32)
    gdn_ref[...] = g_ref[2 * units :].astype(f32)


def widen(g, units):
    tiles, _, tile = g.shape
    return pl.pallas_call(
        widen_kernel,
        grid=(tiles,),
        out_shape=(
            jax.ShapeDtypeStruct((units, 2, tiles * tile), f32),
            jax.ShapeDtypeStruct((units, tiles * tile), f32),
        ),
        in_specs=[pl.BlockSpec((None, 3 * units, tile), lambda n: (n, 0, 0))],
        out_specs=(
            pl.BlockSpec((units, 2, tile), lambda n: (0, 0, n)),
            pl.BlockSpec((units, tile), lambda n: (0, n)),
        ),
        compiler_params=pltpu.CompilerParams(vmem_limit_bytes=VMEM_BYTES),
        name="widen",
    )(g)


def angle_tables(positions, columns):
    lane = jnp.arange(columns)
    freq = jnp.exp((lane % (HD // 2)).astype(f32) * (-2.0 * math.log(10000.0) / HD))
    angle = positions.astype(f32)[:, None] * freq[None, :]
    sign = jnp.where(lane % HD < HD // 2, -1.0, 1.0)
    return (jnp.cos(angle), jnp.sin(angle) * sign[None, :])


def body(
    tokens, w_qkv, w_out, w_ffn_in, w_ffn_out, g_attn, g_ffn, q_gain, k_gain, doc_starts, d_out
):
    rows, tok, width = tokens.shape
    count = rows * tok
    n_seq = lax.axis_size("seq")
    n_head = lax.axis_size("head")
    first = (lax.axis_index("seq") * n_head + lax.axis_index("head")) * tok
    cosine, sine = angle_tables(first + jnp.arange(count) % tok, GROUP_COLS)
    x = tokens.reshape(count, width)
    dy = d_out.reshape(count, width)
    ga = g_attn[None]
    gf = g_ffn[None]
    qg = jnp.tile(q_gain, PER_GROUP)[None]
    kg = jnp.tile(k_gain, PER_GROUP)[None]
    h1, raw, q, kva, mixed, r1, h2, dy_all = front(
        doc_starts, x, w_qkv, w_out, ga, gf, qg, kg, cosine, sine, d_out
    )
    outp, d_h2, gsum = ffn(h2.reshape(rows, tok, width), dy_all, w_ffn_in, w_ffn_out)
    output, grad_x, grad_gattn, grad_gffn, grad_qgain, grad_kgain, gboth, *pairs = rear(
        doc_starts,
        d_h2.reshape(count, width),
        r1,
        dy,
        x,
        q,
        raw,
        h1,
        mixed,
        kva,
        w_qkv,
        w_out,
        gsum,
        outp,
        ga,
        gf,
        qg,
        kg,
        cosine,
        sine,
    )
    gains = jnp.concatenate([grad_gattn, grad_gffn, grad_qgain, grad_kgain], 1)[0]
    gains = jnp.pad(gains, (0, 40 * 128 - gains.shape[0])).reshape(40, 128)
    grad_qkv, grad_out, gains = projections(*pairs, gains)
    grad_in, grad_down = widen(gboth, w_ffn_out.shape[0])
    gains = gains.reshape(-1)
    heads = gains[2 * width : 2 * width + 2 * GROUP_COLS].reshape(2, PER_GROUP, HD).sum(1)
    return (
        output.reshape(rows, tok, width),
        grad_x.reshape(rows, tok, width),
        grad_qkv,
        grad_out.T,
        grad_in,
        grad_down,
        gains[:width],
        gains[width : 2 * width],
        heads[0],
        heads[1],
    )


def solution(mesh):
    split = Mesh(
        mesh.devices.reshape(4, 2, mesh.shape["seq"], mesh.shape["head"]),
        ("dp_0", "dp_1", "seq", "head"),
    )
    return jax.shard_map(
        body,
        mesh=split,
        in_specs=(
            P(DP, ("seq", "head"), None),
            P(),
            P(),
            P(("seq", "head"), None, None),
            P(("seq", "head"), None),
            P(),
            P(),
            P(),
            P(),
            P(DP, None),
            P(DP, ("seq", "head"), None),
        ),
        out_specs=(
            P(DP, ("seq", "head"), None),
            P(DP, ("seq", "head"), None),
            P(DP_SEQ_HEAD, None),
            P(None, DP_SEQ_HEAD),
            P(("seq", "head"), None, None),
            P(("seq", "head"), None),
            P(),
            P(),
            P(),
            P(),
        ),
        check_vma=False,
    )
```

```python
import functools
import math

import jax
import jax.numpy as jnp
from jax import lax
from jax.experimental import pallas as pl
from jax.experimental.pallas import tpu as pltpu
from jax.sharding import Mesh
from jax.sharding import PartitionSpec as P

HEADS = 28
KV = 7
HD = 64
PER_GROUP = HEADS // KV
DP_SEQ_HEAD = ("dp_0", "dp_1", "seq", "head")
DP = ("dp_0", "dp_1")
RING = 4
BLOCK = 64
MESH = pl.DeviceIdType.MESH
EPS = 1e-06
SCALE = 0.125
f32 = jnp.float32
bf16 = jnp.bfloat16
VMEM_BYTES = 62 * 2**20


def nt(a, b):
    return lax.dot_general(a, b, (((1,), (1,)), ((), ())), preferred_element_type=f32)


def nn(a, b):
    return lax.dot_general(a, b, (((1,), (0,)), ((), ())), preferred_element_type=f32)


def tn(a, b):
    return lax.dot_general(a, b, (((0,), (0,)), ((), ())), preferred_element_type=f32)


def shift(index, by):
    return lax.rem(index + (by + RING), RING)


def barrier_with(partners, core=False):
    barrier = pltpu.get_barrier_semaphore()
    for axis, by in partners:
        pl.semaphore_signal(
            barrier,
            inc=1,
            device_id={axis: shift(lax.axis_index(axis), by)},
            device_id_type=MESH,
        )
    if core:
        other = 1 - lax.axis_index("dp_1")
        pl.semaphore_signal(barrier, inc=1, device_id={"dp_1": other}, device_id_type=MESH)
    pl.semaphore_wait(barrier, len(partners) + int(core))


PLANE = (("seq", 1), ("seq", -1), ("head", 1), ("head", -1))
PAIRED = (("seq", 2), ("head", 1), ("head", -1))
STACK = (("dp_0", 1), ("dp_0", -1))


class Copies:
    def __init__(self, send, recv):
        self.send = send
        self.recv = recv
        self.started = []

    def start(self, slot, src, dst, axis, by):
        copy = pltpu.make_async_remote_copy(
            src_ref=src,
            dst_ref=dst,
            send_sem=self.send.at[slot],
            recv_sem=self.recv.at[slot],
            device_id={axis: shift(lax.axis_index(axis), by)},
            device_id_type=MESH,
        )
        copy.start()
        self.started.append(copy)
        return copy

    def start_to_core(self, slot, src, dst):
        copy = pltpu.make_async_remote_copy(
            src_ref=src,
            dst_ref=dst,
            send_sem=self.send.at[slot],
            recv_sem=self.recv.at[slot],
            device_id={"dp_1": 1 - lax.axis_index("dp_1")},
            device_id_type=MESH,
        )
        copy.start()
        self.started.append(copy)
        return copy

    def finish(self):
        for copy in self.started:
            copy.wait_send()


INNER = ("head", "seq")
GROUP = ("seq", "head")


class PlaneGather:
    def __init__(self, copies, base, half, own, buf):
        self.c = copies
        self.base = base + 8 * half
        self.half = half
        self.own = own
        self.buf = buf
        self.i = lax.axis_index(INNER[half])
        self.g = lax.axis_index(GROUP[half])

    def row(self, by=0):
        return 4 * self.half + shift(self.g, by)

    def step1(self):
        ax = INNER[self.half]
        dst = self.buf.at[self.row(), self.i]
        self.a = self.c.start(self.base, self.own, dst, ax, 1)
        self.b = self.c.start(self.base + 1, self.own, dst, ax, -1)

    def step2(self):
        ax = INNER[self.half]
        n = self.buf.shape[2] // 2
        self.a.wait_recv()
        left = self.buf.at[self.row(), shift(self.i, -1), pl.ds(0, n)]
        self.a = self.c.start(self.base + 2, left, left, ax, 1)
        self.b.wait_recv()
        right = self.buf.at[self.row(), shift(self.i, 1), pl.ds(n, n)]
        self.b = self.c.start(self.base + 3, right, right, ax, -1)

    def step3(self):
        ax = GROUP[self.half]
        self.a.wait_recv()
        self.b.wait_recv()
        rows = self.buf.at[self.row()]
        self.a = self.c.start(self.base + 4, rows, rows, ax, 1)
        self.b = self.c.start(self.base + 5, rows, rows, ax, -1)

    def step4(self):
        ax = GROUP[self.half]
        self.a.wait_recv()
        left = self.buf.at[self.row(-1), pl.ds(0, 2)]
        self.a = self.c.start(self.base + 6, left, left, ax, 1)
        self.b.wait_recv()
        right = self.buf.at[self.row(1), pl.ds(2, 2)]
        self.b = self.c.start(self.base + 7, right, right, ax, -1)

    def finish(self):
        self.a.wait_recv()
        self.b.wait_recv()


class PlaneSum:
    def __init__(self, copies, base, half, part, land1, land2, land3, land4):
        self.c = copies
        self.base = base + 12 * half
        self.half = half
        self.part = part
        self.l1, self.l2, self.l3, self.l4 = (
            ref.at[half] for ref in (land1, land2, land3, land4)
        )
        self.i = lax.axis_index(INNER[half])
        self.g = lax.axis_index(GROUP[half])

    def row(self, by=0):
        return 4 * self.half + shift(self.g, by)

    def add(self, ref, other):
        ref[...] = (ref[...].astype(f32) + other[...].astype(f32)).astype(ref.dtype)

    def far(self):
        ax = GROUP[self.half]
        row = self.row(2)
        self.a = self.c.start(self.base, self.part.at[row, pl.ds(0, 2)], self.l1.at[0], ax, 1)
        self.b = self.c.start(self.base + 1, self.part.at[row, pl.ds(2, 2)], self.l1.at[1], ax, -1)

    def early(self):
        ax = GROUP[self.half]
        one, two = pl.ds(0, 2), pl.ds(2, 2)
        right, left = self.part.at[self.row(1)], self.part.at[self.row(-1)]
        self.ea = self.c.start(self.base + 2, right.at[two], self.l2.at[0, two], ax, 1)
        self.eb = self.c.start(self.base + 3, left.at[one], self.l2.at[1, one], ax, -1)

    def late(self):
        ax = GROUP[self.half]
        one, two = pl.ds(0, 2), pl.ds(2, 2)
        right, left = self.part.at[self.row(1), one], self.part.at[self.row(-1), two]
        self.a.wait_recv()
        self.add(right, self.l1.at[0])
        self.a = self.c.start(self.base + 4, right, self.l2.at[0, one], ax, 1)
        self.b.wait_recv()
        self.add(left, self.l1.at[1])
        self.b = self.c.start(self.base + 5, left, self.l2.at[1, two], ax, -1)

    def inner_start(self):
        ax = INNER[self.half]
        n = self.part.shape[2] // 2
        one, two = pl.ds(0, n), pl.ds(n, n)
        for copy in (self.ea, self.eb, self.a, self.b):
            copy.wait_recv()
        rows = self.part.at[self.row()]

        def sum_of(k):
            rows[k] = (
                rows[k].astype(f32) + self.l2[0, k].astype(f32) + self.l2[1, k].astype(f32)
            ).astype(rows.dtype)

        sum_of(shift(self.i, 2))
        block = rows.at[shift(self.i, 2)]
        self.a = self.c.start(self.base + 6, block.at[one], self.l3.at[0], ax, 1)
        self.b = self.c.start(self.base + 7, block.at[two], self.l3.at[1], ax, -1)
        sum_of(shift(self.i, 1))
        sum_of(shift(self.i, -1))
        right, left = rows.at[shift(self.i, 1)], rows.at[shift(self.i, -1)]
        self.ea = self.c.start(self.base + 8, right.at[two], self.l4.at[0, two], ax, 1)
        self.eb = self.c.start(self.base + 9, left.at[one], self.l4.at[1, one], ax, -1)
        sum_of(self.i)

    def inner_late(self):
        ax = INNER[self.half]
        n = self.part.shape[2] // 2
        one, two = pl.ds(0, n), pl.ds(n, n)
        right = self.part.at[self.row(), shift(self.i, 1), one]
        left = self.part.at[self.row(), shift(self.i, -1), two]
        self.a.wait_recv()
        self.add(right, self.l3.at[0])
        self.a = self.c.start(self.base + 10, right, self.l4.at[0, one], ax, 1)
        self.b.wait_recv()
        self.add(left, self.l3.at[1])
        self.b = self.c.start(self.base + 11, left, self.l4.at[1, two], ax, -1)

    def result(self):
        for copy in (self.ea, self.eb, self.a, self.b):
            copy.wait_recv()
        own = self.part[self.row(), self.i].astype(f32)
        return own + self.l4[0].astype(f32) + self.l4[1].astype(f32)


def sum_landings(columns):
    return [
        pltpu.VMEM((2, 2, 2, BLOCK, columns), bf16),
        pltpu.VMEM((2, 2, 4, BLOCK, columns), bf16),
        pltpu.VMEM((2, 2, BLOCK // 2, columns), bf16),
        pltpu.VMEM((2, 2, BLOCK, columns), bf16),
    ]


class RingSum:
    def __init__(self, copies, base, axis, part, half_land, full_land):
        self.c = copies
        self.base = base
        self.axis = axis
        self.part = part
        self.hl = half_land
        self.fl = full_land
        self.i = lax.axis_index(axis)
        n = part.shape[1] // 2
        self.one, self.two = pl.ds(0, n), pl.ds(n, n)

    def start(self):
        self.far()
        self.early()

    def far(self):
        far = self.part.at[shift(self.i, 2)]
        self.a = self.c.start(self.base, far.at[self.one], self.hl.at[0], self.axis, 1)
        self.b = self.c.start(self.base + 1, far.at[self.two], self.hl.at[1], self.axis, -1)

    def early(self):
        right, left = self.part.at[shift(self.i, 1)], self.part.at[shift(self.i, -1)]
        one, two, ax = self.one, self.two, self.axis
        self.ea = self.c.start(self.base + 2, right.at[two], self.fl.at[0, two], ax, 1)
        self.eb = self.c.start(self.base + 3, left.at[one], self.fl.at[1, one], ax, -1)

    def late(self):
        right = self.part.at[shift(self.i, 1), self.one]
        left = self.part.at[shift(self.i, -1), self.two]
        self.a.wait_recv()
        right[...] = (right[...].astype(f32) + self.hl[0].astype(f32)).astype(bf16)
        self.a = self.c.start(self.base + 4, right, self.fl.at[0, self.one], self.axis, 1)
        self.b.wait_recv()
        left[...] = (left[...].astype(f32) + self.hl[1].astype(f32)).astype(bf16)
        self.b = self.c.start(self.base + 5, left, self.fl.at[1, self.two], self.axis, -1)

    def finish(self):
        for copy in (self.ea, self.eb, self.a, self.b):
            copy.wait_recv()
        own = self.part.at[self.i]
        own[...] = (
            own[...].astype(f32) + self.fl[0].astype(f32) + self.fl[1].astype(f32)
        ).astype(bf16)
        return own


class RingGather:
    def __init__(self, copies, base, axis, full):
        self.c = copies
        self.base = base
        self.axis = axis
        self.full = full
        self.i = lax.axis_index(axis)

    def step1(self):
        own = self.full.at[self.i]
        self.a = self.c.start(self.base, own, own, self.axis, 1)
        self.b = self.c.start(self.base + 1, own, own, self.axis, -1)

    def step2(self):
        n = self.full.shape[1] // 2
        self.a.wait_recv()
        left = self.full.at[shift(self.i, -1), pl.ds(0, n)]
        self.a = self.c.start(self.base + 2, left, left, self.axis, 1)
        self.b.wait_recv()
        right = self.full.at[shift(self.i, 1), pl.ds(n, n)]
        self.b = self.c.start(self.base + 3, right, right, self.axis, -1)

    def finish(self):
        self.a.wait_recv()
        self.b.wait_recv()


class RingThenPair:
    def __init__(self, copies, base, buf):
        self.c = copies
        self.base = base
        self.buf = buf
        self.i = lax.axis_index("head")

    def pair(self, slot, index):
        return self.c.start(
            self.base + slot, self.buf.at[index, 0], self.buf.at[index, 1], "seq", 2
        )

    def start(self):
        own = self.buf.at[self.i, 0]
        self.a = self.c.start(self.base, own, own, "head", 1)
        self.b = self.c.start(self.base + 1, own, own, "head", -1)
        self.pairs = [self.pair(2, self.i)]

    def forward(self):
        n = self.buf.shape[2] // 2
        left, right = shift(self.i, -1), shift(self.i, 1)
        self.a.wait_recv()
        block = self.buf.at[left, 0, pl.ds(0, n)]
        self.a = self.c.start(self.base + 3, block, block, "head", 1)
        self.b.wait_recv()
        block = self.buf.at[right, 0, pl.ds(n, n)]
        self.b = self.c.start(self.base + 4, block, block, "head", -1)
        self.pairs += [self.pair(5, left), self.pair(6, right)]

    def last(self):
        self.a.wait_recv()
        self.b.wait_recv()
        self.pairs.append(self.pair(7, shift(self.i, 2)))

    def finish(self):
        for copy in self.pairs:
            copy.wait_recv()


class PairThenRing:
    def __init__(self, copies, base, buf):
        self.c = copies
        self.base = base
        self.buf = buf
        self.gather = RingGather(copies, base + 1, "head", buf)

    def start(self):
        i = self.gather.i
        self.pair = self.c.start(
            self.base, self.buf.at[i, 0], self.buf.at[i, 1], "seq", 2
        )

    def ring(self):
        self.pair.wait_recv()
        self.gather.step1()

    def forward(self):
        self.gather.step2()

    def finish(self):
        self.gather.finish()


class PairThenRingSum:
    def __init__(self, copies, base, part, pair_land, half_land, full_land):
        self.c = copies
        self.base = base
        self.part = part
        self.pl = pair_land
        self.ring = RingSum(copies, base + 4, "head", part.at[:, 0], half_land, full_land)
        self.i = self.ring.i

    def start(self):
        self.pairs = []
        for n, by in enumerate((2, 1, 3, 0)):
            j = shift(self.i, by)
            self.pairs.append(
                self.c.start(self.base + n, self.part.at[j, 1], self.pl.at[j], "seq", 2)
            )

    def added(self, n, by):
        self.pairs[n].wait_recv()
        j = shift(self.i, by)
        self.part[j, 0] = (self.part[j, 0].astype(f32) + self.pl[j].astype(f32)).astype(bf16)

    def along(self):
        self.added(0, 2)
        self.ring.far()
        self.added(1, 1)
        self.added(2, 3)
        self.ring.early()
        self.added(3, 0)

    def late(self):
        self.ring.late()

    def result(self):
        return self.ring.finish()[...].astype(f32)


class TwoRings:
    def __init__(self, copies, base, buf):
        self.c = copies
        self.base = base
        self.buf = buf
        self.own = RingGather(copies, base + 1, "head", buf.at[:, 0])
        self.other = RingGather(copies, base + 5, "head", buf.at[:, 1])

    def pair(self):
        i = self.own.i
        self.p = self.c.start(self.base, self.buf.at[i, 0], self.buf.at[i, 1], "seq", 2)

    def other_step1(self):
        self.p.wait_recv()
        self.other.step1()

    def finish(self):
        self.own.finish()
        self.other.finish()


class RingThenPairSum:
    def __init__(self, copies, base, part, pair_land, half_land, full_land):
        self.c = copies
        self.base = base
        self.pl = pair_land
        self.ring = RingSum(copies, base + 1, "head", part, half_land, full_land)
        self.far, self.early, self.late = self.ring.far, self.ring.early, self.ring.late

    def pair(self):
        self.own = self.ring.finish()
        self.p = self.c.start(self.base, self.own.at[1], self.pl, "seq", 2)

    def result(self):
        self.p.wait_recv()
        return self.own[0].astype(f32) + self.pl[...].astype(f32)


def ring_then_pair_landings(columns):
    return [
        pltpu.VMEM((BLOCK, columns), bf16),
        pltpu.VMEM((2, 1, BLOCK, columns), bf16),
        pltpu.VMEM((2, 2, BLOCK, columns), bf16),
    ]


def pair_then_ring_landings(columns):
    return [
        pltpu.VMEM((4, BLOCK, columns), bf16),
        pltpu.VMEM((2, BLOCK // 2, columns), bf16),
        pltpu.VMEM((2, BLOCK, columns), bf16),
    ]


def mate():
    return 1 - 2 * lax.rem(lax.axis_index("seq"), 2)


UNIT = 4 * BLOCK


def ffn_kernel(
    h2_ref,
    dy_ref,
    win_ref,
    wdn_ref,
    w_ref,
    outp_ref,
    dh2_ref,
    gsum_ref,
    h2a,
    dya,
    pairs,
    win,
    wdn,
    hid,
    dbo,
    dpt,
    *scratch,
):
    land_a, land_b = scratch[:3], scratch[3:6]
    stage, gst, gland, send, recv, lsem, osem = scratch[6:]
    share = gst.shape[2] // 3
    units, width = wdn.shape
    copies = Copies(send, recv)
    i = lax.axis_index("head")
    part = pairs.shape[0]
    load_pairs = [
        pltpu.make_async_copy(win_ref.at[pl.ds(n * part, part)], pairs, lsem.at[n])
        for n in (0, 1)
    ]
    loads = [
        pltpu.make_async_copy(dy_ref, dya, lsem.at[2]),
        pltpu.make_async_copy(wdn_ref, wdn.at[pl.ds(0, share)], lsem.at[3]),
        pltpu.make_async_copy(
            w_ref.at[pl.ds(2 * share, share)], wdn.at[pl.ds(share, share)], lsem.at[4]
        ),
        pltpu.make_async_copy(w_ref.at[pl.ds(0, share)], win.at[pl.ds(share, share)], lsem.at[5]),
        pltpu.make_async_copy(
            w_ref.at[pl.ds(share, share)], win.at[pl.ds(units + share, share)], lsem.at[6]
        ),
    ]
    for load in (load_pairs[0], *loads):
        load.start()

    def split_pairs(n):
        first = n * part
        win[first : first + part] = pairs[:, 0, :]
        win[units + first : units + first + part] = pairs[:, 1, :]

    barrier_with(PAIRED, core=True)
    for half in (0, 1):
        h2a[half, i, 0] = h2_ref[half]
    gather_a = RingThenPair(copies, 0, h2a.at[0])
    gather_b = PairThenRing(copies, 8, h2a.at[1])
    gather_b.start()
    gather_a.start()

    def places(u):
        if u < 2:
            return None
        return (shift(i, 1), shift(i, -1)) if u == 2 else (i, shift(i, 2))

    def tokens_of(ref, u, cols=slice(None)):
        if u < 2:
            value = ref[0, :, u, :, cols]
            return value.reshape(UNIT, value.shape[-1])
        values = [ref[1, j, :, :, cols] for j in places(u)]
        return jnp.concatenate([v.reshape(UNIT // 2, v.shape[-1]) for v in values], 0)

    def columns_of(u):
        return slice(u * UNIT, (u + 1) * UNIT)

    def hidden_back(u):
        dbo[:units, columns_of(u)] = nt(wdn[...], tokens_of(dya, u)).astype(bf16)

    def forward(u):
        cols = columns_of(u)
        t = tokens_of(h2a, u)
        for s in (0, 1):
            one = slice(s * share, (s + 1) * share)
            two = slice(units + s * share, units + (s + 1) * share)
            gate = nt(win[one], t)
            up = nt(win[two], t)
            sig = 1.0 / (1.0 + jnp.exp(-gate))
            act = gate * sig
            d_hidden = dbo[one, cols].astype(f32)
            hid[one, cols] = (act * up).astype(bf16)
            dbo[one, cols] = (d_hidden * up * (sig * (1.0 + gate * (1.0 - sig)))).astype(bf16)
            dbo[two, cols] = (d_hidden * act).astype(bf16)

    def back(u):
        value = tn(dbo[:, columns_of(u)], win[...]).astype(bf16)
        if u < 2:
            dpt[0, :, u] = value.reshape(4, BLOCK, width)
        else:
            for n, j in enumerate(places(u)):
                dpt[1, j] = value[n * UNIT // 2 : (n + 1) * UNIT // 2].reshape(2, BLOCK, width)

    load_pairs[0].wait()
    split_pairs(0)
    load_pairs[1].start()
    gather_b.ring()
    gather_a.forward()
    load_pairs[1].wait()
    split_pairs(1)
    gather_a.last()
    for load in loads:
        load.wait()
    hidden_back(0)
    forward(0)
    gather_b.forward()
    for u in (2, 1, 3):
        hidden_back(u)
    sum_a = PairThenRingSum(copies, 16, dpt.at[0], *land_a)
    sum_b = RingThenPairSum(copies, 26, dpt.at[1], *land_b)
    forward(2)
    back(2)
    sum_b.early()
    gather_a.finish()
    forward(1)
    back(1)
    sum_a.start()
    gather_b.finish()
    forward(3)
    back(3)
    sum_b.far()
    back(0)

    tiles, half_rows, tile = gland.shape[0], gland.shape[2], gland.shape[3]
    core = lax.axis_index("dp_1")
    mine = pl.ds(pl.multiple_of(core * half_rows, 16), half_rows)
    theirs = pl.ds(pl.multiple_of((1 - core) * half_rows, 16), half_rows)
    swaps = []

    def gradients(n):
        cols = slice(n * tile, (n + 1) * tile)
        value = nn(
            dbo[...], jnp.concatenate([tokens_of(h2a, u, cols) for u in range(4)], 0)
        ).astype(bf16)
        down = nn(
            hid[...], jnp.concatenate([tokens_of(dya, u, cols) for u in range(4)], 0)
        ).astype(bf16)
        for s in (0, 1):
            gst[n, s, :share] = value[s * share : (s + 1) * share]
            gst[n, s, share : 2 * share] = value[units + s * share : units + (s + 1) * share]
            gst[n, s, 2 * share :] = down[s * share : (s + 1) * share]
        swaps.append(copies.start_to_core(34 + n, gst.at[n, :, theirs], gland.at[n]))

    def out_copies(u):
        slot = stage.at[u % 2]
        if u < 2:
            return [pltpu.make_async_copy(slot, outp_ref.at[0, :, u], osem.at[u % 2, 0])]
        return [
            pltpu.make_async_copy(
                slot.at[pl.ds(2 * n, 2)], outp_ref.at[1, j], osem.at[u % 2, n]
            )
            for n, j in enumerate(places(u))
        ]

    def out_part(u):
        if u >= 2:
            for copy in out_copies(u - 2):
                copy.wait()
        value = tn(hid[:, columns_of(u)], wdn[...])
        stage[u % 2] = value.astype(bf16).reshape(4, BLOCK, width)
        for copy in out_copies(u):
            copy.start()

    gradients(0)
    gradients(1)
    sum_b.late()
    gradients(2)
    gradients(3)
    sum_b.pair()
    out_part(0)
    sum_a.along()
    out_part(1)
    sum_a.late()
    out_part(2)
    dh2_ref[1] = sum_b.result()
    out_part(3)
    for n, swap in enumerate(swaps):
        swap.wait_recv()
        gland[n] = (gst[n, :, mine].astype(f32) + gland[n].astype(f32)).astype(bf16)
    keep = pltpu.make_async_copy(gland, gsum_ref, lsem.at[0])
    keep.start()
    dh2_ref[0] = sum_a.result()
    for u in (2, 3):
        for copy in out_copies(u):
            copy.wait()
    keep.wait()
    copies.finish()


def ffn(h2, dy_all, w_in, w_down, weights):
    share, width = w_down.shape
    tokens = 4 * UNIT
    tile = 512
    any_spec = pl.BlockSpec(memory_space=pl.ANY)
    vmem_spec = pl.BlockSpec(memory_space=pltpu.VMEM)
    buffer = (2, 4, 2, BLOCK, width)
    sums = (width // tile, 2, 3 * share // 2, tile)
    return pl.pallas_call(
        ffn_kernel,
        out_shape=(
            jax.ShapeDtypeStruct(buffer, bf16),
            jax.ShapeDtypeStruct((2, BLOCK, width), f32),
            jax.ShapeDtypeStruct(sums, bf16),
        ),
        in_specs=[vmem_spec, *[any_spec] * 4],
        out_specs=(any_spec, vmem_spec, any_spec),
        scratch_shapes=[
            pltpu.VMEM(buffer, bf16),
            pltpu.VMEM(buffer, bf16),
            pltpu.VMEM((share // 2, 2, width), bf16),
            pltpu.VMEM((4 * share, width), bf16),
            pltpu.VMEM((2 * share, width), bf16),
            pltpu.VMEM((2 * share, tokens), bf16),
            pltpu.VMEM((4 * share, tokens), bf16),
            pltpu.VMEM(buffer, bf16),
            *pair_then_ring_landings(width),
            *ring_then_pair_landings(width),
            pltpu.VMEM((2, 4, BLOCK, width), bf16),
            pltpu.VMEM((width // tile, 2, 3 * share, tile), bf16),
            pltpu.VMEM(sums, bf16),
            pltpu.SemaphoreType.DMA((38,)),
            pltpu.SemaphoreType.DMA((38,)),
            pltpu.SemaphoreType.DMA((7,)),
            pltpu.SemaphoreType.DMA((2, 2)),
        ],
        compiler_params=pltpu.CompilerParams(
            collective_id=1, has_side_effects=True, vmem_limit_bytes=VMEM_BYTES
        ),
        name="ffn",
    )(h2, dy_all, w_in, w_down, weights)


def mask_rows(starts_ref, row, transposed, mask_ref):
    seq, head = lax.axis_index("seq"), lax.axis_index("head")
    keys = 16 * BLOCK
    index = lax.broadcasted_iota(jnp.int32, (1, keys), 1)
    if transposed:
        group = lax.div(index, 4 * BLOCK)
        inner = lax.rem(lax.div(index, BLOCK), 4)
        k_pos = (inner * 4 + group) * BLOCK + lax.rem(index, BLOCK)
    else:
        k_pos = index
    first = (seq * 4 + head) * BLOCK
    q_pos = first + lax.broadcasted_iota(jnp.int32, (BLOCK, 1), 0)
    k_doc = jnp.zeros((1, keys), jnp.int32)
    q_doc = jnp.zeros((BLOCK, 1), jnp.int32)
    for d in range(starts_ref.shape[1]):
        start = starts_ref[row, d]
        k_doc += (start <= k_pos).astype(jnp.int32)
        q_doc += (start <= q_pos).astype(jnp.int32)
    seen = (k_pos <= q_pos) & (k_doc == q_doc)
    mask_ref[row] = seen.astype(f32)


LOG2E_SCALE = SCALE * math.log2(math.e)


def stacked(block, where):
    rows = jnp.concatenate([block[:, h * HD : (h + 1) * HD] for h in range(PER_GROUP)], 0)
    zero = jnp.zeros_like(rows)
    return jnp.concatenate([rows, zero] if where == 0 else [zero, rows], 1)


def unstacked(rows):
    return jnp.concatenate([rows[h * BLOCK : (h + 1) * BLOCK] for h in range(PER_GROUP)], 1)


def weights_of(q_rows, kv_rows, mask):
    scores = nt(q_rows, kv_rows)
    keys = kv_rows.shape[0]
    e = jnp.exp2(scores * LOG2E_SCALE).reshape(PER_GROUP, BLOCK, keys) * mask[None]
    return e.reshape(PER_GROUP * BLOCK, keys)


GROUP_COLS = PER_GROUP * HD
KV_COLS = 2 * HD


def head_means(columns=GROUP_COLS):
    a = lax.div(lax.broadcasted_iota(jnp.int32, (columns, columns), 0), HD)
    b = lax.div(lax.broadcasted_iota(jnp.int32, (columns, columns), 1), HD)
    return jnp.where(a == b, 1.0 / HD, 0.0).astype(f32)


def head_mean(v, means):
    return jnp.dot(v, means, precision=lax.Precision.HIGHEST, preferred_element_type=f32)


def swapped(v):
    columns = v.shape[1]
    lane = lax.rem(lax.broadcasted_iota(jnp.int32, v.shape, 1), HD)
    up = pltpu.roll(v, columns - HD // 2, 1)
    down = pltpu.roll(v, HD // 2, 1)
    return jnp.where(lane < HD // 2, up, down)


def turned(raw, gain, cosine, sine, means):
    normed = raw * lax.rsqrt(head_mean(raw * raw, means) + EPS)
    v = normed * gain
    return v * cosine + swapped(v) * sine


def turned_back(grad, raw, gain, cosine, sine, means):
    inverse = lax.rsqrt(head_mean(raw * raw, means) + EPS)
    normed = raw * inverse
    u = grad * cosine - swapped(grad) * sine
    gain_grad = jnp.sum(u * normed, axis=0, keepdims=True)
    e = u * gain
    return inverse * (e - normed * head_mean(e * normed, means)), gain_grad


def rms_parts(v):
    inverse = lax.rsqrt(jnp.mean(v * v, axis=-1, keepdims=True) + EPS)
    return (v * inverse, inverse)


def rms_back(grad, normed, inverse):
    return inverse * (grad - normed * jnp.mean(grad * normed, axis=-1, keepdims=True))


def front_kernel(
    starts_ref,
    x_ref,
    wqkv_ref,
    wout_ref,
    ga_ref,
    gf_ref,
    qg_ref,
    kg_ref,
    cos_ref,
    sin_ref,
    dy_ref,
    win_ref,
    wdn_ref,
    h1_ref,
    raw_ref,
    q_ref,
    kva_ref,
    mixed_ref,
    r1_ref,
    h2_ref,
    dya_ref,
    w_ref,
    wq,
    wkv,
    wo,
    own,
    kva,
    dya,
    pown,
    wsend,
    wall,
    qst,
    mask,
    oacc,
    lacc,
    send,
    recv,
    lsem,
):
    count, width = x_ref.shape
    q_cols = HEADS * HD
    k_cols = KV * HD
    loads = [
        pltpu.make_async_copy(wqkv_ref.at[:, pl.ds(q_cols, 2 * k_cols)], wkv, lsem.at[0]),
        pltpu.make_async_copy(wqkv_ref.at[:, pl.ds(0, q_cols)], wq, lsem.at[1]),
        pltpu.make_async_copy(wout_ref, wo, lsem.at[2]),
    ]
    share = wdn_ref.shape[0]
    z, core = lax.axis_index("dp_0"), lax.axis_index("dp_1")
    strip = wsend.shape[1]
    strip_cols = pl.ds(pl.multiple_of((z * 2 + core) * strip, strip), strip)
    strips = [
        pltpu.make_async_copy(win_ref.at[:, :, strip_cols], pown, lsem.at[5]),
        pltpu.make_async_copy(
            wdn_ref.at[:, strip_cols], wsend.at[pl.ds(2 * share, share)], lsem.at[6]
        ),
    ]
    for load in strips + loads:
        load.start()
    copies = Copies(send, recv)
    barrier_with(PLANE + STACK + (("seq", 2),), core=True)
    head = lax.axis_index("head")
    for half in (0, 1):
        dya[half, head, 0] = dy_ref[half]
    cotangents = [TwoRings(copies, 16 + 9 * half, dya.at[half]) for half in (0, 1)]
    cotangents[0].own.step1()
    for load in strips:
        load.wait()
    wsend[:share] = pown[:, 0, :]
    wsend[share : 2 * share] = pown[:, 1, :]
    strip_move = copies.start(34, wsend, wall.at[z, core], "seq", mate())
    stack = RingGather(copies, 35, "dp_0", wall.at[:, core])
    strip_swaps = []

    def swap_strip(by):
        block = wall.at[shift(z, by), core]
        strip_swaps.append(copies.start_to_core(39 + by % 4, block, block))

    means = head_means()
    cosine, sine = cos_ref[...], sin_ref[...]
    q_gain, k_gain = (jnp.concatenate([ref[...]] * PER_GROUP, 1) for ref in (qg_ref, kg_ref))
    x = x_ref[...].astype(f32)
    h1_ref[...] = (rms_parts(x)[0] * ga_ref[...]).astype(bf16)
    loads[0].wait()
    kv = nn(h1_ref[...], wkv[...])
    raw_ref[:, q_cols:] = kv
    keys = jnp.concatenate(
        [
            turned(kv[:, c : c + GROUP_COLS], k_gain, cosine, sine, means)
            for c in (0, GROUP_COLS)
        ],
        1,
    )
    for g in range(KV):
        k = keys[:, g * HD : (g + 1) * HD]
        v = kv[:, k_cols + g * HD : k_cols + (g + 1) * HD]
        own[:, :, g * KV_COLS : (g + 1) * KV_COLS] = (
            jnp.concatenate([k, v], 1).astype(bf16).reshape(2, BLOCK, KV_COLS)
        )
    gathers = [PlaneGather(copies, 0, half, own.at[half], kva) for half in (0, 1)]
    for gather in gathers:
        gather.step1()
    for half in (0, 1):
        kva[gathers[half].row(), gathers[half].i] = own[half]
    loads[1].wait()

    def queries(g):
        cols = slice(g * GROUP_COLS, (g + 1) * GROUP_COLS)
        raw = nn(h1_ref[...], wq[:, cols])
        raw_ref[:, cols] = raw
        q = turned(raw, q_gain, cosine, sine, means).astype(bf16)
        q_ref[:, cols] = q
        for row in (0, 1):
            qst[row * KV + g] = stacked(q[row * BLOCK : (row + 1) * BLOCK], 0)

    for g in range(3):
        queries(g)
    for gather in gathers:
        gather.step2()
    for g in range(3, KV):
        queries(g)
    for gather in gathers:
        gather.step3()
    mask_rows(starts_ref, 0, False, mask)
    mask_rows(starts_ref, 1, True, mask)
    seq = lax.axis_index("seq")

    def scored(row, by, first):
        group = lax.rem(seq + row * (head - seq) + by + 4, 4)
        seen = mask[row, :, pl.ds(pl.multiple_of(group * 4 * BLOCK, 4 * BLOCK), 4 * BLOCK)]
        for g in range(KV):
            index = row * KV + g
            kv_rows = kva[
                4 * row + group, :, :, g * KV_COLS : (g + 1) * KV_COLS
            ].reshape(4 * BLOCK, KV_COLS)
            e = weights_of(qst[index], kv_rows, seen)
            total = e[:, : 2 * BLOCK] + e[:, 2 * BLOCK :]
            mixed = nn(e.astype(bf16), kv_rows)
            if first:
                lacc[index] = total
                oacc[index] = mixed
            else:
                lacc[index] += total
                oacc[index] += mixed

    @pl.loop(0, 2)
    def _(row):
        scored(row, 0, True)

    strip_move.wait_recv()
    stack.step1()
    swap_strip(0)
    for gather in gathers:
        gather.step4()
    for gather in cotangents:
        gather.pair()
    cotangents[0].own.step2()
    cotangents[1].own.step1()

    @pl.loop(0, 4)
    def _(k):
        scored(lax.div(k, 2), 1 - 2 * lax.rem(k, 2), False)

    for gather in gathers:
        gather.finish()
    keep = pltpu.make_async_copy(kva, kva_ref, lsem.at[3])
    keep.start()

    @pl.loop(0, 2)
    def _(row):
        scored(row, 2, False)

    for row in (0, 1):
        for g in range(KV):
            index = row * KV + g
            mixed = oacc[index][:, HD:] / jnp.sum(lacc[index], axis=1, keepdims=True)
            mixed_ref[
                row * BLOCK : (row + 1) * BLOCK, g * GROUP_COLS : (g + 1) * GROUP_COLS
            ] = unstacked(mixed.astype(bf16))
    cotangents[1].own.step2()
    for gather in cotangents:
        gather.other_step1()
    stack.step2()
    swap_strip(1)
    swap_strip(-1)
    loads[2].wait()
    tile = 512
    for n in range(width // tile):
        cols = slice(n * tile, (n + 1) * tile)
        r1_ref[:, cols] = x_ref[:, cols].astype(f32) + nn(mixed_ref[...], wo[:, cols])
    h2_ref[...] = (rms_parts(r1_ref[...])[0] * gf_ref[...]).astype(bf16)
    keeps = [keep]

    def write(n, src, dst):
        copy = pltpu.make_async_copy(src, dst, lsem.at[n])
        copy.start()
        keeps.append(copy)

    for gather in cotangents:
        gather.other.step2()
    stack.finish()
    swap_strip(2)
    for swap in strip_swaps:
        swap.wait_recv()
    for k in range(8):
        write(9 + k, wall.at[k // 2, k % 2], w_ref.at[:, pl.ds(k * strip, strip)])
    for gather in cotangents:
        gather.finish()
    write(17, dya, dya_ref)
    for copy in keeps:
        copy.wait()
    copies.finish()


def front(
    starts, x, w_qkv, w_out, g_attn, g_ffn, q_gain, k_gain, cosine, sine, dy, w_in, w_down
):
    count, width = x.shape
    share = w_down.shape[0]
    q_cols = HEADS * HD
    kv_cols = 2 * KV * HD
    vmem_spec = pl.BlockSpec(memory_space=pltpu.VMEM)
    any_spec = pl.BlockSpec(memory_space=pl.ANY)
    return pl.pallas_call(
        front_kernel,
        out_shape=(
            jax.ShapeDtypeStruct((count, width), bf16),
            jax.ShapeDtypeStruct((count, q_cols + kv_cols), f32),
            jax.ShapeDtypeStruct((count, q_cols), bf16),
            jax.ShapeDtypeStruct((8, 4, BLOCK, kv_cols), bf16),
            jax.ShapeDtypeStruct((count, q_cols), bf16),
            jax.ShapeDtypeStruct((count, width), f32),
            jax.ShapeDtypeStruct((count, width), bf16),
            jax.ShapeDtypeStruct((2, 4, 2, BLOCK, width), bf16),
            jax.ShapeDtypeStruct((3 * share, width), bf16),
        ),
        in_specs=[
            pl.BlockSpec(memory_space=pltpu.SMEM),
            vmem_spec,
            any_spec,
            any_spec,
            *[vmem_spec] * 7,
            any_spec,
            any_spec,
        ],
        out_specs=(
            vmem_spec,
            vmem_spec,
            vmem_spec,
            any_spec,
            vmem_spec,
            vmem_spec,
            vmem_spec,
            any_spec,
            any_spec,
        ),
        scratch_shapes=[
            pltpu.VMEM((width, q_cols), bf16),
            pltpu.VMEM((width, kv_cols), bf16),
            pltpu.VMEM((q_cols, width), bf16),
            pltpu.VMEM((2, BLOCK, kv_cols), bf16),
            pltpu.VMEM((8, 4, BLOCK, kv_cols), bf16),
            pltpu.VMEM((2, 4, 2, BLOCK, width), bf16),
            pltpu.VMEM((share, 2, width // 8), bf16),
            pltpu.VMEM((3 * share, width // 8), bf16),
            pltpu.VMEM((4, 2, 3 * share, width // 8), bf16),
            pltpu.VMEM((2 * KV, PER_GROUP * BLOCK, KV_COLS), bf16),
            pltpu.VMEM((2, BLOCK, 16 * BLOCK), f32),
            pltpu.VMEM((2 * KV, PER_GROUP * BLOCK, KV_COLS), f32),
            pltpu.VMEM((2 * KV, PER_GROUP * BLOCK, 2 * BLOCK), f32),
            pltpu.SemaphoreType.DMA((43,)),
            pltpu.SemaphoreType.DMA((43,)),
            pltpu.SemaphoreType.DMA((18,)),
        ],
        compiler_params=pltpu.CompilerParams(
            collective_id=2, has_side_effects=True, vmem_limit_bytes=VMEM_BYTES
        ),
        name="front",
    )(starts, x, w_qkv, w_out, g_attn, g_ffn, q_gain, k_gain, cosine, sine, dy, w_in, w_down)


GAIN_ROWS = 40


def rear_kernel(
    starts_ref,
    dh2_ref,
    r1_ref,
    dy_ref,
    x_ref,
    q_ref,
    raw_ref,
    h1_ref,
    mix_ref,
    kva_ref,
    wqkv_ref,
    wout_ref,
    gsum_ref,
    outp_ref,
    ga_ref,
    gf_ref,
    qg_ref,
    kg_ref,
    cos_ref,
    sin_ref,
    y_ref,
    gx_ref,
    gain_ref,
    gpart_ref,
    h1_out,
    da_out,
    dq_out,
    mx_out,
    wbuf,
    wkv,
    kva,
    gsum,
    gl1,
    gl2,
    gpair,
    gpart,
    outp,
    mask,
    d_r1,
    d_o,
    dq,
    d_h1,
    da,
    h1c,
    dac,
    dqc,
    mxc,
    *scratch,
):
    landings, out_landings = scratch[:4], (scratch[4:7], scratch[7:10])
    send, recv, lsem = scratch[10:]
    count, width = x_ref.shape
    q_cols = HEADS * HD
    k_cols = KV * HD
    seq, head = lax.axis_index("seq"), lax.axis_index("head")
    loads = [
        pltpu.make_async_copy(outp_ref.at[0], outp.at[0], lsem.at[6]),
        pltpu.make_async_copy(outp_ref.at[1], outp.at[1], lsem.at[7]),
        pltpu.make_async_copy(gsum_ref, gsum, lsem.at[3]),
    ]
    loads += [
        pltpu.make_async_copy(wout_ref, wbuf.at[pl.ds(0, q_cols)], lsem.at[0]),
        pltpu.make_async_copy(kva_ref, kva, lsem.at[1]),
        pltpu.make_async_copy(wqkv_ref.at[:, pl.ds(q_cols, 2 * k_cols)], wkv, lsem.at[2]),
    ]
    for load in loads:
        load.start()
    load_wo, load_kva, load_wkv = loads[-3:]
    load_wq = pltpu.make_async_copy(
        wqkv_ref.at[:, pl.ds(0, q_cols)], wbuf.at[:, pl.ds(0, q_cols)], lsem.at[5]
    )
    copies = Copies(send, recv)
    core = lax.axis_index("dp_1")
    mine, theirs = pl.ds(0, count), pl.ds(count, count)

    def piece(z, which):
        return pl.ds(pl.multiple_of(z * 512 + which * 256, 256), 256)

    barrier_with(PLANE + STACK + (("seq", 2),), core=True)
    outs = [
        RingThenPairSum(copies, 24 + 7 * half, outp.at[half], *out_landings[half])
        for half in (0, 1)
    ]
    gring = RingSum(copies, 38, "dp_0", gsum, gl1, gl2)
    for half in (0, 1):
        loads[half].wait()
        outs[half].far()
    loads[2].wait()
    gring.start()
    for total in outs:
        total.early()
    lanes128 = gain_ref.shape[1]
    n_rows = width // lanes128

    def put_gain(first, value):
        for n in range(value.shape[1] // lanes128):
            gain_ref[first + n : first + n + 1] = value[:, n * lanes128 : (n + 1) * lanes128]

    n2, inv2 = rms_parts(r1_ref[...])
    d_h2 = dh2_ref[...]
    gain_ref[...] = jnp.zeros_like(gain_ref)
    put_gain(n_rows, jnp.sum(d_h2 * n2, axis=0, keepdims=True))
    d_r1[...] = dy_ref[...].astype(f32) + rms_back(d_h2 * gf_ref[...], n2, inv2)
    da[...] = d_r1[...].astype(bf16)
    swaps = [copies.start_to_core(58, mix_ref, mxc.at[theirs])]
    for z in range(4):
        cols = pl.ds(z * 256, 256)
        h1c[mine, cols] = h1_ref[:, piece(z, core)]
        dac[mine, cols] = da[:, piece(z, core)]
        swaps.append(
            copies.start_to_core(60 + 2 * z, h1_ref.at[:, piece(z, 1 - core)], h1c.at[theirs, cols])
        )
        swaps.append(
            copies.start_to_core(61 + 2 * z, da.at[:, piece(z, 1 - core)], dac.at[theirs, cols])
        )
    mxc[mine] = mix_ref[...]
    mask_rows(starts_ref, 0, False, mask)
    mask_rows(starts_ref, 1, True, mask)
    load_wo.wait()
    for g in range(KV):
        cols = slice(g * GROUP_COLS, (g + 1) * GROUP_COLS)
        d_o[:, cols] = nt(da[...], wbuf[cols]).astype(bf16)
    load_wq.start()
    load_kva.wait()
    sums = [PlaneSum(copies, 0, half, kva, *landings) for half in (0, 1)]
    for row in (0, 1):
        rows = slice(row * BLOCK, (row + 1) * BLOCK)
        for g in range(KV):
            cols = slice(g * GROUP_COLS, (g + 1) * GROUP_COLS)
            lanes = slice(g * KV_COLS, (g + 1) * KV_COLS)
            q_rows = stacked(q_ref[rows, cols], 0)
            do_rows = stacked(d_o[rows, cols], 1)
            kv_rows = kva[4 * row : 4 * row + 4, :, :, lanes].reshape(16 * BLOCK, KV_COLS)
            e = weights_of(q_rows, kv_rows, mask[row])
            probs = e * (1.0 / jnp.sum(e, axis=1, keepdims=True))
            d_probs = nt(do_rows, kv_rows)
            delta = jnp.sum(probs * d_probs, axis=1, keepdims=True)
            d_scores = (probs * (d_probs - delta)).astype(bf16)
            dq_rows = nn(d_scores, kv_rows)[:, :HD] * SCALE
            dq[rows, cols] = unstacked(dq_rows.astype(bf16))
            dkv = tn(d_scores, q_rows * jnp.asarray(SCALE, bf16)) + tn(probs.astype(bf16), do_rows)
            kva[4 * row : 4 * row + 4, :, :, lanes] = dkv.astype(bf16).reshape(
                4, 4, BLOCK, KV_COLS
            )
        sums[row].far()
        sums[row].early()
        if row == 0:
            gring.late()
    means = head_means()
    cosine, sine = cos_ref[...], sin_ref[...]
    q_gain, k_gain = (jnp.concatenate([ref[...]] * PER_GROUP, 1) for ref in (qg_ref, kg_ref))

    def queries(g):
        cols = slice(g * GROUP_COLS, (g + 1) * GROUP_COLS)
        value, gain = turned_back(
            dq[:, cols].astype(f32), raw_ref[:, cols], q_gain, cosine, sine, means
        )
        dqc[mine, cols] = value.astype(bf16)
        return gain

    gain = queries(0)
    for g in range(1, KV):
        gain += queries(g)
    put_gain(2 * n_rows, gain)
    swaps.append(
        copies.start_to_core(
            68, dqc.at[mine, pl.ds(0, q_cols)], dqc.at[theirs, pl.ds(0, q_cols)]
        )
    )
    for total in sums:
        total.late()
    for total in outs:
        total.late()
    load_wq.wait()
    load_wkv.wait()
    tile = 512
    for n in range(width // tile):
        cols = slice(n * tile, (n + 1) * tile)
        d_h1[:, cols] = nt(dqc[mine, :q_cols], wbuf[cols, :q_cols])
    for total in sums:
        total.inner_start()
    for total in outs:
        total.pair()
    for total in sums:
        total.inner_late()
    own_sums = gring.finish()
    gmove = copies.start(44, own_sums.at[1], gpair, "seq", mate())
    d_kv = jnp.concatenate([total.result().astype(bf16) for total in sums], 0)
    pieces = [d_kv[:, g * KV_COLS : g * KV_COLS + HD] for g in range(KV)]
    pieces += [d_kv[:, g * KV_COLS + HD : (g + 1) * KV_COLS] for g in range(KV)]
    d_kv = jnp.concatenate(pieces, 1)
    first, gain1 = turned_back(
        d_kv[:, :GROUP_COLS].astype(f32),
        raw_ref[:, q_cols : q_cols + GROUP_COLS],
        k_gain,
        cosine,
        sine,
        means,
    )
    second, gain2 = turned_back(
        d_kv[:, GROUP_COLS : 2 * GROUP_COLS].astype(f32),
        raw_ref[:, q_cols + GROUP_COLS : q_cols + 2 * GROUP_COLS],
        k_gain,
        cosine,
        sine,
        means,
    )
    lane = lax.broadcasted_iota(jnp.int32, gain2.shape, 1)
    put_gain(
        2 * n_rows + GROUP_COLS // lanes128,
        gain1 + jnp.where(lane < k_cols - GROUP_COLS, gain2, 0.0),
    )
    dqc[mine, q_cols : q_cols + GROUP_COLS] = first.astype(bf16)
    lane = lax.broadcasted_iota(jnp.int32, second.shape, 1)
    dqc[mine, q_cols + GROUP_COLS : q_cols + 2 * GROUP_COLS] = jnp.where(
        lane < k_cols - GROUP_COLS,
        second.astype(bf16),
        d_kv[:, GROUP_COLS : 2 * GROUP_COLS],
    )
    dqc[mine, q_cols + 2 * GROUP_COLS :] = d_kv[:, 2 * GROUP_COLS :]
    kv_part = pl.ds(q_cols, 2 * k_cols)
    swaps.append(copies.start_to_core(69, dqc.at[mine, kv_part], dqc.at[theirs, kv_part]))
    for n in range(width // tile):
        cols = slice(n * tile, (n + 1) * tile)
        d_h1[:, cols] += nt(dqc[mine, q_cols:], wkv[cols])
    n1, inv1 = rms_parts(x_ref[...].astype(f32))
    put_gain(0, jnp.sum(d_h1[...] * n1, axis=0, keepdims=True))
    gx_ref[...] = (d_r1[...] + rms_back(d_h1[...] * ga_ref[...], n1, inv1)).astype(bf16)
    for half in (0, 1):
        rows = slice(half * BLOCK, (half + 1) * BLOCK)
        y_ref[rows] = (r1_ref[rows] + outs[half].result()).astype(bf16)
    gmove.wait_recv()
    gpart[...] = (own_sums[0].astype(f32) + gpair[...].astype(f32)).astype(bf16)
    gkeep = pltpu.make_async_copy(gpart, gpart_ref, lsem.at[4])
    gkeep.start()
    for swap in swaps:
        swap.wait_recv()
    keeps = [
        pltpu.make_async_copy(h1c, h1_out, lsem.at[0]),
        pltpu.make_async_copy(dac, da_out, lsem.at[1]),
        pltpu.make_async_copy(dqc, dq_out, lsem.at[2]),
        pltpu.make_async_copy(mxc, mx_out, lsem.at[3]),
    ]
    for keep in keeps:
        keep.start()
    for keep in keeps:
        keep.wait()
    gkeep.wait()
    copies.finish()


def rear(
    starts,
    d_h2,
    r1,
    dy,
    x,
    q,
    raw,
    h1,
    mixed,
    kva,
    w_qkv,
    w_out,
    gsum,
    outp,
    g_attn,
    g_ffn,
    q_gain,
    k_gain,
    cosine,
    sine,
):
    count, width = x.shape
    q_cols = HEADS * HD
    kv_cols = 2 * KV * HD
    vmem_spec = pl.BlockSpec(memory_space=pltpu.VMEM)
    any_spec = pl.BlockSpec(memory_space=pl.ANY)
    sums = gsum.shape
    pair_shapes = [
        (2 * count, width // 2),
        (2 * count, width // 2),
        (2 * count, q_cols + kv_cols),
        (2 * count, q_cols),
    ]
    return pl.pallas_call(
        rear_kernel,
        out_shape=(
            jax.ShapeDtypeStruct((count, width), bf16),
            jax.ShapeDtypeStruct((count, width), bf16),
            jax.ShapeDtypeStruct((GAIN_ROWS, 128), f32),
            jax.ShapeDtypeStruct(sums[2:], bf16),
            *[jax.ShapeDtypeStruct(shape, bf16) for shape in pair_shapes],
        ),
        in_specs=[
            pl.BlockSpec(memory_space=pltpu.SMEM),
            *[vmem_spec] * 8,
            *[any_spec] * 5,
            *[vmem_spec] * 6,
        ],
        out_specs=(*[vmem_spec] * 3, *[any_spec] * 5),
        scratch_shapes=[
            pltpu.VMEM((width, width), bf16),
            pltpu.VMEM((width, kv_cols), bf16),
            pltpu.VMEM((8, 4, BLOCK, kv_cols), bf16),
            pltpu.VMEM(sums, bf16),
            pltpu.VMEM((2, 1, *sums[2:]), bf16),
            pltpu.VMEM((2, 2, *sums[2:]), bf16),
            pltpu.VMEM(sums[2:], bf16),
            pltpu.VMEM(sums[2:], bf16),
            pltpu.VMEM((2, 4, 2, BLOCK, width), bf16),
            pltpu.VMEM((2, BLOCK, 16 * BLOCK), f32),
            pltpu.VMEM((count, width), f32),
            pltpu.VMEM((count, q_cols), bf16),
            pltpu.VMEM((count, q_cols), bf16),
            pltpu.VMEM((count, width), f32),
            pltpu.VMEM((count, width), bf16),
            *[pltpu.VMEM(shape, bf16) for shape in pair_shapes],
            *sum_landings(kv_cols),
            *ring_then_pair_landings(width),
            *ring_then_pair_landings(width),
            pltpu.SemaphoreType.DMA((70,)),
            pltpu.SemaphoreType.DMA((70,)),
            pltpu.SemaphoreType.DMA((8,)),
        ],
        compiler_params=pltpu.CompilerParams(
            collective_id=3, has_side_effects=True, vmem_limit_bytes=VMEM_BYTES
        ),
        name="rear",
    )(
        starts,
        d_h2,
        r1,
        dy,
        x,
        q,
        raw,
        h1,
        mixed,
        kva,
        w_qkv,
        w_out,
        gsum,
        outp,
        g_attn,
        g_ffn,
        q_gain,
        k_gain,
        cosine,
        sine,
    )


AXIS_ORDERS = (("head", "dp_0", "seq"), ("seq", "head", "dp_0"), ("dp_0", "seq", "head"))
SLICES = (
    (0, ((True, 0, 896),)),
    (1, ((False, 640, 1024),)),
    (2, ((False, 0, 384),)),
    (0, ((True, 896, 896),)),
    (1, ((False, 1664, 1024),)),
    (2, ((False, 384, 256),)),
)
CHIP_AXES = ("dp_0", "seq", "head")


def projections_kernel(
    h1_ref,
    da_ref,
    dq_ref,
    mix_ref,
    gain_ref,
    gpart_ref,
    left_ref,
    right_ref,
    gain_out,
    gboth_ref,
    *scratch,
):
    count = len(SLICES)
    gsum, gboth = scratch[:2]
    parts, half1, full1, half2, full2, last = (
        scratch[2 + count * k : 2 + count * (k + 1)] for k in range(6)
    )
    send, recv, lsem = scratch[2 + 6 * count :]
    copies = Copies(send, recv)
    barrier = pltpu.get_barrier_semaphore()
    core = lax.axis_index("dp_1")
    for axis in CHIP_AXES:
        for by in (1, 2, 3):
            pl.semaphore_signal(
                barrier,
                inc=1,
                device_id={axis: shift(lax.axis_index(axis), by)},
                device_id_type=MESH,
            )
    pl.semaphore_signal(barrier, inc=1, device_id={"dp_1": 1 - core}, device_id_type=MESH)
    pl.semaphore_wait(barrier, 10)
    gain_move = copies.start_to_core(0, gain_ref, gsum.at[3, core])
    grows = gpart_ref.shape[0]
    place = pl.ds(pl.multiple_of(core * grows, 16), grows)
    stack = RingGather(copies, 100, "dp_0", gboth.at[:, place])
    z = lax.axis_index("dp_0")
    gboth[z, place] = gpart_ref[...]
    stack.step1()
    swaps = []

    def swap_rows(by):
        block = gboth.at[shift(z, by), place]
        swaps.append(copies.start_to_core(104 + by % 4, block, block))

    swap_rows(0)
    base = 10
    orders = [AXIS_ORDERS[order] for order, _ in SLICES]
    rings = [
        RingSum(copies, base + 15 * k, orders[k][0], parts[k], half1[k], full1[k])
        for k in range(count)
    ]

    def make(k):
        order, pieces = SLICES[k]
        part = parts[k]

        @pl.loop(0, 4)
        def _(z):
            cols = pl.ds(pl.multiple_of(z * 256, 256), 256)
            place = 0
            for attention, first, width in pieces:
                lhs, rhs = (da_ref, mix_ref) if attention else (h1_ref, dq_ref)
                value = tn(lhs[:, cols], rhs[:, first : first + width]).astype(bf16)
                value = value.reshape(4, 4, 16, width)
                to = slice(place, place + width)
                if order == 2:
                    part[z, :, :, :, to] = value
                elif order == 1:
                    part[:, :, z, :, to] = value
                else:
                    for y in range(4):
                        part[:, z, y, :, to] = value[y]
                place += width

    def gain_step(k, axis, value):
        i = lax.axis_index(axis)
        gsum[k, i] = value
        out = []
        for n, by in enumerate((1, 2, 3)):
            src = gsum.at[k, i]
            out.append(copies.start(1 + 3 * k + n, src, src, axis, by))
        return out

    def gain_total(k, moves):
        for move in moves:
            move.wait_recv()
        return gsum[k, 0] + gsum[k, 1] + gsum[k, 2] + gsum[k, 3]

    first, second = range(count // 2), range(count // 2, count)
    owns = [None] * count
    rings2 = [None] * count
    ends = [None] * count

    def next_axis(k):
        owns[k] = rings[k].finish()
        rings2[k] = RingSum(
            copies, base + 15 * k + 6, orders[k][1], owns[k], half2[k], full2[k]
        )
        rings2[k].start()

    def last_axis(k):
        owns[k] = rings2[k].finish()
        axis = orders[k][2]
        i = lax.axis_index(axis)
        ends[k] = [
            copies.start(
                base + 15 * k + 12 + n, owns[k].at[shift(i, by)], last[k].at[n], axis, by
            )
            for n, by in enumerate((1, 2, 3))
        ]

    for k in first:
        make(k)
        rings[k].start()
    gain_move.wait_recv()
    gsum[3, core] = gain_ref[...]
    gmoves = gain_step(0, CHIP_AXES[0], gsum[3, 0] + gsum[3, 1])
    for k in second:
        make(k)
    for k in first:
        rings[k].late()
        rings[k + count // 2].start()
    gmoves = gain_step(1, CHIP_AXES[1], gain_total(0, gmoves))
    stack.step2()
    swap_rows(1)
    swap_rows(-1)
    for k in first:
        next_axis(k)
    for k in second:
        rings[k].late()
    gmoves = gain_step(2, CHIP_AXES[2], gain_total(1, gmoves))
    for k in first:
        rings2[k].late()
    for k in first:
        last_axis(k)
    for k in second:
        next_axis(k)
    gain_out[...] = gain_total(2, gmoves)
    stack.finish()
    swap_rows(2)
    for k in second:
        rings2[k].late()
    for k in second:
        last_axis(k)
    for swap in swaps:
        swap.wait_recv()
    keep = pltpu.make_async_copy(gboth, gboth_ref, lsem.at[0])
    keep.start()
    for k in range(count):
        i = lax.axis_index(orders[k][2])
        for end in ends[k]:
            end.wait_recv()
        value = owns[k][i].astype(f32)
        for n in range(3):
            value = value + last[k][n].astype(f32)
        place = 0
        for attention, column, width in SLICES[k][1]:
            ref = right_ref if attention else left_ref
            ref[:, column : column + width] = value[:, place : place + width]
            place += width
    keep.wait()
    copies.finish()


def projections(h1, d_attn, d_qkv, mixed, gains, gpart):
    qkv_width = d_qkv.shape[1]
    widths = [sum(width for _, _, width in pieces) for _, pieces in SLICES]
    both = (4, 2 * gpart.shape[0], gpart.shape[1])
    vmem_spec = pl.BlockSpec(memory_space=pltpu.VMEM)

    def each(make):
        return [pltpu.VMEM(make(width), bf16) for width in widths]

    return pl.pallas_call(
        projections_kernel,
        out_shape=(
            jax.ShapeDtypeStruct((16, qkv_width), f32),
            jax.ShapeDtypeStruct((16, mixed.shape[1]), f32),
            jax.ShapeDtypeStruct(gains.shape, f32),
            jax.ShapeDtypeStruct(both, bf16),
        ),
        in_specs=[vmem_spec] * 6,
        out_specs=(*[vmem_spec] * 3, pl.BlockSpec(memory_space=pl.ANY)),
        scratch_shapes=[
            pltpu.VMEM((4, 4, *gains.shape), f32),
            pltpu.VMEM(both, bf16),
            *each(lambda w: (4, 4, 4, 16, w)),
            *each(lambda w: (2, 2, 4, 16, w)),
            *each(lambda w: (2, 4, 4, 16, w)),
            *each(lambda w: (2, 2, 16, w)),
            *each(lambda w: (2, 4, 16, w)),
            *each(lambda w: (3, 16, w)),
            pltpu.SemaphoreType.DMA((108,)),
            pltpu.SemaphoreType.DMA((108,)),
            pltpu.SemaphoreType.DMA((1,)),
        ],
        compiler_params=pltpu.CompilerParams(
            collective_id=4, has_side_effects=True, vmem_limit_bytes=VMEM_BYTES
        ),
        name="projections",
    )(h1, d_attn, d_qkv, mixed, gains, gpart)


def widen_kernel(
    g_ref, y_ref, gx_ref, left_ref, right_ref, gain_ref,
    gin_out, gdn_out, y_out, gx_out, left_out, right_out, ga_out, gf_out, gq_out, gk_out,
):
    units = gdn_out.shape[0]
    gin_out[:, 0, :] = g_ref[:units].astype(f32)
    gin_out[:, 1, :] = g_ref[units : 2 * units].astype(f32)
    gdn_out[...] = g_ref[2 * units :].astype(f32)
    y_out[...] = y_ref[...]
    gx_out[...] = gx_ref[...]
    left_out[...] = left_ref[...]
    right_out[...] = right_ref[...]
    n = ga_out.shape[0]
    ga_out[...] = gain_ref[:n]
    gf_out[...] = gain_ref[n : 2 * n]
    for ref, first in ((gq_out, 2 * n), (gk_out, 2 * n + 2)):
        both = gain_ref[first : first + 1] + gain_ref[first + 1 : first + 2]
        ref[...] = both[:, :HD] + both[:, HD:]


def widen(g, y, gx, left, right, gains, units):
    tiles, _, tile = g.shape
    count, width = y.shape

    def whole(shape):
        return pl.BlockSpec(shape, lambda n: (0,) * len(shape))

    by_tile = pl.BlockSpec((count, tile), lambda n: (0, n))
    gain_rows = width // 128
    return pl.pallas_call(
        widen_kernel,
        grid=(tiles,),
        out_shape=(
            jax.ShapeDtypeStruct((units, 2, width), f32),
            jax.ShapeDtypeStruct((units, width), f32),
            jax.ShapeDtypeStruct(y.shape, bf16),
            jax.ShapeDtypeStruct(gx.shape, bf16),
            jax.ShapeDtypeStruct(left.shape, f32),
            jax.ShapeDtypeStruct(right.shape, f32),
            jax.ShapeDtypeStruct((gain_rows, 128), f32),
            jax.ShapeDtypeStruct((gain_rows, 128), f32),
            jax.ShapeDtypeStruct((1, HD), f32),
            jax.ShapeDtypeStruct((1, HD), f32),
        ),
        in_specs=[
            pl.BlockSpec((None, 3 * units, tile), lambda n: (n, 0, 0)),
            by_tile,
            by_tile,
            whole(left.shape),
            whole(right.shape),
            whole(gains.shape),
        ],
        out_specs=(
            pl.BlockSpec((units, 2, tile), lambda n: (0, 0, n)),
            pl.BlockSpec((units, tile), lambda n: (0, n)),
            by_tile,
            by_tile,
            whole(left.shape),
            whole(right.shape),
            whole((gain_rows, 128)),
            whole((gain_rows, 128)),
            whole((1, HD)),
            whole((1, HD)),
        ),
        compiler_params=pltpu.CompilerParams(vmem_limit_bytes=VMEM_BYTES),
        name="widen",
    )(g, y, gx, left, right, gains)


def angle_tables(positions, columns):
    lane = jnp.arange(columns)
    freq = jnp.exp((lane % (HD // 2)).astype(f32) * (-2.0 * math.log(10000.0) / HD))
    angle = positions.astype(f32)[:, None] * freq[None, :]
    sign = jnp.where(lane % HD < HD // 2, -1.0, 1.0)
    return (jnp.cos(angle), jnp.sin(angle) * sign[None, :])


def body(
    tokens, w_qkv, w_out, w_ffn_in, w_ffn_out, g_attn, g_ffn, q_gain, k_gain, doc_starts, d_out
):
    rows, tok, width = tokens.shape
    count = rows * tok
    n_seq = lax.axis_size("seq")
    n_head = lax.axis_size("head")
    first = (lax.axis_index("seq") * n_head + lax.axis_index("head")) * tok
    cosine, sine = angle_tables(first + jnp.arange(count) % tok, GROUP_COLS)
    x = tokens.reshape(count, width)
    dy = d_out.reshape(count, width)
    ga = g_attn[None]
    gf = g_ffn[None]
    qg = q_gain[None]
    kg = k_gain[None]
    h1, raw, q, kva, mixed, r1, h2, dy_all, weights = front(
        doc_starts, x, w_qkv, w_out, ga, gf, qg, kg, cosine, sine, d_out, w_ffn_in, w_ffn_out
    )
    outp, d_h2, gsum = ffn(
        h2.reshape(rows, tok, width), dy_all, w_ffn_in, w_ffn_out, weights
    )
    output, grad_x, gains, gpart, *pairs = rear(
        doc_starts,
        d_h2.reshape(count, width),
        r1,
        dy,
        x,
        q,
        raw,
        h1,
        mixed,
        kva,
        w_qkv,
        w_out,
        gsum,
        outp,
        ga,
        gf,
        qg,
        kg,
        cosine,
        sine,
    )
    grad_qkv, grad_out, gains, gboth = projections(*pairs, gains, gpart)
    grad_in, grad_down, output, grad_x, grad_qkv, grad_out, *gains = widen(
        gboth, output, grad_x, grad_qkv, grad_out, gains, w_ffn_out.shape[0]
    )
    return (
        output.reshape(rows, tok, width),
        grad_x.reshape(rows, tok, width),
        grad_qkv,
        grad_out.T,
        grad_in,
        grad_down,
        *[gain.reshape(-1) for gain in gains],
    )


def solution(mesh):
    split = Mesh(
        mesh.devices.reshape(4, 2, mesh.shape["seq"], mesh.shape["head"]),
        ("dp_0", "dp_1", "seq", "head"),
    )
    return jax.shard_map(
        body,
        mesh=split,
        in_specs=(
            P(DP, ("seq", "head"), None),
            P(),
            P(),
            P(("seq", "head"), None, None),
            P(("seq", "head"), None),
            P(),
            P(),
            P(),
            P(),
            P(DP, None),
            P(DP, ("seq", "head"), None),
        ),
        out_specs=(
            P(DP, ("seq", "head"), None),
            P(DP, ("seq", "head"), None),
            P(DP_SEQ_HEAD, None),
            P(None, DP_SEQ_HEAD),
            P(("seq", "head"), None, None),
            P(("seq", "head"), None),
            P(),
            P(),
            P(),
            P(),
        ),
        check_vma=False,
    )
```

```python
import functools
import math

import jax
import jax.numpy as jnp
from jax import lax
from jax.experimental import pallas as pl
from jax.experimental.pallas import tpu as pltpu
from jax.sharding import Mesh
from jax.sharding import PartitionSpec as P

HEADS = 28
KV = 7
HD = 64
PER_GROUP = HEADS // KV
DP_SEQ_HEAD = ("dp_0", "dp_1", "seq", "head")
DP = ("dp_0", "dp_1")
RING = 4
BLOCK = 64
MESH = pl.DeviceIdType.MESH
EPS = 1e-06
SCALE = 0.125
f32 = jnp.float32
bf16 = jnp.bfloat16
VMEM_BYTES = 62 * 2**20


def nt(a, b):
    return lax.dot_general(a, b, (((1,), (1,)), ((), ())), preferred_element_type=f32)


def nn(a, b):
    return lax.dot_general(a, b, (((1,), (0,)), ((), ())), preferred_element_type=f32)


def tn(a, b):
    return lax.dot_general(a, b, (((0,), (0,)), ((), ())), preferred_element_type=f32)


def shift(index, by):
    return lax.rem(index + (by + RING), RING)


def barrier_with(partners, core=False):
    barrier = pltpu.get_barrier_semaphore()
    for axis, by in partners:
        pl.semaphore_signal(
            barrier,
            inc=1,
            device_id={axis: shift(lax.axis_index(axis), by)},
            device_id_type=MESH,
        )
    if core:
        other = 1 - lax.axis_index("dp_1")
        pl.semaphore_signal(barrier, inc=1, device_id={"dp_1": other}, device_id_type=MESH)
    pl.semaphore_wait(barrier, len(partners) + int(core))


PLANE = (("seq", 1), ("seq", -1), ("head", 1), ("head", -1))
PAIRED = (("seq", 2), ("head", 1), ("head", -1))
STACK = (("dp_0", 1), ("dp_0", -1))


class Copies:
    def __init__(self, send, recv):
        self.send = send
        self.recv = recv
        self.started = []

    def start(self, slot, src, dst, axis, by):
        copy = pltpu.make_async_remote_copy(
            src_ref=src,
            dst_ref=dst,
            send_sem=self.send.at[slot],
            recv_sem=self.recv.at[slot],
            device_id={axis: shift(lax.axis_index(axis), by)},
            device_id_type=MESH,
        )
        copy.start()
        self.started.append(copy)
        return copy

    def start_to_core(self, slot, src, dst):
        copy = pltpu.make_async_remote_copy(
            src_ref=src,
            dst_ref=dst,
            send_sem=self.send.at[slot],
            recv_sem=self.recv.at[slot],
            device_id={"dp_1": 1 - lax.axis_index("dp_1")},
            device_id_type=MESH,
        )
        copy.start()
        self.started.append(copy)
        return copy

    def finish(self):
        for copy in self.started:
            copy.wait_send()


INNER = ("head", "seq")
GROUP = ("seq", "head")


class PlaneGather:
    def __init__(self, copies, base, half, own, buf):
        self.c = copies
        self.base = base + 8 * half
        self.half = half
        self.own = own
        self.buf = buf
        self.i = lax.axis_index(INNER[half])
        self.g = lax.axis_index(GROUP[half])

    def row(self, by=0):
        return 4 * self.half + shift(self.g, by)

    def step1(self):
        ax = INNER[self.half]
        dst = self.buf.at[self.row(), self.i]
        self.a = self.c.start(self.base, self.own, dst, ax, 1)
        self.b = self.c.start(self.base + 1, self.own, dst, ax, -1)

    def step2(self):
        ax = INNER[self.half]
        n = self.buf.shape[2] // 2
        self.a.wait_recv()
        left = self.buf.at[self.row(), shift(self.i, -1), pl.ds(0, n)]
        self.a = self.c.start(self.base + 2, left, left, ax, 1)
        self.b.wait_recv()
        right = self.buf.at[self.row(), shift(self.i, 1), pl.ds(n, n)]
        self.b = self.c.start(self.base + 3, right, right, ax, -1)

    def step3(self):
        ax = GROUP[self.half]
        self.a.wait_recv()
        self.b.wait_recv()
        rows = self.buf.at[self.row()]
        self.a = self.c.start(self.base + 4, rows, rows, ax, 1)
        self.b = self.c.start(self.base + 5, rows, rows, ax, -1)

    def step4(self):
        ax = GROUP[self.half]
        self.a.wait_recv()
        left = self.buf.at[self.row(-1), pl.ds(0, 2)]
        self.a = self.c.start(self.base + 6, left, left, ax, 1)
        self.b.wait_recv()
        right = self.buf.at[self.row(1), pl.ds(2, 2)]
        self.b = self.c.start(self.base + 7, right, right, ax, -1)

    def finish(self):
        self.a.wait_recv()
        self.b.wait_recv()


class PlaneSum:
    def __init__(self, copies, base, half, part, land1, land2, land3, land4):
        self.c = copies
        self.base = base + 12 * half
        self.half = half
        self.part = part
        self.l1, self.l2, self.l3, self.l4 = (
            ref.at[half] for ref in (land1, land2, land3, land4)
        )
        self.i = lax.axis_index(INNER[half])
        self.g = lax.axis_index(GROUP[half])

    def row(self, by=0):
        return 4 * self.half + shift(self.g, by)

    def add(self, ref, other):
        ref[...] = (ref[...].astype(f32) + other[...].astype(f32)).astype(ref.dtype)

    def far(self):
        ax = GROUP[self.half]
        row = self.row(2)
        self.a = self.c.start(self.base, self.part.at[row, pl.ds(0, 2)], self.l1.at[0], ax, 1)
        self.b = self.c.start(self.base + 1, self.part.at[row, pl.ds(2, 2)], self.l1.at[1], ax, -1)

    def early(self):
        ax = GROUP[self.half]
        one, two = pl.ds(0, 2), pl.ds(2, 2)
        right, left = self.part.at[self.row(1)], self.part.at[self.row(-1)]
        self.ea = self.c.start(self.base + 2, right.at[two], self.l2.at[0, two], ax, 1)
        self.eb = self.c.start(self.base + 3, left.at[one], self.l2.at[1, one], ax, -1)

    def late(self):
        ax = GROUP[self.half]
        one, two = pl.ds(0, 2), pl.ds(2, 2)
        right, left = self.part.at[self.row(1), one], self.part.at[self.row(-1), two]
        self.a.wait_recv()
        self.add(right, self.l1.at[0])
        self.a = self.c.start(self.base + 4, right, self.l2.at[0, one], ax, 1)
        self.b.wait_recv()
        self.add(left, self.l1.at[1])
        self.b = self.c.start(self.base + 5, left, self.l2.at[1, two], ax, -1)

    def inner_start(self):
        ax = INNER[self.half]
        n = self.part.shape[2] // 2
        one, two = pl.ds(0, n), pl.ds(n, n)
        for copy in (self.ea, self.eb, self.a, self.b):
            copy.wait_recv()
        rows = self.part.at[self.row()]

        def sum_of(k):
            rows[k] = (
                rows[k].astype(f32) + self.l2[0, k].astype(f32) + self.l2[1, k].astype(f32)
            ).astype(rows.dtype)

        sum_of(shift(self.i, 2))
        block = rows.at[shift(self.i, 2)]
        self.a = self.c.start(self.base + 6, block.at[one], self.l3.at[0], ax, 1)
        self.b = self.c.start(self.base + 7, block.at[two], self.l3.at[1], ax, -1)
        sum_of(shift(self.i, 1))
        sum_of(shift(self.i, -1))
        right, left = rows.at[shift(self.i, 1)], rows.at[shift(self.i, -1)]
        self.ea = self.c.start(self.base + 8, right.at[two], self.l4.at[0, two], ax, 1)
        self.eb = self.c.start(self.base + 9, left.at[one], self.l4.at[1, one], ax, -1)
        sum_of(self.i)

    def inner_late(self):
        ax = INNER[self.half]
        n = self.part.shape[2] // 2
        one, two = pl.ds(0, n), pl.ds(n, n)
        right = self.part.at[self.row(), shift(self.i, 1), one]
        left = self.part.at[self.row(), shift(self.i, -1), two]
        self.a.wait_recv()
        self.add(right, self.l3.at[0])
        self.a = self.c.start(self.base + 10, right, self.l4.at[0, one], ax, 1)
        self.b.wait_recv()
        self.add(left, self.l3.at[1])
        self.b = self.c.start(self.base + 11, left, self.l4.at[1, two], ax, -1)

    def result(self):
        for copy in (self.ea, self.eb, self.a, self.b):
            copy.wait_recv()
        own = self.part[self.row(), self.i].astype(f32)
        return own + self.l4[0].astype(f32) + self.l4[1].astype(f32)


def sum_landings(columns):
    return [
        pltpu.VMEM((2, 2, 2, BLOCK, columns), bf16),
        pltpu.VMEM((2, 2, 4, BLOCK, columns), bf16),
        pltpu.VMEM((2, 2, BLOCK // 2, columns), bf16),
        pltpu.VMEM((2, 2, BLOCK, columns), bf16),
    ]


class RingSum:
    def __init__(self, copies, base, axis, part, half_land, full_land):
        self.c = copies
        self.base = base
        self.axis = axis
        self.part = part
        self.hl = half_land
        self.fl = full_land
        self.i = lax.axis_index(axis)
        n = part.shape[1] // 2
        self.one, self.two = pl.ds(0, n), pl.ds(n, n)

    def start(self):
        self.far()
        self.early()

    def far(self):
        far = self.part.at[shift(self.i, 2)]
        self.a = self.c.start(self.base, far.at[self.one], self.hl.at[0], self.axis, 1)
        self.b = self.c.start(self.base + 1, far.at[self.two], self.hl.at[1], self.axis, -1)

    def early(self):
        right, left = self.part.at[shift(self.i, 1)], self.part.at[shift(self.i, -1)]
        one, two, ax = self.one, self.two, self.axis
        self.ea = self.c.start(self.base + 2, right.at[two], self.fl.at[0, two], ax, 1)
        self.eb = self.c.start(self.base + 3, left.at[one], self.fl.at[1, one], ax, -1)

    def late(self):
        right = self.part.at[shift(self.i, 1), self.one]
        left = self.part.at[shift(self.i, -1), self.two]
        self.a.wait_recv()
        right[...] = (right[...].astype(f32) + self.hl[0].astype(f32)).astype(bf16)
        self.a = self.c.start(self.base + 4, right, self.fl.at[0, self.one], self.axis, 1)
        self.b.wait_recv()
        left[...] = (left[...].astype(f32) + self.hl[1].astype(f32)).astype(bf16)
        self.b = self.c.start(self.base + 5, left, self.fl.at[1, self.two], self.axis, -1)

    def finish(self):
        for copy in (self.ea, self.eb, self.a, self.b):
            copy.wait_recv()
        own = self.part.at[self.i]
        own[...] = (
            own[...].astype(f32) + self.fl[0].astype(f32) + self.fl[1].astype(f32)
        ).astype(bf16)
        return own


class RingGather:
    def __init__(self, copies, base, axis, full):
        self.c = copies
        self.base = base
        self.axis = axis
        self.full = full
        self.i = lax.axis_index(axis)

    def step1(self):
        own = self.full.at[self.i]
        self.a = self.c.start(self.base, own, own, self.axis, 1)
        self.b = self.c.start(self.base + 1, own, own, self.axis, -1)

    def step2(self):
        n = self.full.shape[1] // 2
        self.a.wait_recv()
        left = self.full.at[shift(self.i, -1), pl.ds(0, n)]
        self.a = self.c.start(self.base + 2, left, left, self.axis, 1)
        self.b.wait_recv()
        right = self.full.at[shift(self.i, 1), pl.ds(n, n)]
        self.b = self.c.start(self.base + 3, right, right, self.axis, -1)

    def finish(self):
        self.a.wait_recv()
        self.b.wait_recv()


class RingThenPair:
    def __init__(self, copies, base, buf):
        self.c = copies
        self.base = base
        self.buf = buf
        self.i = lax.axis_index("head")

    def pair(self, slot, index):
        return self.c.start(
            self.base + slot, self.buf.at[index, 0], self.buf.at[index, 1], "seq", 2
        )

    def start(self):
        own = self.buf.at[self.i, 0]
        self.a = self.c.start(self.base, own, own, "head", 1)
        self.b = self.c.start(self.base + 1, own, own, "head", -1)
        self.pairs = [self.pair(2, self.i)]

    def forward(self):
        n = self.buf.shape[2] // 2
        left, right = shift(self.i, -1), shift(self.i, 1)
        self.a.wait_recv()
        block = self.buf.at[left, 0, pl.ds(0, n)]
        self.a = self.c.start(self.base + 3, block, block, "head", 1)
        self.b.wait_recv()
        block = self.buf.at[right, 0, pl.ds(n, n)]
        self.b = self.c.start(self.base + 4, block, block, "head", -1)
        self.pairs += [self.pair(5, left), self.pair(6, right)]

    def last(self):
        self.a.wait_recv()
        self.b.wait_recv()
        self.pairs.append(self.pair(7, shift(self.i, 2)))

    def finish(self):
        for copy in self.pairs:
            copy.wait_recv()


class PairThenRing:
    def __init__(self, copies, base, buf):
        self.c = copies
        self.base = base
        self.buf = buf
        self.gather = RingGather(copies, base + 1, "head", buf)

    def start(self):
        i = self.gather.i
        self.pair = self.c.start(
            self.base, self.buf.at[i, 0], self.buf.at[i, 1], "seq", 2
        )

    def ring(self):
        self.pair.wait_recv()
        self.gather.step1()

    def forward(self):
        self.gather.step2()

    def finish(self):
        self.gather.finish()


class PairThenRingSum:
    def __init__(self, copies, base, part, pair_land, half_land, full_land):
        self.c = copies
        self.base = base
        self.part = part
        self.pl = pair_land
        self.ring = RingSum(copies, base + 4, "head", part.at[:, 0], half_land, full_land)
        self.i = self.ring.i

    def start(self):
        self.pairs = []
        for n, by in enumerate((2, 1, 3, 0)):
            j = shift(self.i, by)
            self.pairs.append(
                self.c.start(self.base + n, self.part.at[j, 1], self.pl.at[j], "seq", 2)
            )

    def added(self, n, by):
        self.pairs[n].wait_recv()
        j = shift(self.i, by)
        self.part[j, 0] = (self.part[j, 0].astype(f32) + self.pl[j].astype(f32)).astype(bf16)

    def along(self):
        self.added(0, 2)
        self.ring.far()
        self.added(1, 1)
        self.added(2, 3)
        self.ring.early()
        self.added(3, 0)

    def late(self):
        self.ring.late()

    def result(self):
        return self.ring.finish()[...].astype(f32)


class TwoRings:
    def __init__(self, copies, base, buf):
        self.c = copies
        self.base = base
        self.buf = buf
        self.own = RingGather(copies, base + 1, "head", buf.at[:, 0])
        self.other = RingGather(copies, base + 5, "head", buf.at[:, 1])

    def pair(self):
        i = self.own.i
        self.p = self.c.start(self.base, self.buf.at[i, 0], self.buf.at[i, 1], "seq", 2)

    def other_step1(self):
        self.p.wait_recv()
        self.other.step1()

    def finish(self):
        self.own.finish()
        self.other.finish()


class RingThenPairSum:
    def __init__(self, copies, base, part, pair_land, half_land, full_land):
        self.c = copies
        self.base = base
        self.pl = pair_land
        self.ring = RingSum(copies, base + 1, "head", part, half_land, full_land)
        self.far, self.early, self.late = self.ring.far, self.ring.early, self.ring.late

    def pair(self):
        self.own = self.ring.finish()
        self.p = self.c.start(self.base, self.own.at[1], self.pl, "seq", 2)

    def result(self):
        self.p.wait_recv()
        return self.own[0].astype(f32) + self.pl[...].astype(f32)


def ring_then_pair_landings(columns):
    return [
        pltpu.VMEM((BLOCK, columns), bf16),
        pltpu.VMEM((2, 1, BLOCK, columns), bf16),
        pltpu.VMEM((2, 2, BLOCK, columns), bf16),
    ]


def pair_then_ring_landings(columns):
    return [
        pltpu.VMEM((4, BLOCK, columns), bf16),
        pltpu.VMEM((2, BLOCK // 2, columns), bf16),
        pltpu.VMEM((2, BLOCK, columns), bf16),
    ]


def mate():
    return 1 - 2 * lax.rem(lax.axis_index("seq"), 2)


UNIT = 4 * BLOCK


def ffn_kernel(
    h2_ref,
    dy_ref,
    win_ref,
    wdn_ref,
    w_ref,
    outp_ref,
    dh2_ref,
    gsum_ref,
    h2a,
    dya,
    pairs,
    win,
    wdn,
    hid,
    dbo,
    dpt,
    *scratch,
):
    land_a, land_b = scratch[:3], scratch[3:6]
    stage, gst, gland, send, recv, lsem, osem = scratch[6:]
    share = gst.shape[2] // 3
    units, width = wdn.shape
    copies = Copies(send, recv)
    i = lax.axis_index("head")
    part = pairs.shape[0]
    load_pairs = [
        pltpu.make_async_copy(win_ref.at[pl.ds(n * part, part)], pairs, lsem.at[n])
        for n in (0, 1)
    ]
    loads = [
        pltpu.make_async_copy(dy_ref, dya, lsem.at[2]),
        pltpu.make_async_copy(wdn_ref, wdn.at[pl.ds(0, share)], lsem.at[3]),
        pltpu.make_async_copy(
            w_ref.at[pl.ds(2 * share, share)], wdn.at[pl.ds(share, share)], lsem.at[4]
        ),
        pltpu.make_async_copy(w_ref.at[pl.ds(0, share)], win.at[pl.ds(share, share)], lsem.at[5]),
        pltpu.make_async_copy(
            w_ref.at[pl.ds(share, share)], win.at[pl.ds(units + share, share)], lsem.at[6]
        ),
    ]
    for load in (load_pairs[0], *loads):
        load.start()

    def split_pairs(n):
        first = n * part
        win[first : first + part] = pairs[:, 0, :]
        win[units + first : units + first + part] = pairs[:, 1, :]

    barrier_with(PAIRED, core=True)
    for half in (0, 1):
        h2a[half, i, 0] = h2_ref[half]
    gather_a = RingThenPair(copies, 0, h2a.at[0])
    gather_b = PairThenRing(copies, 8, h2a.at[1])
    gather_b.start()
    gather_a.start()

    def places(u):
        if u < 2:
            return None
        return (shift(i, 1), shift(i, -1)) if u == 2 else (i, shift(i, 2))

    def tokens_of(ref, u, cols=slice(None)):
        if u < 2:
            value = ref[0, :, u, :, cols]
            return value.reshape(UNIT, value.shape[-1])
        values = [ref[1, j, :, :, cols] for j in places(u)]
        return jnp.concatenate([v.reshape(UNIT // 2, v.shape[-1]) for v in values], 0)

    def columns_of(u):
        return slice(u * UNIT, (u + 1) * UNIT)

    def hidden_back(u):
        dbo[:units, columns_of(u)] = nt(wdn[...], tokens_of(dya, u)).astype(bf16)

    def forward(u):
        cols = columns_of(u)
        t = tokens_of(h2a, u)
        for s in (0, 1):
            one = slice(s * share, (s + 1) * share)
            two = slice(units + s * share, units + (s + 1) * share)
            gate = nt(win[one], t)
            up = nt(win[two], t)
            sig = 1.0 / (1.0 + jnp.exp(-gate))
            act = gate * sig
            d_hidden = dbo[one, cols].astype(f32)
            hid[one, cols] = (act * up).astype(bf16)
            dbo[one, cols] = (d_hidden * up * (sig * (1.0 + gate * (1.0 - sig)))).astype(bf16)
            dbo[two, cols] = (d_hidden * act).astype(bf16)

    def back(u):
        value = tn(dbo[:, columns_of(u)], win[...]).astype(bf16)
        if u < 2:
            dpt[0, :, u] = value.reshape(4, BLOCK, width)
        else:
            for n, j in enumerate(places(u)):
                dpt[1, j] = value[n * UNIT // 2 : (n + 1) * UNIT // 2].reshape(2, BLOCK, width)

    load_pairs[0].wait()
    split_pairs(0)
    load_pairs[1].start()
    gather_b.ring()
    gather_a.forward()
    load_pairs[1].wait()
    split_pairs(1)
    gather_a.last()
    for load in loads:
        load.wait()
    hidden_back(0)
    forward(0)
    gather_b.forward()
    for u in (2, 1, 3):
        hidden_back(u)
    sum_a = PairThenRingSum(copies, 16, dpt.at[0], *land_a)
    sum_b = RingThenPairSum(copies, 26, dpt.at[1], *land_b)
    forward(2)
    back(2)
    sum_b.early()
    gather_a.finish()
    forward(1)
    back(1)
    sum_a.start()
    gather_b.finish()
    forward(3)
    back(3)
    sum_b.far()
    back(0)

    tiles, half_rows, tile = gland.shape[0], gland.shape[2], gland.shape[3]
    core = lax.axis_index("dp_1")
    mine = pl.ds(pl.multiple_of(core * half_rows, 16), half_rows)
    theirs = pl.ds(pl.multiple_of((1 - core) * half_rows, 16), half_rows)
    swaps = []

    def gradients(n):
        cols = slice(n * tile, (n + 1) * tile)
        value = nn(
            dbo[...], jnp.concatenate([tokens_of(h2a, u, cols) for u in range(4)], 0)
        ).astype(bf16)
        down = nn(
            hid[...], jnp.concatenate([tokens_of(dya, u, cols) for u in range(4)], 0)
        ).astype(bf16)
        for s in (0, 1):
            gst[n, s, :share] = value[s * share : (s + 1) * share]
            gst[n, s, share : 2 * share] = value[units + s * share : units + (s + 1) * share]
            gst[n, s, 2 * share :] = down[s * share : (s + 1) * share]
        swaps.append(copies.start_to_core(34 + n, gst.at[n, :, theirs], gland.at[n]))

    def out_copies(u):
        slot = stage.at[u % 2]
        if u < 2:
            return [pltpu.make_async_copy(slot, outp_ref.at[0, :, u], osem.at[u % 2, 0])]
        return [
            pltpu.make_async_copy(
                slot.at[pl.ds(2 * n, 2)], outp_ref.at[1, j], osem.at[u % 2, n]
            )
            for n, j in enumerate(places(u))
        ]

    def out_part(u):
        if u >= 2:
            for copy in out_copies(u - 2):
                copy.wait()
        value = tn(hid[:, columns_of(u)], wdn[...])
        stage[u % 2] = value.astype(bf16).reshape(4, BLOCK, width)
        for copy in out_copies(u):
            copy.start()

    gradients(0)
    gradients(1)
    sum_b.late()
    gradients(2)
    gradients(3)
    sum_b.pair()
    out_part(0)
    sum_a.along()
    out_part(1)
    sum_a.late()
    out_part(2)
    dh2_ref[1] = sum_b.result()
    out_part(3)
    for n, swap in enumerate(swaps):
        swap.wait_recv()
        gland[n] = (gst[n, :, mine].astype(f32) + gland[n].astype(f32)).astype(bf16)
    keep = pltpu.make_async_copy(gland, gsum_ref, lsem.at[0])
    keep.start()
    dh2_ref[0] = sum_a.result()
    for u in (2, 3):
        for copy in out_copies(u):
            copy.wait()
    keep.wait()
    copies.finish()


def ffn(h2, dy_all, w_in, w_down, weights):
    share, width = w_down.shape
    tokens = 4 * UNIT
    tile = 512
    any_spec = pl.BlockSpec(memory_space=pl.ANY)
    vmem_spec = pl.BlockSpec(memory_space=pltpu.VMEM)
    buffer = (2, 4, 2, BLOCK, width)
    sums = (width // tile, 2, 3 * share // 2, tile)
    return pl.pallas_call(
        ffn_kernel,
        out_shape=(
            jax.ShapeDtypeStruct(buffer, bf16),
            jax.ShapeDtypeStruct((2, BLOCK, width), f32),
            jax.ShapeDtypeStruct(sums, bf16),
        ),
        in_specs=[vmem_spec, *[any_spec] * 4],
        out_specs=(any_spec, vmem_spec, any_spec),
        scratch_shapes=[
            pltpu.VMEM(buffer, bf16),
            pltpu.VMEM(buffer, bf16),
            pltpu.VMEM((share // 2, 2, width), bf16),
            pltpu.VMEM((4 * share, width), bf16),
            pltpu.VMEM((2 * share, width), bf16),
            pltpu.VMEM((2 * share, tokens), bf16),
            pltpu.VMEM((4 * share, tokens), bf16),
            pltpu.VMEM(buffer, bf16),
            *pair_then_ring_landings(width),
            *ring_then_pair_landings(width),
            pltpu.VMEM((2, 4, BLOCK, width), bf16),
            pltpu.VMEM((width // tile, 2, 3 * share, tile), bf16),
            pltpu.VMEM(sums, bf16),
            pltpu.SemaphoreType.DMA((38,)),
            pltpu.SemaphoreType.DMA((38,)),
            pltpu.SemaphoreType.DMA((7,)),
            pltpu.SemaphoreType.DMA((2, 2)),
        ],
        compiler_params=pltpu.CompilerParams(
            collective_id=1, has_side_effects=True, vmem_limit_bytes=VMEM_BYTES
        ),
        name="ffn",
    )(h2, dy_all, w_in, w_down, weights)


def mask_rows(starts_ref, row, transposed, mask_ref):
    seq, head = lax.axis_index("seq"), lax.axis_index("head")
    keys = 16 * BLOCK
    index = lax.broadcasted_iota(jnp.int32, (1, keys), 1)
    if transposed:
        group = lax.div(index, 4 * BLOCK)
        inner = lax.rem(lax.div(index, BLOCK), 4)
        k_pos = (inner * 4 + group) * BLOCK + lax.rem(index, BLOCK)
    else:
        k_pos = index
    first = (seq * 4 + head) * BLOCK
    q_pos = first + lax.broadcasted_iota(jnp.int32, (BLOCK, 1), 0)
    k_doc = jnp.zeros((1, keys), jnp.int32)
    q_doc = jnp.zeros((BLOCK, 1), jnp.int32)
    for d in range(starts_ref.shape[1]):
        start = starts_ref[row, d]
        k_doc += (start <= k_pos).astype(jnp.int32)
        q_doc += (start <= q_pos).astype(jnp.int32)
    seen = (k_pos <= q_pos) & (k_doc == q_doc)
    mask_ref[row] = seen.astype(f32)


LOG2E_SCALE = SCALE * math.log2(math.e)


def stacked(block, where):
    rows = jnp.concatenate([block[:, h * HD : (h + 1) * HD] for h in range(PER_GROUP)], 0)
    zero = jnp.zeros_like(rows)
    return jnp.concatenate([rows, zero] if where == 0 else [zero, rows], 1)


def unstacked(rows):
    return jnp.concatenate([rows[h * BLOCK : (h + 1) * BLOCK] for h in range(PER_GROUP)], 1)


def weights_of(q_rows, kv_rows, mask):
    scores = nt(q_rows, kv_rows)
    keys = kv_rows.shape[0]
    e = jnp.exp2(scores * LOG2E_SCALE).reshape(PER_GROUP, BLOCK, keys) * mask[None]
    return e.reshape(PER_GROUP * BLOCK, keys)


GROUP_COLS = PER_GROUP * HD
KV_COLS = 2 * HD


def head_means(columns=GROUP_COLS):
    a = lax.div(lax.broadcasted_iota(jnp.int32, (columns, columns), 0), HD)
    b = lax.div(lax.broadcasted_iota(jnp.int32, (columns, columns), 1), HD)
    return jnp.where(a == b, 1.0 / HD, 0.0).astype(f32)


def head_mean(v, means):
    return jnp.dot(v, means, precision=lax.Precision.HIGHEST, preferred_element_type=f32)


def swapped(v):
    columns = v.shape[1]
    lane = lax.rem(lax.broadcasted_iota(jnp.int32, v.shape, 1), HD)
    up = pltpu.roll(v, columns - HD // 2, 1)
    down = pltpu.roll(v, HD // 2, 1)
    return jnp.where(lane < HD // 2, up, down)


def turned(raw, gain, cosine, sine, means):
    normed = raw * lax.rsqrt(head_mean(raw * raw, means) + EPS)
    v = normed * gain
    return v * cosine + swapped(v) * sine


def turned_back(grad, raw, gain, cosine, sine, means):
    inverse = lax.rsqrt(head_mean(raw * raw, means) + EPS)
    normed = raw * inverse
    u = grad * cosine - swapped(grad) * sine
    gain_grad = jnp.sum(u * normed, axis=0, keepdims=True)
    e = u * gain
    return inverse * (e - normed * head_mean(e * normed, means)), gain_grad


def rms_parts(v):
    inverse = lax.rsqrt(jnp.mean(v * v, axis=-1, keepdims=True) + EPS)
    return (v * inverse, inverse)


def rms_back(grad, normed, inverse):
    return inverse * (grad - normed * jnp.mean(grad * normed, axis=-1, keepdims=True))


def front_kernel(
    starts_ref,
    x_ref,
    wqkv_ref,
    wout_ref,
    ga_ref,
    gf_ref,
    qg_ref,
    kg_ref,
    cos_ref,
    sin_ref,
    dy_ref,
    win_ref,
    wdn_ref,
    h1_ref,
    raw_ref,
    q_ref,
    kva_ref,
    mixed_ref,
    r1_ref,
    h2_ref,
    dya_ref,
    w_ref,
    wq,
    wkv,
    wo,
    own,
    kva,
    dya,
    pown,
    wsend,
    wall,
    qst,
    mask,
    oacc,
    lacc,
    send,
    recv,
    lsem,
):
    count, width = x_ref.shape
    q_cols = HEADS * HD
    k_cols = KV * HD
    loads = [
        pltpu.make_async_copy(wqkv_ref.at[:, pl.ds(q_cols, 2 * k_cols)], wkv, lsem.at[0]),
        pltpu.make_async_copy(wqkv_ref.at[:, pl.ds(0, q_cols)], wq, lsem.at[1]),
        pltpu.make_async_copy(wout_ref, wo, lsem.at[2]),
    ]
    share = wdn_ref.shape[0]
    z, core = lax.axis_index("dp_0"), lax.axis_index("dp_1")
    strip = wsend.shape[1]
    strip_cols = pl.ds(pl.multiple_of((z * 2 + core) * strip, strip), strip)
    strips = [
        pltpu.make_async_copy(win_ref.at[:, :, strip_cols], pown, lsem.at[5]),
        pltpu.make_async_copy(
            wdn_ref.at[:, strip_cols], wsend.at[pl.ds(2 * share, share)], lsem.at[6]
        ),
    ]
    for load in strips + loads:
        load.start()
    copies = Copies(send, recv)
    barrier_with(PLANE + STACK + (("seq", 2),), core=True)
    head = lax.axis_index("head")
    for half in (0, 1):
        dya[half, head, 0] = dy_ref[half]
    cotangents = [TwoRings(copies, 16 + 9 * half, dya.at[half]) for half in (0, 1)]
    cotangents[0].own.step1()
    for load in strips:
        load.wait()
    wsend[:share] = pown[:, 0, :]
    wsend[share : 2 * share] = pown[:, 1, :]
    strip_move = copies.start(34, wsend, wall.at[z, core], "seq", mate())
    stack = RingGather(copies, 35, "dp_0", wall.at[:, core])
    strip_swaps = []

    def swap_strip(by):
        block = wall.at[shift(z, by), core]
        strip_swaps.append(copies.start_to_core(39 + by % 4, block, block))

    means = head_means()
    cosine, sine = cos_ref[...], sin_ref[...]
    q_gain, k_gain = (jnp.concatenate([ref[...]] * PER_GROUP, 1) for ref in (qg_ref, kg_ref))
    x = x_ref[...].astype(f32)
    h1_ref[...] = (rms_parts(x)[0] * ga_ref[...]).astype(bf16)
    loads[0].wait()
    kv = nn(h1_ref[...], wkv[...])
    raw_ref[:, q_cols:] = kv
    keys = jnp.concatenate(
        [
            turned(kv[:, c : c + GROUP_COLS], k_gain, cosine, sine, means)
            for c in (0, GROUP_COLS)
        ],
        1,
    )
    for g in range(KV):
        k = keys[:, g * HD : (g + 1) * HD]
        v = kv[:, k_cols + g * HD : k_cols + (g + 1) * HD]
        own[:, :, g * KV_COLS : (g + 1) * KV_COLS] = (
            jnp.concatenate([k, v], 1).astype(bf16).reshape(2, BLOCK, KV_COLS)
        )
    gathers = [PlaneGather(copies, 0, half, own.at[half], kva) for half in (0, 1)]
    for gather in gathers:
        gather.step1()
    for half in (0, 1):
        kva[gathers[half].row(), gathers[half].i] = own[half]
    loads[1].wait()

    def queries(g):
        cols = slice(g * GROUP_COLS, (g + 1) * GROUP_COLS)
        raw = nn(h1_ref[...], wq[:, cols])
        raw_ref[:, cols] = raw
        q = turned(raw, q_gain, cosine, sine, means).astype(bf16)
        q_ref[:, cols] = q
        for row in (0, 1):
            qst[row * KV + g] = stacked(q[row * BLOCK : (row + 1) * BLOCK], 0)

    for g in range(3):
        queries(g)
    for gather in gathers:
        gather.step2()
    for g in range(3, KV):
        queries(g)
    for gather in gathers:
        gather.step3()
    mask_rows(starts_ref, 0, False, mask)
    mask_rows(starts_ref, 1, True, mask)
    seq = lax.axis_index("seq")

    def scored(row, by, first):
        group = lax.rem(seq + row * (head - seq) + by + 4, 4)
        seen = mask[row, :, pl.ds(pl.multiple_of(group * 4 * BLOCK, 4 * BLOCK), 4 * BLOCK)]
        for g in range(KV):
            index = row * KV + g
            kv_rows = kva[
                4 * row + group, :, :, g * KV_COLS : (g + 1) * KV_COLS
            ].reshape(4 * BLOCK, KV_COLS)
            e = weights_of(qst[index], kv_rows, seen)
            total = e[:, : 2 * BLOCK] + e[:, 2 * BLOCK :]
            mixed = nn(e.astype(bf16), kv_rows)
            if first:
                lacc[index] = total
                oacc[index] = mixed
            else:
                lacc[index] += total
                oacc[index] += mixed

    @pl.loop(0, 2)
    def _(row):
        scored(row, 0, True)

    strip_move.wait_recv()
    stack.step1()
    swap_strip(0)
    for gather in gathers:
        gather.step4()
    for gather in cotangents:
        gather.pair()
    cotangents[0].own.step2()
    cotangents[1].own.step1()

    @pl.loop(0, 4)
    def _(k):
        scored(lax.div(k, 2), 1 - 2 * lax.rem(k, 2), False)

    for gather in gathers:
        gather.finish()
    keep = pltpu.make_async_copy(kva, kva_ref, lsem.at[3])
    keep.start()

    @pl.loop(0, 2)
    def _(row):
        scored(row, 2, False)

    for row in (0, 1):
        for g in range(KV):
            index = row * KV + g
            mixed = oacc[index][:, HD:] / jnp.sum(lacc[index], axis=1, keepdims=True)
            mixed_ref[
                row * BLOCK : (row + 1) * BLOCK, g * GROUP_COLS : (g + 1) * GROUP_COLS
            ] = unstacked(mixed.astype(bf16))
    cotangents[1].own.step2()
    for gather in cotangents:
        gather.other_step1()
    stack.step2()
    swap_strip(1)
    swap_strip(-1)
    loads[2].wait()
    tile = 512
    for n in range(width // tile):
        cols = slice(n * tile, (n + 1) * tile)
        r1_ref[:, cols] = x_ref[:, cols].astype(f32) + nn(mixed_ref[...], wo[:, cols])
    h2_ref[...] = (rms_parts(r1_ref[...])[0] * gf_ref[...]).astype(bf16)
    keeps = [keep]

    def write(n, src, dst):
        copy = pltpu.make_async_copy(src, dst, lsem.at[n])
        copy.start()
        keeps.append(copy)

    for gather in cotangents:
        gather.other.step2()
    stack.finish()
    swap_strip(2)
    for swap in strip_swaps:
        swap.wait_recv()
    for k in range(8):
        write(9 + k, wall.at[k // 2, k % 2], w_ref.at[:, pl.ds(k * strip, strip)])
    for gather in cotangents:
        gather.finish()
    write(17, dya, dya_ref)
    for copy in keeps:
        copy.wait()
    copies.finish()


def front(
    starts, x, w_qkv, w_out, g_attn, g_ffn, q_gain, k_gain, cosine, sine, dy, w_in, w_down
):
    count, width = x.shape
    share = w_down.shape[0]
    q_cols = HEADS * HD
    kv_cols = 2 * KV * HD
    vmem_spec = pl.BlockSpec(memory_space=pltpu.VMEM)
    any_spec = pl.BlockSpec(memory_space=pl.ANY)
    return pl.pallas_call(
        front_kernel,
        out_shape=(
            jax.ShapeDtypeStruct((count, width), bf16),
            jax.ShapeDtypeStruct((count, q_cols + kv_cols), f32),
            jax.ShapeDtypeStruct((count, q_cols), bf16),
            jax.ShapeDtypeStruct((8, 4, BLOCK, kv_cols), bf16),
            jax.ShapeDtypeStruct((count, q_cols), bf16),
            jax.ShapeDtypeStruct((count, width), f32),
            jax.ShapeDtypeStruct((count, width), bf16),
            jax.ShapeDtypeStruct((2, 4, 2, BLOCK, width), bf16),
            jax.ShapeDtypeStruct((3 * share, width), bf16),
        ),
        in_specs=[
            pl.BlockSpec(memory_space=pltpu.SMEM),
            vmem_spec,
            any_spec,
            any_spec,
            *[vmem_spec] * 7,
            any_spec,
            any_spec,
        ],
        out_specs=(
            vmem_spec,
            vmem_spec,
            vmem_spec,
            any_spec,
            vmem_spec,
            vmem_spec,
            vmem_spec,
            any_spec,
            any_spec,
        ),
        scratch_shapes=[
            pltpu.VMEM((width, q_cols), bf16),
            pltpu.VMEM((width, kv_cols), bf16),
            pltpu.VMEM((q_cols, width), bf16),
            pltpu.VMEM((2, BLOCK, kv_cols), bf16),
            pltpu.VMEM((8, 4, BLOCK, kv_cols), bf16),
            pltpu.VMEM((2, 4, 2, BLOCK, width), bf16),
            pltpu.VMEM((share, 2, width // 8), bf16),
            pltpu.VMEM((3 * share, width // 8), bf16),
            pltpu.VMEM((4, 2, 3 * share, width // 8), bf16),
            pltpu.VMEM((2 * KV, PER_GROUP * BLOCK, KV_COLS), bf16),
            pltpu.VMEM((2, BLOCK, 16 * BLOCK), f32),
            pltpu.VMEM((2 * KV, PER_GROUP * BLOCK, KV_COLS), f32),
            pltpu.VMEM((2 * KV, PER_GROUP * BLOCK, 2 * BLOCK), f32),
            pltpu.SemaphoreType.DMA((43,)),
            pltpu.SemaphoreType.DMA((43,)),
            pltpu.SemaphoreType.DMA((18,)),
        ],
        compiler_params=pltpu.CompilerParams(
            collective_id=2, has_side_effects=True, vmem_limit_bytes=VMEM_BYTES
        ),
        name="front",
    )(starts, x, w_qkv, w_out, g_attn, g_ffn, q_gain, k_gain, cosine, sine, dy, w_in, w_down)


AXIS_ORDERS = (("head", "dp_0", "seq"), ("seq", "head", "dp_0"))
OUT_SLICES = ((0, 0, 896), (1, 896, 896))
QKV_SLICES = ((0, 0, 768), (1, 1280, 896), (0, 768, 512), (1, 2176, 512))
CHIP_AXES = ("dp_0", "seq", "head")


class Slices:
    sems = 15

    def __init__(self, copies, base, slices, lhs, rhs, scratch):
        self.c = copies
        self.base = base
        self.slices = slices
        self.lhs = lhs
        self.rhs = rhs
        n = len(slices)
        self.parts, half1, full1, self.half2, self.full2, self.last = (
            scratch[n * k : n * (k + 1)] for k in range(6)
        )
        self.orders = [AXIS_ORDERS[order] for order, _, _ in slices]
        self.rings = [
            RingSum(copies, base + 15 * k, self.orders[k][0], self.parts[k], half1[k], full1[k])
            for k in range(n)
        ]
        self.rings2 = [None] * n
        self.owns = [None] * n
        self.ends = [None] * n

    @staticmethod
    def scratch(slices):
        def each(make):
            return [pltpu.VMEM(make(width), bf16) for _, _, width in slices]

        return [
            *each(lambda w: (4, 4, 4, 16, w)),
            *each(lambda w: (2, 2, 4, 16, w)),
            *each(lambda w: (2, 4, 4, 16, w)),
            *each(lambda w: (2, 2, 16, w)),
            *each(lambda w: (2, 4, 16, w)),
            *each(lambda w: (3, 16, w)),
        ]

    def make(self, k):
        order, first, width = self.slices[k]
        part = self.parts[k]

        @pl.loop(0, 4)
        def _(z):
            cols = pl.ds(pl.multiple_of(z * 256, 256), 256)
            value = tn(self.lhs[:, cols], self.rhs[:, first : first + width]).astype(bf16)
            value = value.reshape(4, 4, 16, width)
            if order == 1:
                part[:, :, z] = value
            else:
                for y in range(4):
                    part[:, z, y] = value[y]

    def begin(self):
        for k in range(len(self.slices)):
            self.make(k)
            self.rings[k].start()

    def late(self, k):
        self.rings[k].late()

    def next_axis(self, k):
        own = self.rings[k].finish()
        self.rings2[k] = RingSum(
            self.c, self.base + 15 * k + 6, self.orders[k][1], own, self.half2[k], self.full2[k]
        )
        self.rings2[k].start()

    def late2(self, k):
        self.rings2[k].late()

    def last_axis(self, k):
        self.owns[k] = self.rings2[k].finish()
        axis = self.orders[k][2]
        i = lax.axis_index(axis)
        self.ends[k] = [
            self.c.start(
                self.base + 15 * k + 12 + n, self.owns[k].at[shift(i, by)], self.last[k].at[n], axis, by
            )
            for n, by in enumerate((1, 2, 3))
        ]

    def store(self, k, ref):
        i = lax.axis_index(self.orders[k][2])
        for end in self.ends[k]:
            end.wait_recv()
        value = self.owns[k][i].astype(f32)
        for n in range(3):
            value = value + self.last[k][n].astype(f32)
        _, first, width = self.slices[k]
        ref[:, first : first + width] = value


GAIN_ROWS = 40


def rear_kernel(
    starts_ref,
    dh2_ref,
    r1_ref,
    dy_ref,
    x_ref,
    q_ref,
    raw_ref,
    h1_ref,
    mix_ref,
    kva_ref,
    wqkv_ref,
    wout_ref,
    gsum_ref,
    outp_ref,
    ga_ref,
    gf_ref,
    qg_ref,
    kg_ref,
    cos_ref,
    sin_ref,
    y_ref,
    gx_ref,
    gain_ref,
    gpart_ref,
    h1_out,
    dq_out,
    right_ref,
    wbuf,
    wkv,
    kva,
    gsum,
    gl1,
    gl2,
    gpair,
    gpart,
    outp,
    mask,
    d_r1,
    d_o,
    dq,
    d_h1,
    da,
    h1c,
    dac,
    dqc,
    mxc,
    *scratch,
):
    landings, out_landings = scratch[:4], (scratch[4:7], scratch[7:10])
    send, recv, lsem = scratch[-3:]
    count, width = x_ref.shape
    q_cols = HEADS * HD
    k_cols = KV * HD
    seq, head = lax.axis_index("seq"), lax.axis_index("head")
    loads = [
        pltpu.make_async_copy(outp_ref.at[0], outp.at[0], lsem.at[6]),
        pltpu.make_async_copy(outp_ref.at[1], outp.at[1], lsem.at[7]),
        pltpu.make_async_copy(gsum_ref, gsum, lsem.at[3]),
    ]
    loads += [
        pltpu.make_async_copy(wout_ref, wbuf.at[pl.ds(0, q_cols)], lsem.at[0]),
        pltpu.make_async_copy(kva_ref, kva, lsem.at[1]),
        pltpu.make_async_copy(wqkv_ref.at[:, pl.ds(q_cols, 2 * k_cols)], wkv, lsem.at[2]),
    ]
    for load in loads:
        load.start()
    load_wo, load_kva, load_wkv = loads[-3:]
    load_wq = pltpu.make_async_copy(
        wqkv_ref.at[:, pl.ds(0, q_cols)], wbuf.at[:, pl.ds(0, q_cols)], lsem.at[5]
    )
    copies = Copies(send, recv)
    core = lax.axis_index("dp_1")
    mine, theirs = pl.ds(0, count), pl.ds(count, count)

    def piece(z, which):
        return pl.ds(pl.multiple_of(z * 512 + which * 256, 256), 256)

    barrier_with(PLANE + STACK + (("seq", 2), ("dp_0", 2), ("head", 2)), core=True)
    out_slices = Slices(copies, 70, OUT_SLICES, dac, mxc, scratch[10:-3])
    outs = [
        RingThenPairSum(copies, 24 + 7 * half, outp.at[half], *out_landings[half])
        for half in (0, 1)
    ]
    gring = RingSum(copies, 38, "dp_0", gsum, gl1, gl2)
    for half in (0, 1):
        loads[half].wait()
        outs[half].far()
    loads[2].wait()
    gring.start()
    for total in outs:
        total.early()
    lanes128 = gain_ref.shape[1]
    n_rows = width // lanes128

    def put_gain(first, value):
        for n in range(value.shape[1] // lanes128):
            gain_ref[first + n : first + n + 1] = value[:, n * lanes128 : (n + 1) * lanes128]

    n2, inv2 = rms_parts(r1_ref[...])
    d_h2 = dh2_ref[...]
    gain_ref[...] = jnp.zeros_like(gain_ref)
    put_gain(n_rows, jnp.sum(d_h2 * n2, axis=0, keepdims=True))
    d_r1[...] = dy_ref[...].astype(f32) + rms_back(d_h2 * gf_ref[...], n2, inv2)
    da[...] = d_r1[...].astype(bf16)
    swaps = [copies.start_to_core(58, mix_ref, mxc.at[theirs])]
    for z in range(4):
        cols = pl.ds(z * 256, 256)
        h1c[mine, cols] = h1_ref[:, piece(z, core)]
        dac[mine, cols] = da[:, piece(z, core)]
        swaps.append(
            copies.start_to_core(60 + 2 * z, h1_ref.at[:, piece(z, 1 - core)], h1c.at[theirs, cols])
        )
        swaps.append(
            copies.start_to_core(61 + 2 * z, da.at[:, piece(z, 1 - core)], dac.at[theirs, cols])
        )
    mxc[mine] = mix_ref[...]
    mask_rows(starts_ref, 0, False, mask)
    mask_rows(starts_ref, 1, True, mask)
    load_wo.wait()
    for g in range(KV):
        cols = slice(g * GROUP_COLS, (g + 1) * GROUP_COLS)
        d_o[:, cols] = nt(da[...], wbuf[cols]).astype(bf16)
    load_wq.start()
    for swap in swaps:
        swap.wait_recv()
    swaps = []
    load_kva.wait()
    sums = [PlaneSum(copies, 0, half, kva, *landings) for half in (0, 1)]
    for row in (0, 1):
        rows = slice(row * BLOCK, (row + 1) * BLOCK)
        for g in range(KV):
            if row == 1 and g == 2:
                gring.late()
            cols = slice(g * GROUP_COLS, (g + 1) * GROUP_COLS)
            lanes = slice(g * KV_COLS, (g + 1) * KV_COLS)
            q_rows = stacked(q_ref[rows, cols], 0)
            do_rows = stacked(d_o[rows, cols], 1)
            kv_rows = kva[4 * row : 4 * row + 4, :, :, lanes].reshape(16 * BLOCK, KV_COLS)
            e = weights_of(q_rows, kv_rows, mask[row])
            probs = e * (1.0 / jnp.sum(e, axis=1, keepdims=True))
            d_probs = nt(do_rows, kv_rows)
            delta = jnp.sum(probs * d_probs, axis=1, keepdims=True)
            d_scores = (probs * (d_probs - delta)).astype(bf16)
            dq_rows = nn(d_scores, kv_rows)[:, :HD] * SCALE
            dq[rows, cols] = unstacked(dq_rows.astype(bf16))
            dkv = tn(d_scores, q_rows * jnp.asarray(SCALE, bf16)) + tn(probs.astype(bf16), do_rows)
            kva[4 * row : 4 * row + 4, :, :, lanes] = dkv.astype(bf16).reshape(
                4, 4, BLOCK, KV_COLS
            )
        sums[row].far()
        sums[row].early()
        if row == 0:
            out_slices.begin()
    means = head_means()
    cosine, sine = cos_ref[...], sin_ref[...]
    q_gain, k_gain = (jnp.concatenate([ref[...]] * PER_GROUP, 1) for ref in (qg_ref, kg_ref))

    def queries(g):
        cols = slice(g * GROUP_COLS, (g + 1) * GROUP_COLS)
        value, gain = turned_back(
            dq[:, cols].astype(f32), raw_ref[:, cols], q_gain, cosine, sine, means
        )
        dqc[mine, cols] = value.astype(bf16)
        return gain

    gain = queries(0)
    for g in range(1, KV):
        gain += queries(g)
    put_gain(2 * n_rows, gain)
    swaps.append(
        copies.start_to_core(
            68, dqc.at[mine, pl.ds(0, q_cols)], dqc.at[theirs, pl.ds(0, q_cols)]
        )
    )
    for total in sums:
        total.late()
    for total in outs:
        total.late()
    for k in (0, 1):
        out_slices.late(k)
    load_wq.wait()
    load_wkv.wait()
    tile = 512
    for n in range(width // tile):
        cols = slice(n * tile, (n + 1) * tile)
        d_h1[:, cols] = nt(dqc[mine, :q_cols], wbuf[cols, :q_cols])
    for total in sums:
        total.inner_start()
    for total in outs:
        total.pair()
    for total in sums:
        total.inner_late()
    for k in (0, 1):
        out_slices.next_axis(k)
    own_sums = gring.finish()
    gmove = copies.start(44, own_sums.at[1], gpair, "seq", mate())
    d_kv = jnp.concatenate([total.result().astype(bf16) for total in sums], 0)
    pieces = [d_kv[:, g * KV_COLS : g * KV_COLS + HD] for g in range(KV)]
    pieces += [d_kv[:, g * KV_COLS + HD : (g + 1) * KV_COLS] for g in range(KV)]
    d_kv = jnp.concatenate(pieces, 1)
    first, gain1 = turned_back(
        d_kv[:, :GROUP_COLS].astype(f32),
        raw_ref[:, q_cols : q_cols + GROUP_COLS],
        k_gain,
        cosine,
        sine,
        means,
    )
    second, gain2 = turned_back(
        d_kv[:, GROUP_COLS : 2 * GROUP_COLS].astype(f32),
        raw_ref[:, q_cols + GROUP_COLS : q_cols + 2 * GROUP_COLS],
        k_gain,
        cosine,
        sine,
        means,
    )
    lane = lax.broadcasted_iota(jnp.int32, gain2.shape, 1)
    put_gain(
        2 * n_rows + GROUP_COLS // lanes128,
        gain1 + jnp.where(lane < k_cols - GROUP_COLS, gain2, 0.0),
    )
    dqc[mine, q_cols : q_cols + GROUP_COLS] = first.astype(bf16)
    lane = lax.broadcasted_iota(jnp.int32, second.shape, 1)
    dqc[mine, q_cols + GROUP_COLS : q_cols + 2 * GROUP_COLS] = jnp.where(
        lane < k_cols - GROUP_COLS,
        second.astype(bf16),
        d_kv[:, GROUP_COLS : 2 * GROUP_COLS],
    )
    dqc[mine, q_cols + 2 * GROUP_COLS :] = d_kv[:, 2 * GROUP_COLS :]
    kv_part = pl.ds(q_cols, 2 * k_cols)
    swaps.append(copies.start_to_core(69, dqc.at[mine, kv_part], dqc.at[theirs, kv_part]))
    for n in range(width // tile):
        cols = slice(n * tile, (n + 1) * tile)
        d_h1[:, cols] += nt(dqc[mine, q_cols:], wkv[cols])
    for k in (0, 1):
        out_slices.late2(k)
    n1, inv1 = rms_parts(x_ref[...].astype(f32))
    put_gain(0, jnp.sum(d_h1[...] * n1, axis=0, keepdims=True))
    gx_ref[...] = (d_r1[...] + rms_back(d_h1[...] * ga_ref[...], n1, inv1)).astype(bf16)
    for k in (0, 1):
        out_slices.last_axis(k)
    for half in (0, 1):
        rows = slice(half * BLOCK, (half + 1) * BLOCK)
        y_ref[rows] = (r1_ref[rows] + outs[half].result()).astype(bf16)
    gmove.wait_recv()
    gpart[...] = (own_sums[0].astype(f32) + gpair[...].astype(f32)).astype(bf16)
    gkeep = pltpu.make_async_copy(gpart, gpart_ref, lsem.at[4])
    gkeep.start()
    for swap in swaps:
        swap.wait_recv()
    keeps = [
        pltpu.make_async_copy(h1c, h1_out, lsem.at[0]),
        pltpu.make_async_copy(dqc, dq_out, lsem.at[2]),
    ]
    for keep in keeps:
        keep.start()
    for k in (0, 1):
        out_slices.store(k, right_ref)
    for keep in keeps:
        keep.wait()
    gkeep.wait()
    copies.finish()


def rear(
    starts,
    d_h2,
    r1,
    dy,
    x,
    q,
    raw,
    h1,
    mixed,
    kva,
    w_qkv,
    w_out,
    gsum,
    outp,
    g_attn,
    g_ffn,
    q_gain,
    k_gain,
    cosine,
    sine,
):
    count, width = x.shape
    q_cols = HEADS * HD
    kv_cols = 2 * KV * HD
    vmem_spec = pl.BlockSpec(memory_space=pltpu.VMEM)
    any_spec = pl.BlockSpec(memory_space=pl.ANY)
    sums = gsum.shape
    pair_shapes = [
        (2 * count, width // 2),
        (2 * count, width // 2),
        (2 * count, q_cols + kv_cols),
        (2 * count, q_cols),
    ]
    return pl.pallas_call(
        rear_kernel,
        out_shape=(
            jax.ShapeDtypeStruct((count, width), bf16),
            jax.ShapeDtypeStruct((count, width), bf16),
            jax.ShapeDtypeStruct((GAIN_ROWS, 128), f32),
            jax.ShapeDtypeStruct(sums[2:], bf16),
            jax.ShapeDtypeStruct(pair_shapes[0], bf16),
            jax.ShapeDtypeStruct(pair_shapes[2], bf16),
            jax.ShapeDtypeStruct((16, q_cols), f32),
        ),
        in_specs=[
            pl.BlockSpec(memory_space=pltpu.SMEM),
            *[vmem_spec] * 8,
            *[any_spec] * 5,
            *[vmem_spec] * 6,
        ],
        out_specs=(*[vmem_spec] * 3, *[any_spec] * 3, vmem_spec),
        scratch_shapes=[
            pltpu.VMEM((width, width), bf16),
            pltpu.VMEM((width, kv_cols), bf16),
            pltpu.VMEM((8, 4, BLOCK, kv_cols), bf16),
            pltpu.VMEM(sums, bf16),
            pltpu.VMEM((2, 1, *sums[2:]), bf16),
            pltpu.VMEM((2, 2, *sums[2:]), bf16),
            pltpu.VMEM(sums[2:], bf16),
            pltpu.VMEM(sums[2:], bf16),
            pltpu.VMEM((2, 4, 2, BLOCK, width), bf16),
            pltpu.VMEM((2, BLOCK, 16 * BLOCK), f32),
            pltpu.VMEM((count, width), f32),
            pltpu.VMEM((count, q_cols), bf16),
            pltpu.VMEM((count, q_cols), bf16),
            pltpu.VMEM((count, width), f32),
            pltpu.VMEM((count, width), bf16),
            *[pltpu.VMEM(shape, bf16) for shape in pair_shapes],
            *sum_landings(kv_cols),
            *ring_then_pair_landings(width),
            *ring_then_pair_landings(width),
            *Slices.scratch(OUT_SLICES),
            pltpu.SemaphoreType.DMA((100,)),
            pltpu.SemaphoreType.DMA((100,)),
            pltpu.SemaphoreType.DMA((8,)),
        ],
        compiler_params=pltpu.CompilerParams(
            collective_id=3, has_side_effects=True, vmem_limit_bytes=VMEM_BYTES
        ),
        name="rear",
    )(
        starts,
        d_h2,
        r1,
        dy,
        x,
        q,
        raw,
        h1,
        mixed,
        kva,
        w_qkv,
        w_out,
        gsum,
        outp,
        g_attn,
        g_ffn,
        q_gain,
        k_gain,
        cosine,
        sine,
    )


def projections_kernel(
    h1_ref, dq_ref, gain_ref, gpart_ref, left_ref, gain_out, gboth_ref, gsum, gboth, *scratch
):
    send, recv, lsem = scratch[-3:]
    copies = Copies(send, recv)
    barrier_with(tuple((axis, by) for axis in CHIP_AXES for by in (1, 2, 3)), core=True)
    core = lax.axis_index("dp_1")
    gain_move = copies.start_to_core(0, gain_ref, gsum.at[3, core])
    grows = gpart_ref.shape[0]
    place = pl.ds(pl.multiple_of(core * grows, 16), grows)
    stack = RingGather(copies, 10, "dp_0", gboth.at[:, place])
    z = lax.axis_index("dp_0")
    gboth[z, place] = gpart_ref[...]
    stack.step1()
    swaps = []

    def swap_rows(by):
        block = gboth.at[shift(z, by), place]
        swaps.append(copies.start_to_core(14 + by % 4, block, block))

    swap_rows(0)
    work = Slices(copies, 18, QKV_SLICES, h1_ref, dq_ref, scratch[:-3])
    first, second = (0, 1), (2, 3)

    def gain_step(k, axis, value):
        i = lax.axis_index(axis)
        gsum[k, i] = value
        out = []
        for n, by in enumerate((1, 2, 3)):
            src = gsum.at[k, i]
            out.append(copies.start(1 + 3 * k + n, src, src, axis, by))
        return out

    def gain_total(k, moves):
        for move in moves:
            move.wait_recv()
        return gsum[k, 0] + gsum[k, 1] + gsum[k, 2] + gsum[k, 3]

    for k in first:
        work.make(k)
        work.rings[k].start()
    gain_move.wait_recv()
    gsum[3, core] = gain_ref[...]
    gmoves = gain_step(0, CHIP_AXES[0], gsum[3, 0] + gsum[3, 1])
    for k in second:
        work.make(k)
    for k in first:
        work.late(k)
        work.rings[k + 2].start()
    gmoves = gain_step(1, CHIP_AXES[1], gain_total(0, gmoves))
    stack.step2()
    swap_rows(1)
    swap_rows(-1)
    for k in first:
        work.next_axis(k)
    for k in second:
        work.late(k)
    gmoves = gain_step(2, CHIP_AXES[2], gain_total(1, gmoves))
    for k in first:
        work.late2(k)
    for k in first:
        work.last_axis(k)
    for k in second:
        work.next_axis(k)
    gain_out[...] = gain_total(2, gmoves)
    stack.finish()
    swap_rows(2)
    for k in second:
        work.late2(k)
    for k in second:
        work.last_axis(k)
    for swap in swaps:
        swap.wait_recv()
    keep = pltpu.make_async_copy(gboth, gboth_ref, lsem.at[0])
    keep.start()
    for k in range(len(QKV_SLICES)):
        work.store(k, left_ref)
    keep.wait()
    copies.finish()


def projections(h1, d_qkv, gains, gpart):
    vmem_spec = pl.BlockSpec(memory_space=pltpu.VMEM)
    both = (4, 2 * gpart.shape[0], gpart.shape[1])
    return pl.pallas_call(
        projections_kernel,
        out_shape=(
            jax.ShapeDtypeStruct((16, d_qkv.shape[1]), f32),
            jax.ShapeDtypeStruct(gains.shape, f32),
            jax.ShapeDtypeStruct(both, bf16),
        ),
        in_specs=[vmem_spec] * 4,
        out_specs=(vmem_spec, vmem_spec, pl.BlockSpec(memory_space=pl.ANY)),
        scratch_shapes=[
            pltpu.VMEM((4, 4, *gains.shape), f32),
            pltpu.VMEM(both, bf16),
            *Slices.scratch(QKV_SLICES),
            pltpu.SemaphoreType.DMA((78,)),
            pltpu.SemaphoreType.DMA((78,)),
            pltpu.SemaphoreType.DMA((1,)),
        ],
        compiler_params=pltpu.CompilerParams(
            collective_id=4, has_side_effects=True, vmem_limit_bytes=VMEM_BYTES
        ),
        name="projections",
    )(h1, d_qkv, gains, gpart)


def widen_kernel(
    g_ref, y_ref, gx_ref, left_ref, right_ref, gain_ref,
    gin_out, gdn_out, y_out, gx_out, left_out, right_out, ga_out, gf_out, gq_out, gk_out,
):
    units = gdn_out.shape[0]
    gin_out[:, 0, :] = g_ref[:units].astype(f32)
    gin_out[:, 1, :] = g_ref[units : 2 * units].astype(f32)
    gdn_out[...] = g_ref[2 * units :].astype(f32)
    y_out[...] = y_ref[...]
    gx_out[...] = gx_ref[...]
    left_out[...] = left_ref[...]
    right_out[...] = right_ref[...]
    n = ga_out.shape[0]
    ga_out[...] = gain_ref[:n]
    gf_out[...] = gain_ref[n : 2 * n]
    for ref, first in ((gq_out, 2 * n), (gk_out, 2 * n + 2)):
        both = gain_ref[first : first + 1] + gain_ref[first + 1 : first + 2]
        ref[...] = both[:, :HD] + both[:, HD:]


def widen(g, y, gx, left, right, gains, units):
    tiles, _, tile = g.shape
    count, width = y.shape

    def whole(shape):
        return pl.BlockSpec(shape, lambda n: (0,) * len(shape))

    by_tile = pl.BlockSpec((count, tile), lambda n: (0, n))
    gain_rows = width // 128
    return pl.pallas_call(
        widen_kernel,
        grid=(tiles,),
        out_shape=(
            jax.ShapeDtypeStruct((units, 2, width), f32),
            jax.ShapeDtypeStruct((units, width), f32),
            jax.ShapeDtypeStruct(y.shape, bf16),
            jax.ShapeDtypeStruct(gx.shape, bf16),
            jax.ShapeDtypeStruct(left.shape, f32),
            jax.ShapeDtypeStruct(right.shape, f32),
            jax.ShapeDtypeStruct((gain_rows, 128), f32),
            jax.ShapeDtypeStruct((gain_rows, 128), f32),
            jax.ShapeDtypeStruct((1, HD), f32),
            jax.ShapeDtypeStruct((1, HD), f32),
        ),
        in_specs=[
            pl.BlockSpec((None, 3 * units, tile), lambda n: (n, 0, 0)),
            by_tile,
            by_tile,
            whole(left.shape),
            whole(right.shape),
            whole(gains.shape),
        ],
        out_specs=(
            pl.BlockSpec((units, 2, tile), lambda n: (0, 0, n)),
            pl.BlockSpec((units, tile), lambda n: (0, n)),
            by_tile,
            by_tile,
            whole(left.shape),
            whole(right.shape),
            whole((gain_rows, 128)),
            whole((gain_rows, 128)),
            whole((1, HD)),
            whole((1, HD)),
        ),
        compiler_params=pltpu.CompilerParams(vmem_limit_bytes=VMEM_BYTES),
        name="widen",
    )(g, y, gx, left, right, gains)


def angle_tables(positions, columns):
    lane = jnp.arange(columns)
    freq = jnp.exp((lane % (HD // 2)).astype(f32) * (-2.0 * math.log(10000.0) / HD))
    angle = positions.astype(f32)[:, None] * freq[None, :]
    sign = jnp.where(lane % HD < HD // 2, -1.0, 1.0)
    return (jnp.cos(angle), jnp.sin(angle) * sign[None, :])


def body(
    tokens, w_qkv, w_out, w_ffn_in, w_ffn_out, g_attn, g_ffn, q_gain, k_gain, doc_starts, d_out
):
    rows, tok, width = tokens.shape
    count = rows * tok
    n_seq = lax.axis_size("seq")
    n_head = lax.axis_size("head")
    first = (lax.axis_index("seq") * n_head + lax.axis_index("head")) * tok
    cosine, sine = angle_tables(first + jnp.arange(count) % tok, GROUP_COLS)
    x = tokens.reshape(count, width)
    dy = d_out.reshape(count, width)
    ga = g_attn[None]
    gf = g_ffn[None]
    qg = q_gain[None]
    kg = k_gain[None]
    h1, raw, q, kva, mixed, r1, h2, dy_all, weights = front(
        doc_starts, x, w_qkv, w_out, ga, gf, qg, kg, cosine, sine, d_out, w_ffn_in, w_ffn_out
    )
    outp, d_h2, gsum = ffn(
        h2.reshape(rows, tok, width), dy_all, w_ffn_in, w_ffn_out, weights
    )
    output, grad_x, gains, gpart, h1_pair, d_qkv, grad_out = rear(
        doc_starts,
        d_h2.reshape(count, width),
        r1,
        dy,
        x,
        q,
        raw,
        h1,
        mixed,
        kva,
        w_qkv,
        w_out,
        gsum,
        outp,
        ga,
        gf,
        qg,
        kg,
        cosine,
        sine,
    )
    grad_qkv, gains, gboth = projections(h1_pair, d_qkv, gains, gpart)
    grad_in, grad_down, output, grad_x, grad_qkv, grad_out, *gains = widen(
        gboth, output, grad_x, grad_qkv, grad_out, gains, w_ffn_out.shape[0]
    )
    return (
        output.reshape(rows, tok, width),
        grad_x.reshape(rows, tok, width),
        grad_qkv,
        grad_out.T,
        grad_in,
        grad_down,
        *[gain.reshape(-1) for gain in gains],
    )


def solution(mesh):
    split = Mesh(
        mesh.devices.reshape(4, 2, mesh.shape["seq"], mesh.shape["head"]),
        ("dp_0", "dp_1", "seq", "head"),
    )
    return jax.shard_map(
        body,
        mesh=split,
        in_specs=(
            P(DP, ("seq", "head"), None),
            P(),
            P(),
            P(("seq", "head"), None, None),
            P(("seq", "head"), None),
            P(),
            P(),
            P(),
            P(),
            P(DP, None),
            P(DP, ("seq", "head"), None),
        ),
        out_specs=(
            P(DP, ("seq", "head"), None),
            P(DP, ("seq", "head"), None),
            P(DP_SEQ_HEAD, None),
            P(None, DP_SEQ_HEAD),
            P(("seq", "head"), None, None),
            P(("seq", "head"), None),
            P(),
            P(),
            P(),
            P(),
        ),
        check_vma=False,
    )
```

```python
import functools
import math

import jax
import jax.numpy as jnp
from jax import lax
from jax.experimental import pallas as pl
from jax.experimental.pallas import tpu as pltpu
from jax.sharding import Mesh
from jax.sharding import PartitionSpec as P

HEADS = 28
KV = 7
HD = 64
PER_GROUP = HEADS // KV
DP_SEQ_HEAD = ("dp_0", "dp_1", "seq", "head")
DP = ("dp_0", "dp_1")
RING = 4
BLOCK = 64
MESH = pl.DeviceIdType.MESH
EPS = 1e-06
SCALE = 0.125
f32 = jnp.float32
bf16 = jnp.bfloat16
VMEM_BYTES = 62 * 2**20


def nt(a, b):
    return lax.dot_general(a, b, (((1,), (1,)), ((), ())), preferred_element_type=f32)


def nn(a, b):
    return lax.dot_general(a, b, (((1,), (0,)), ((), ())), preferred_element_type=f32)


def tn(a, b):
    return lax.dot_general(a, b, (((0,), (0,)), ((), ())), preferred_element_type=f32)


def shift(index, by):
    return lax.rem(index + (by + RING), RING)


def barrier_with(partners, core=False):
    barrier = pltpu.get_barrier_semaphore()
    for axis, by in partners:
        pl.semaphore_signal(
            barrier,
            inc=1,
            device_id={axis: shift(lax.axis_index(axis), by)},
            device_id_type=MESH,
        )
    if core:
        other = 1 - lax.axis_index("dp_1")
        pl.semaphore_signal(barrier, inc=1, device_id={"dp_1": other}, device_id_type=MESH)
    pl.semaphore_wait(barrier, len(partners) + int(core))


PLANE = (("seq", 1), ("seq", -1), ("head", 1), ("head", -1))
PAIRED = (("seq", 2), ("head", 1), ("head", -1))
STACK = (("dp_0", 1), ("dp_0", -1))


class Copies:
    def __init__(self, send, recv):
        self.send = send
        self.recv = recv
        self.started = []

    def start(self, slot, src, dst, axis, by):
        copy = pltpu.make_async_remote_copy(
            src_ref=src,
            dst_ref=dst,
            send_sem=self.send.at[slot],
            recv_sem=self.recv.at[slot],
            device_id={axis: shift(lax.axis_index(axis), by)},
            device_id_type=MESH,
        )
        copy.start()
        self.started.append(copy)
        return copy

    def start_to_core(self, slot, src, dst):
        copy = pltpu.make_async_remote_copy(
            src_ref=src,
            dst_ref=dst,
            send_sem=self.send.at[slot],
            recv_sem=self.recv.at[slot],
            device_id={"dp_1": 1 - lax.axis_index("dp_1")},
            device_id_type=MESH,
        )
        copy.start()
        self.started.append(copy)
        return copy

    def finish(self):
        for copy in self.started:
            copy.wait_send()


INNER = ("head", "seq")
GROUP = ("seq", "head")


class PlaneGather:
    def __init__(self, copies, base, half, own, buf):
        self.c = copies
        self.base = base + 8 * half
        self.half = half
        self.own = own
        self.buf = buf
        self.i = lax.axis_index(INNER[half])
        self.g = lax.axis_index(GROUP[half])

    def row(self, by=0):
        return 4 * self.half + shift(self.g, by)

    def step1(self):
        ax = INNER[self.half]
        dst = self.buf.at[self.row(), self.i]
        self.a = self.c.start(self.base, self.own, dst, ax, 1)
        self.b = self.c.start(self.base + 1, self.own, dst, ax, -1)

    def step2(self):
        ax = INNER[self.half]
        n = self.buf.shape[2] // 2
        self.a.wait_recv()
        left = self.buf.at[self.row(), shift(self.i, -1), pl.ds(0, n)]
        self.a = self.c.start(self.base + 2, left, left, ax, 1)
        self.b.wait_recv()
        right = self.buf.at[self.row(), shift(self.i, 1), pl.ds(n, n)]
        self.b = self.c.start(self.base + 3, right, right, ax, -1)

    def step3(self):
        ax = GROUP[self.half]
        self.a.wait_recv()
        self.b.wait_recv()
        rows = self.buf.at[self.row()]
        self.a = self.c.start(self.base + 4, rows, rows, ax, 1)
        self.b = self.c.start(self.base + 5, rows, rows, ax, -1)

    def step4(self):
        ax = GROUP[self.half]
        self.a.wait_recv()
        left = self.buf.at[self.row(-1), pl.ds(0, 2)]
        self.a = self.c.start(self.base + 6, left, left, ax, 1)
        self.b.wait_recv()
        right = self.buf.at[self.row(1), pl.ds(2, 2)]
        self.b = self.c.start(self.base + 7, right, right, ax, -1)

    def finish(self):
        self.a.wait_recv()
        self.b.wait_recv()


class PlaneSum:
    def __init__(self, copies, base, half, part, land1, land2, land3, land4):
        self.c = copies
        self.base = base + 12 * half
        self.half = half
        self.part = part
        self.l1, self.l2, self.l3, self.l4 = (
            ref.at[half] for ref in (land1, land2, land3, land4)
        )
        self.i = lax.axis_index(INNER[half])
        self.g = lax.axis_index(GROUP[half])

    def row(self, by=0):
        return 4 * self.half + shift(self.g, by)

    def add(self, ref, other):
        ref[...] = (ref[...].astype(f32) + other[...].astype(f32)).astype(ref.dtype)

    def far(self):
        ax = GROUP[self.half]
        row = self.row(2)
        self.a = self.c.start(self.base, self.part.at[row, pl.ds(0, 2)], self.l1.at[0], ax, 1)
        self.b = self.c.start(self.base + 1, self.part.at[row, pl.ds(2, 2)], self.l1.at[1], ax, -1)

    def early(self):
        ax = GROUP[self.half]
        one, two = pl.ds(0, 2), pl.ds(2, 2)
        right, left = self.part.at[self.row(1)], self.part.at[self.row(-1)]
        self.ea = self.c.start(self.base + 2, right.at[two], self.l2.at[0, two], ax, 1)
        self.eb = self.c.start(self.base + 3, left.at[one], self.l2.at[1, one], ax, -1)

    def late(self):
        ax = GROUP[self.half]
        one, two = pl.ds(0, 2), pl.ds(2, 2)
        right, left = self.part.at[self.row(1), one], self.part.at[self.row(-1), two]
        self.a.wait_recv()
        self.add(right, self.l1.at[0])
        self.a = self.c.start(self.base + 4, right, self.l2.at[0, one], ax, 1)
        self.b.wait_recv()
        self.add(left, self.l1.at[1])
        self.b = self.c.start(self.base + 5, left, self.l2.at[1, two], ax, -1)

    def inner_start(self):
        ax = INNER[self.half]
        n = self.part.shape[2] // 2
        one, two = pl.ds(0, n), pl.ds(n, n)
        for copy in (self.ea, self.eb, self.a, self.b):
            copy.wait_recv()
        rows = self.part.at[self.row()]

        def sum_of(k):
            rows[k] = (
                rows[k].astype(f32) + self.l2[0, k].astype(f32) + self.l2[1, k].astype(f32)
            ).astype(rows.dtype)

        sum_of(shift(self.i, 2))
        block = rows.at[shift(self.i, 2)]
        self.a = self.c.start(self.base + 6, block.at[one], self.l3.at[0], ax, 1)
        self.b = self.c.start(self.base + 7, block.at[two], self.l3.at[1], ax, -1)
        sum_of(shift(self.i, 1))
        sum_of(shift(self.i, -1))
        right, left = rows.at[shift(self.i, 1)], rows.at[shift(self.i, -1)]
        self.ea = self.c.start(self.base + 8, right.at[two], self.l4.at[0, two], ax, 1)
        self.eb = self.c.start(self.base + 9, left.at[one], self.l4.at[1, one], ax, -1)
        sum_of(self.i)

    def inner_late(self):
        ax = INNER[self.half]
        n = self.part.shape[2] // 2
        one, two = pl.ds(0, n), pl.ds(n, n)
        right = self.part.at[self.row(), shift(self.i, 1), one]
        left = self.part.at[self.row(), shift(self.i, -1), two]
        self.a.wait_recv()
        self.add(right, self.l3.at[0])
        self.a = self.c.start(self.base + 10, right, self.l4.at[0, one], ax, 1)
        self.b.wait_recv()
        self.add(left, self.l3.at[1])
        self.b = self.c.start(self.base + 11, left, self.l4.at[1, two], ax, -1)

    def result(self):
        for copy in (self.ea, self.eb, self.a, self.b):
            copy.wait_recv()
        own = self.part[self.row(), self.i].astype(f32)
        return own + self.l4[0].astype(f32) + self.l4[1].astype(f32)


def sum_landings(columns):
    return [
        pltpu.VMEM((2, 2, 2, BLOCK, columns), bf16),
        pltpu.VMEM((2, 2, 4, BLOCK, columns), bf16),
        pltpu.VMEM((2, 2, BLOCK // 2, columns), bf16),
        pltpu.VMEM((2, 2, BLOCK, columns), bf16),
    ]


class RingSum:
    def __init__(self, copies, base, axis, part, half_land, full_land):
        self.c = copies
        self.base = base
        self.axis = axis
        self.part = part
        self.hl = half_land
        self.fl = full_land
        self.i = lax.axis_index(axis)
        n = part.shape[1] // 2
        self.one, self.two = pl.ds(0, n), pl.ds(n, n)

    def start(self):
        self.far()
        self.early()

    def far(self):
        far = self.part.at[shift(self.i, 2)]
        self.a = self.c.start(self.base, far.at[self.one], self.hl.at[0], self.axis, 1)
        self.b = self.c.start(self.base + 1, far.at[self.two], self.hl.at[1], self.axis, -1)

    def early(self):
        right, left = self.part.at[shift(self.i, 1)], self.part.at[shift(self.i, -1)]
        one, two, ax = self.one, self.two, self.axis
        self.ea = self.c.start(self.base + 2, right.at[two], self.fl.at[0, two], ax, 1)
        self.eb = self.c.start(self.base + 3, left.at[one], self.fl.at[1, one], ax, -1)

    def late(self):
        right = self.part.at[shift(self.i, 1), self.one]
        left = self.part.at[shift(self.i, -1), self.two]
        self.a.wait_recv()
        right[...] = (right[...].astype(f32) + self.hl[0].astype(f32)).astype(bf16)
        self.a = self.c.start(self.base + 4, right, self.fl.at[0, self.one], self.axis, 1)
        self.b.wait_recv()
        left[...] = (left[...].astype(f32) + self.hl[1].astype(f32)).astype(bf16)
        self.b = self.c.start(self.base + 5, left, self.fl.at[1, self.two], self.axis, -1)

    def finish(self):
        for copy in (self.ea, self.eb, self.a, self.b):
            copy.wait_recv()
        own = self.part.at[self.i]
        own[...] = (
            own[...].astype(f32) + self.fl[0].astype(f32) + self.fl[1].astype(f32)
        ).astype(bf16)
        return own


class RingGather:
    def __init__(self, copies, base, axis, full):
        self.c = copies
        self.base = base
        self.axis = axis
        self.full = full
        self.i = lax.axis_index(axis)

    def step1(self):
        own = self.full.at[self.i]
        self.a = self.c.start(self.base, own, own, self.axis, 1)
        self.b = self.c.start(self.base + 1, own, own, self.axis, -1)

    def step2(self):
        n = self.full.shape[1] // 2
        self.a.wait_recv()
        left = self.full.at[shift(self.i, -1), pl.ds(0, n)]
        self.a = self.c.start(self.base + 2, left, left, self.axis, 1)
        self.b.wait_recv()
        right = self.full.at[shift(self.i, 1), pl.ds(n, n)]
        self.b = self.c.start(self.base + 3, right, right, self.axis, -1)

    def finish(self):
        self.a.wait_recv()
        self.b.wait_recv()


class RingThenPair:
    def __init__(self, copies, base, buf):
        self.c = copies
        self.base = base
        self.buf = buf
        self.i = lax.axis_index("head")

    def pair(self, slot, index):
        return self.c.start(
            self.base + slot, self.buf.at[index, 0], self.buf.at[index, 1], "seq", 2
        )

    def start(self):
        own = self.buf.at[self.i, 0]
        self.a = self.c.start(self.base, own, own, "head", 1)
        self.b = self.c.start(self.base + 1, own, own, "head", -1)
        self.pairs = [self.pair(2, self.i)]

    def forward(self):
        n = self.buf.shape[2] // 2
        left, right = shift(self.i, -1), shift(self.i, 1)
        self.a.wait_recv()
        block = self.buf.at[left, 0, pl.ds(0, n)]
        self.a = self.c.start(self.base + 3, block, block, "head", 1)
        self.b.wait_recv()
        block = self.buf.at[right, 0, pl.ds(n, n)]
        self.b = self.c.start(self.base + 4, block, block, "head", -1)
        self.pairs += [self.pair(5, left), self.pair(6, right)]

    def last(self):
        self.a.wait_recv()
        self.b.wait_recv()
        self.pairs.append(self.pair(7, shift(self.i, 2)))

    def finish(self):
        for copy in self.pairs:
            copy.wait_recv()


class PairThenRing:
    def __init__(self, copies, base, buf):
        self.c = copies
        self.base = base
        self.buf = buf
        self.gather = RingGather(copies, base + 1, "head", buf)

    def start(self):
        i = self.gather.i
        self.pair = self.c.start(
            self.base, self.buf.at[i, 0], self.buf.at[i, 1], "seq", 2
        )

    def ring(self):
        self.pair.wait_recv()
        self.gather.step1()

    def forward(self):
        self.gather.step2()

    def finish(self):
        self.gather.finish()


class PairThenRingSum:
    def __init__(self, copies, base, part, pair_land, half_land, full_land):
        self.c = copies
        self.base = base
        self.part = part
        self.pl = pair_land
        self.ring = RingSum(copies, base + 4, "head", part.at[:, 0], half_land, full_land)
        self.i = self.ring.i

    def start(self):
        self.pairs = []
        for n, by in enumerate((2, 1, 3, 0)):
            j = shift(self.i, by)
            self.pairs.append(
                self.c.start(self.base + n, self.part.at[j, 1], self.pl.at[j], "seq", 2)
            )

    def added(self, n, by):
        self.pairs[n].wait_recv()
        j = shift(self.i, by)
        self.part[j, 0] = (self.part[j, 0].astype(f32) + self.pl[j].astype(f32)).astype(bf16)

    def along(self):
        self.added(0, 2)
        self.ring.far()
        self.added(1, 1)
        self.added(2, 3)
        self.ring.early()
        self.added(3, 0)

    def late(self):
        self.ring.late()

    def result(self):
        return self.ring.finish()[...].astype(f32)


class TwoRings:
    def __init__(self, copies, base, buf):
        self.c = copies
        self.base = base
        self.buf = buf
        self.own = RingGather(copies, base + 1, "head", buf.at[:, 0])
        self.other = RingGather(copies, base + 5, "head", buf.at[:, 1])

    def pair(self):
        i = self.own.i
        self.p = self.c.start(self.base, self.buf.at[i, 0], self.buf.at[i, 1], "seq", 2)

    def other_step1(self):
        self.p.wait_recv()
        self.other.step1()

    def finish(self):
        self.own.finish()
        self.other.finish()


class RingThenPairSum:
    def __init__(self, copies, base, part, pair_land, half_land, full_land):
        self.c = copies
        self.base = base
        self.pl = pair_land
        self.ring = RingSum(copies, base + 1, "head", part, half_land, full_land)
        self.far, self.early, self.late = self.ring.far, self.ring.early, self.ring.late

    def pair(self):
        self.own = self.ring.finish()
        self.p = self.c.start(self.base, self.own.at[1], self.pl, "seq", 2)

    def result(self):
        self.p.wait_recv()
        return self.own[0].astype(f32) + self.pl[...].astype(f32)


def ring_then_pair_landings(columns):
    return [
        pltpu.VMEM((BLOCK, columns), bf16),
        pltpu.VMEM((2, 1, BLOCK, columns), bf16),
        pltpu.VMEM((2, 2, BLOCK, columns), bf16),
    ]


def pair_then_ring_landings(columns):
    return [
        pltpu.VMEM((4, BLOCK, columns), bf16),
        pltpu.VMEM((2, BLOCK // 2, columns), bf16),
        pltpu.VMEM((2, BLOCK, columns), bf16),
    ]


def mate():
    return 1 - 2 * lax.rem(lax.axis_index("seq"), 2)


UNIT = 4 * BLOCK


def ffn_kernel(
    h2_ref,
    dy_ref,
    win_ref,
    wdn_ref,
    w_ref,
    outp_ref,
    dh2_ref,
    gsum_ref,
    h2a,
    dya,
    pairs,
    win,
    wdn,
    hid,
    dbo,
    dpt,
    *scratch,
):
    land_a, land_b = scratch[:3], scratch[3:6]
    stage, gst, gland, send, recv, lsem, osem = scratch[6:]
    share = gst.shape[2] // 3
    units, width = wdn.shape
    copies = Copies(send, recv)
    i = lax.axis_index("head")
    part = pairs.shape[0]
    load_pairs = [
        pltpu.make_async_copy(win_ref.at[pl.ds(n * part, part)], pairs, lsem.at[n])
        for n in (0, 1)
    ]
    loads = [
        pltpu.make_async_copy(dy_ref, dya, lsem.at[2]),
        pltpu.make_async_copy(wdn_ref, wdn.at[pl.ds(0, share)], lsem.at[3]),
        pltpu.make_async_copy(
            w_ref.at[pl.ds(2 * share, share)], wdn.at[pl.ds(share, share)], lsem.at[4]
        ),
        pltpu.make_async_copy(w_ref.at[pl.ds(0, share)], win.at[pl.ds(share, share)], lsem.at[5]),
        pltpu.make_async_copy(
            w_ref.at[pl.ds(share, share)], win.at[pl.ds(units + share, share)], lsem.at[6]
        ),
    ]
    for load in (load_pairs[0], *loads):
        load.start()

    def split_pairs(n):
        first = n * part
        win[first : first + part] = pairs[:, 0, :]
        win[units + first : units + first + part] = pairs[:, 1, :]

    barrier_with(PAIRED, core=True)
    for half in (0, 1):
        h2a[half, i, 0] = h2_ref[half]
    gather_a = RingThenPair(copies, 0, h2a.at[0])
    gather_b = PairThenRing(copies, 8, h2a.at[1])
    gather_b.start()
    gather_a.start()

    def places(u):
        if u < 2:
            return None
        return (shift(i, 1), shift(i, -1)) if u == 2 else (i, shift(i, 2))

    def tokens_of(ref, u, cols=slice(None)):
        if u < 2:
            value = ref[0, :, u, :, cols]
            return value.reshape(UNIT, value.shape[-1])
        values = [ref[1, j, :, :, cols] for j in places(u)]
        return jnp.concatenate([v.reshape(UNIT // 2, v.shape[-1]) for v in values], 0)

    def columns_of(u):
        return slice(u * UNIT, (u + 1) * UNIT)

    def hidden_back(u):
        dbo[:units, columns_of(u)] = nt(wdn[...], tokens_of(dya, u)).astype(bf16)

    def forward(u):
        cols = columns_of(u)
        t = tokens_of(h2a, u)
        for s in (0, 1):
            one = slice(s * share, (s + 1) * share)
            two = slice(units + s * share, units + (s + 1) * share)
            gate = nt(win[one], t)
            up = nt(win[two], t)
            sig = 1.0 / (1.0 + jnp.exp(-gate))
            act = gate * sig
            d_hidden = dbo[one, cols].astype(f32)
            hid[one, cols] = (act * up).astype(bf16)
            dbo[one, cols] = (d_hidden * up * (sig * (1.0 + gate * (1.0 - sig)))).astype(bf16)
            dbo[two, cols] = (d_hidden * act).astype(bf16)

    def back(u):
        value = tn(dbo[:, columns_of(u)], win[...]).astype(bf16)
        if u < 2:
            dpt[0, :, u] = value.reshape(4, BLOCK, width)
        else:
            for n, j in enumerate(places(u)):
                dpt[1, j] = value[n * UNIT // 2 : (n + 1) * UNIT // 2].reshape(2, BLOCK, width)

    load_pairs[0].wait()
    split_pairs(0)
    load_pairs[1].start()
    gather_b.ring()
    gather_a.forward()
    load_pairs[1].wait()
    split_pairs(1)
    gather_a.last()
    for load in loads:
        load.wait()
    hidden_back(0)
    forward(0)
    gather_b.forward()
    for u in (2, 1, 3):
        hidden_back(u)
    sum_a = PairThenRingSum(copies, 16, dpt.at[0], *land_a)
    sum_b = RingThenPairSum(copies, 26, dpt.at[1], *land_b)
    forward(2)
    back(2)
    sum_b.early()
    gather_a.finish()
    forward(1)
    back(1)
    sum_a.start()
    gather_b.finish()
    forward(3)
    back(3)
    sum_b.far()
    back(0)

    tiles, half_rows, tile = gland.shape[0], gland.shape[2], gland.shape[3]
    core = lax.axis_index("dp_1")
    mine = pl.ds(pl.multiple_of(core * half_rows, 16), half_rows)
    theirs = pl.ds(pl.multiple_of((1 - core) * half_rows, 16), half_rows)
    swaps = []

    def gradients(n):
        cols = slice(n * tile, (n + 1) * tile)
        value = nn(
            dbo[...], jnp.concatenate([tokens_of(h2a, u, cols) for u in range(4)], 0)
        ).astype(bf16)
        down = nn(
            hid[...], jnp.concatenate([tokens_of(dya, u, cols) for u in range(4)], 0)
        ).astype(bf16)
        for s in (0, 1):
            gst[n, s, :share] = value[s * share : (s + 1) * share]
            gst[n, s, share : 2 * share] = value[units + s * share : units + (s + 1) * share]
            gst[n, s, 2 * share :] = down[s * share : (s + 1) * share]
        swaps.append(copies.start_to_core(34 + n, gst.at[n, :, theirs], gland.at[n]))

    def out_copies(u):
        slot = stage.at[u % 2]
        if u < 2:
            return [pltpu.make_async_copy(slot, outp_ref.at[0, :, u], osem.at[u % 2, 0])]
        return [
            pltpu.make_async_copy(
                slot.at[pl.ds(2 * n, 2)], outp_ref.at[1, j], osem.at[u % 2, n]
            )
            for n, j in enumerate(places(u))
        ]

    def out_part(u):
        if u >= 2:
            for copy in out_copies(u - 2):
                copy.wait()
        value = tn(hid[:, columns_of(u)], wdn[...])
        stage[u % 2] = value.astype(bf16).reshape(4, BLOCK, width)
        for copy in out_copies(u):
            copy.start()

    gradients(0)
    gradients(1)
    sum_b.late()
    gradients(2)
    gradients(3)
    sum_b.pair()
    out_part(0)
    sum_a.along()
    out_part(1)
    sum_a.late()
    out_part(2)
    dh2_ref[1] = sum_b.result()
    out_part(3)
    for n, swap in enumerate(swaps):
        swap.wait_recv()
        gland[n] = (gst[n, :, mine].astype(f32) + gland[n].astype(f32)).astype(bf16)
    keep = pltpu.make_async_copy(gland, gsum_ref, lsem.at[0])
    keep.start()
    dh2_ref[0] = sum_a.result()
    for u in (2, 3):
        for copy in out_copies(u):
            copy.wait()
    keep.wait()
    copies.finish()


def ffn(h2, dy_all, w_in, w_down, weights):
    share, width = w_down.shape
    tokens = 4 * UNIT
    tile = 512
    any_spec = pl.BlockSpec(memory_space=pl.ANY)
    vmem_spec = pl.BlockSpec(memory_space=pltpu.VMEM)
    buffer = (2, 4, 2, BLOCK, width)
    sums = (width // tile, 2, 3 * share // 2, tile)
    return pl.pallas_call(
        ffn_kernel,
        out_shape=(
            jax.ShapeDtypeStruct(buffer, bf16),
            jax.ShapeDtypeStruct((2, BLOCK, width), f32),
            jax.ShapeDtypeStruct(sums, bf16),
        ),
        in_specs=[vmem_spec, *[any_spec] * 4],
        out_specs=(any_spec, vmem_spec, any_spec),
        scratch_shapes=[
            pltpu.VMEM(buffer, bf16),
            pltpu.VMEM(buffer, bf16),
            pltpu.VMEM((share // 2, 2, width), bf16),
            pltpu.VMEM((4 * share, width), bf16),
            pltpu.VMEM((2 * share, width), bf16),
            pltpu.VMEM((2 * share, tokens), bf16),
            pltpu.VMEM((4 * share, tokens), bf16),
            pltpu.VMEM(buffer, bf16),
            *pair_then_ring_landings(width),
            *ring_then_pair_landings(width),
            pltpu.VMEM((2, 4, BLOCK, width), bf16),
            pltpu.VMEM((width // tile, 2, 3 * share, tile), bf16),
            pltpu.VMEM(sums, bf16),
            pltpu.SemaphoreType.DMA((38,)),
            pltpu.SemaphoreType.DMA((38,)),
            pltpu.SemaphoreType.DMA((7,)),
            pltpu.SemaphoreType.DMA((2, 2)),
        ],
        compiler_params=pltpu.CompilerParams(
            collective_id=1, has_side_effects=True, vmem_limit_bytes=VMEM_BYTES
        ),
        name="ffn",
    )(h2, dy_all, w_in, w_down, weights)


def mask_rows(starts_ref, row, transposed, mask_ref):
    seq, head = lax.axis_index("seq"), lax.axis_index("head")
    keys = 16 * BLOCK
    index = lax.broadcasted_iota(jnp.int32, (1, keys), 1)
    if transposed:
        group = lax.div(index, 4 * BLOCK)
        inner = lax.rem(lax.div(index, BLOCK), 4)
        k_pos = (inner * 4 + group) * BLOCK + lax.rem(index, BLOCK)
    else:
        k_pos = index
    first = (seq * 4 + head) * BLOCK
    q_pos = first + lax.broadcasted_iota(jnp.int32, (BLOCK, 1), 0)
    k_doc = jnp.zeros((1, keys), jnp.int32)
    q_doc = jnp.zeros((BLOCK, 1), jnp.int32)
    for d in range(starts_ref.shape[1]):
        start = starts_ref[row, d]
        k_doc += (start <= k_pos).astype(jnp.int32)
        q_doc += (start <= q_pos).astype(jnp.int32)
    seen = (k_pos <= q_pos) & (k_doc == q_doc)
    mask_ref[row] = seen.astype(f32)


LOG2E_SCALE = SCALE * math.log2(math.e)


def stacked(block, where):
    rows = jnp.concatenate([block[:, h * HD : (h + 1) * HD] for h in range(PER_GROUP)], 0)
    zero = jnp.zeros_like(rows)
    return jnp.concatenate([rows, zero] if where == 0 else [zero, rows], 1)


def unstacked(rows):
    return jnp.concatenate([rows[h * BLOCK : (h + 1) * BLOCK] for h in range(PER_GROUP)], 1)


def weights_of(q_rows, kv_rows, mask):
    scores = nt(q_rows, kv_rows)
    keys = kv_rows.shape[0]
    e = jnp.exp2(scores * LOG2E_SCALE).reshape(PER_GROUP, BLOCK, keys) * mask[None]
    return e.reshape(PER_GROUP * BLOCK, keys)


GROUP_COLS = PER_GROUP * HD
KV_COLS = 2 * HD


def head_means(columns=GROUP_COLS):
    a = lax.div(lax.broadcasted_iota(jnp.int32, (columns, columns), 0), HD)
    b = lax.div(lax.broadcasted_iota(jnp.int32, (columns, columns), 1), HD)
    return jnp.where(a == b, 1.0 / HD, 0.0).astype(f32)


def head_mean(v, means):
    return jnp.dot(v, means, precision=lax.Precision.HIGHEST, preferred_element_type=f32)


def swapped(v):
    columns = v.shape[1]
    lane = lax.rem(lax.broadcasted_iota(jnp.int32, v.shape, 1), HD)
    up = pltpu.roll(v, columns - HD // 2, 1)
    down = pltpu.roll(v, HD // 2, 1)
    return jnp.where(lane < HD // 2, up, down)


def turned(raw, gain, cosine, sine, means):
    normed = raw * lax.rsqrt(head_mean(raw * raw, means) + EPS)
    v = normed * gain
    return v * cosine + swapped(v) * sine


def turned_back(grad, raw, gain, cosine, sine, means):
    inverse = lax.rsqrt(head_mean(raw * raw, means) + EPS)
    normed = raw * inverse
    u = grad * cosine - swapped(grad) * sine
    gain_grad = jnp.sum(u * normed, axis=0, keepdims=True)
    e = u * gain
    return inverse * (e - normed * head_mean(e * normed, means)), gain_grad


def rms_parts(v):
    inverse = lax.rsqrt(jnp.mean(v * v, axis=-1, keepdims=True) + EPS)
    return (v * inverse, inverse)


def rms_back(grad, normed, inverse):
    return inverse * (grad - normed * jnp.mean(grad * normed, axis=-1, keepdims=True))


def front_kernel(
    starts_ref,
    x_ref,
    wqkv_ref,
    wout_ref,
    ga_ref,
    gf_ref,
    qg_ref,
    kg_ref,
    cos_ref,
    sin_ref,
    dy_ref,
    win_ref,
    wdn_ref,
    h1_out,
    raw_out,
    q_out,
    kva_ref,
    mixed_out,
    r1_ref,
    h2_ref,
    dya_ref,
    w_ref,
    h1_ref,
    raw_ref,
    q_ref,
    mixed_ref,
    wq,
    wkv,
    wo,
    own,
    kva,
    dya,
    pown,
    wsend,
    wall,
    qst,
    mask,
    oacc,
    lacc,
    send,
    recv,
    lsem,
):
    count, width = x_ref.shape
    q_cols = HEADS * HD
    k_cols = KV * HD
    loads = [
        pltpu.make_async_copy(wqkv_ref.at[:, pl.ds(q_cols, 2 * k_cols)], wkv, lsem.at[0]),
        pltpu.make_async_copy(wqkv_ref.at[:, pl.ds(0, q_cols)], wq, lsem.at[1]),
        pltpu.make_async_copy(wout_ref, wo, lsem.at[2]),
    ]
    share = wdn_ref.shape[0]
    z, core = lax.axis_index("dp_0"), lax.axis_index("dp_1")
    strip = wsend.shape[1]
    strip_cols = pl.ds(pl.multiple_of((z * 2 + core) * strip, strip), strip)
    strips = [
        pltpu.make_async_copy(win_ref.at[:, :, strip_cols], pown, lsem.at[5]),
        pltpu.make_async_copy(
            wdn_ref.at[:, strip_cols], wsend.at[pl.ds(2 * share, share)], lsem.at[6]
        ),
    ]
    for load in strips + loads:
        load.start()
    copies = Copies(send, recv)
    barrier_with(PLANE + STACK + (("seq", 2),), core=True)
    head = lax.axis_index("head")
    for half in (0, 1):
        dya[half, head, 0] = dy_ref[half]
    cotangents = [TwoRings(copies, 16 + 9 * half, dya.at[half]) for half in (0, 1)]
    cotangents[0].own.step1()
    for load in strips:
        load.wait()
    wsend[:share] = pown[:, 0, :]
    wsend[share : 2 * share] = pown[:, 1, :]
    strip_move = copies.start(34, wsend, wall.at[z, core], "seq", mate())
    stack = RingGather(copies, 35, "dp_0", wall.at[:, core])
    strip_swaps = []

    def swap_strip(by):
        block = wall.at[shift(z, by), core]
        strip_swaps.append(copies.start_to_core(39 + by % 4, block, block))

    means = head_means()
    cosine, sine = cos_ref[...], sin_ref[...]
    q_gain, k_gain = (jnp.concatenate([ref[...]] * PER_GROUP, 1) for ref in (qg_ref, kg_ref))
    x = x_ref[...].astype(f32)
    h1_ref[...] = (rms_parts(x)[0] * ga_ref[...]).astype(bf16)
    loads[0].wait()
    kv = nn(h1_ref[...], wkv[...])
    raw_ref[:, q_cols:] = kv
    keys = jnp.concatenate(
        [
            turned(kv[:, c : c + GROUP_COLS], k_gain, cosine, sine, means)
            for c in (0, GROUP_COLS)
        ],
        1,
    )
    for g in range(KV):
        k = keys[:, g * HD : (g + 1) * HD]
        v = kv[:, k_cols + g * HD : k_cols + (g + 1) * HD]
        own[:, :, g * KV_COLS : (g + 1) * KV_COLS] = (
            jnp.concatenate([k, v], 1).astype(bf16).reshape(2, BLOCK, KV_COLS)
        )
    gathers = [PlaneGather(copies, 0, half, own.at[half], kva) for half in (0, 1)]
    for gather in gathers:
        gather.step1()
    for half in (0, 1):
        kva[gathers[half].row(), gathers[half].i] = own[half]
    loads[1].wait()

    def queries(g):
        cols = slice(g * GROUP_COLS, (g + 1) * GROUP_COLS)
        raw = nn(h1_ref[...], wq[:, cols])
        raw_ref[:, cols] = raw
        q = turned(raw, q_gain, cosine, sine, means).astype(bf16)
        q_ref[:, cols] = q
        for row in (0, 1):
            qst[row * KV + g] = stacked(q[row * BLOCK : (row + 1) * BLOCK], 0)

    for g in range(3):
        queries(g)
    for gather in gathers:
        gather.step2()
    for g in range(3, KV):
        queries(g)
    for gather in gathers:
        gather.step3()
    early = [
        pltpu.make_async_copy(src, dst, lsem.at[18 + n])
        for n, (src, dst) in enumerate(((h1_ref, h1_out), (raw_ref, raw_out), (q_ref, q_out)))
    ]
    for copy in early:
        copy.start()
    mask_rows(starts_ref, 0, False, mask)
    mask_rows(starts_ref, 1, True, mask)
    seq = lax.axis_index("seq")

    def scored(row, by, first):
        group = lax.rem(seq + row * (head - seq) + by + 4, 4)
        seen = mask[row, :, pl.ds(pl.multiple_of(group * 4 * BLOCK, 4 * BLOCK), 4 * BLOCK)]
        for g in range(KV):
            index = row * KV + g
            kv_rows = kva[
                4 * row + group, :, :, g * KV_COLS : (g + 1) * KV_COLS
            ].reshape(4 * BLOCK, KV_COLS)
            e = weights_of(qst[index], kv_rows, seen)
            total = e[:, : 2 * BLOCK] + e[:, 2 * BLOCK :]
            mixed = nn(e.astype(bf16), kv_rows)
            if first:
                lacc[index] = total
                oacc[index] = mixed
            else:
                lacc[index] += total
                oacc[index] += mixed

    @pl.loop(0, 2)
    def _(row):
        scored(row, 0, True)

    strip_move.wait_recv()
    stack.step1()
    swap_strip(0)
    for gather in gathers:
        gather.step4()
    for gather in cotangents:
        gather.pair()
    cotangents[0].own.step2()
    cotangents[1].own.step1()

    @pl.loop(0, 4)
    def _(k):
        scored(lax.div(k, 2), 1 - 2 * lax.rem(k, 2), False)

    for gather in gathers:
        gather.finish()
    keep = pltpu.make_async_copy(kva, kva_ref, lsem.at[3])
    keep.start()

    @pl.loop(0, 2)
    def _(row):
        scored(row, 2, False)

    for row in (0, 1):
        for g in range(KV):
            index = row * KV + g
            mixed = oacc[index][:, HD:] / jnp.sum(lacc[index], axis=1, keepdims=True)
            mixed_ref[
                row * BLOCK : (row + 1) * BLOCK, g * GROUP_COLS : (g + 1) * GROUP_COLS
            ] = unstacked(mixed.astype(bf16))
    stack.step2()
    swap_strip(1)
    swap_strip(-1)
    cotangents[1].own.step2()
    for gather in cotangents:
        gather.other_step1()
    loads[2].wait()
    tile = 512
    for n in range(width // tile):
        cols = slice(n * tile, (n + 1) * tile)
        r1_ref[:, cols] = x_ref[:, cols].astype(f32) + nn(mixed_ref[...], wo[:, cols])
    h2_ref[...] = (rms_parts(r1_ref[...])[0] * gf_ref[...]).astype(bf16)
    keeps = [keep, *early]

    def write(n, src, dst):
        copy = pltpu.make_async_copy(src, dst, lsem.at[n])
        copy.start()
        keeps.append(copy)

    for gather in cotangents:
        gather.other.step2()
    stack.finish()
    swap_strip(2)
    for swap in strip_swaps:
        swap.wait_recv()
    for k in range(8):
        write(9 + k, wall.at[k // 2, k % 2], w_ref.at[:, pl.ds(k * strip, strip)])
    for gather in cotangents:
        gather.finish()
    write(17, dya, dya_ref)
    write(21, mixed_ref, mixed_out)
    for copy in keeps:
        copy.wait()
    copies.finish()


def front(
    starts, x, w_qkv, w_out, g_attn, g_ffn, q_gain, k_gain, cosine, sine, dy, w_in, w_down
):
    count, width = x.shape
    share = w_down.shape[0]
    q_cols = HEADS * HD
    kv_cols = 2 * KV * HD
    vmem_spec = pl.BlockSpec(memory_space=pltpu.VMEM)
    any_spec = pl.BlockSpec(memory_space=pl.ANY)
    return pl.pallas_call(
        front_kernel,
        out_shape=(
            jax.ShapeDtypeStruct((count, width), bf16),
            jax.ShapeDtypeStruct((count, q_cols + kv_cols), f32),
            jax.ShapeDtypeStruct((count, q_cols), bf16),
            jax.ShapeDtypeStruct((8, 4, BLOCK, kv_cols), bf16),
            jax.ShapeDtypeStruct((count, q_cols), bf16),
            jax.ShapeDtypeStruct((count, width), f32),
            jax.ShapeDtypeStruct((count, width), bf16),
            jax.ShapeDtypeStruct((2, 4, 2, BLOCK, width), bf16),
            jax.ShapeDtypeStruct((3 * share, width), bf16),
        ),
        in_specs=[
            pl.BlockSpec(memory_space=pltpu.SMEM),
            vmem_spec,
            any_spec,
            any_spec,
            *[vmem_spec] * 7,
            any_spec,
            any_spec,
        ],
        out_specs=(
            any_spec,
            any_spec,
            any_spec,
            any_spec,
            any_spec,
            vmem_spec,
            vmem_spec,
            any_spec,
            any_spec,
        ),
        scratch_shapes=[
            pltpu.VMEM((count, width), bf16),
            pltpu.VMEM((count, q_cols + kv_cols), f32),
            pltpu.VMEM((count, q_cols), bf16),
            pltpu.VMEM((count, q_cols), bf16),
            pltpu.VMEM((width, q_cols), bf16),
            pltpu.VMEM((width, kv_cols), bf16),
            pltpu.VMEM((q_cols, width), bf16),
            pltpu.VMEM((2, BLOCK, kv_cols), bf16),
            pltpu.VMEM((8, 4, BLOCK, kv_cols), bf16),
            pltpu.VMEM((2, 4, 2, BLOCK, width), bf16),
            pltpu.VMEM((share, 2, width // 8), bf16),
            pltpu.VMEM((3 * share, width // 8), bf16),
            pltpu.VMEM((4, 2, 3 * share, width // 8), bf16),
            pltpu.VMEM((2 * KV, PER_GROUP * BLOCK, KV_COLS), bf16),
            pltpu.VMEM((2, BLOCK, 16 * BLOCK), f32),
            pltpu.VMEM((2 * KV, PER_GROUP * BLOCK, KV_COLS), f32),
            pltpu.VMEM((2 * KV, PER_GROUP * BLOCK, 2 * BLOCK), f32),
            pltpu.SemaphoreType.DMA((43,)),
            pltpu.SemaphoreType.DMA((43,)),
            pltpu.SemaphoreType.DMA((22,)),
        ],
        compiler_params=pltpu.CompilerParams(
            collective_id=2, has_side_effects=True, vmem_limit_bytes=VMEM_BYTES
        ),
        name="front",
    )(starts, x, w_qkv, w_out, g_attn, g_ffn, q_gain, k_gain, cosine, sine, dy, w_in, w_down)


AXIS_ORDERS = (("head", "dp_0", "seq"), ("seq", "head", "dp_0"))
OUT_SLICES = ((0, 0, 896), (1, 896, 896))
QKV_SLICES = ((0, 0, 768), (1, 1280, 896), (0, 768, 512), (1, 2176, 512))
CHIP_AXES = ("dp_0", "seq", "head")


class Slices:
    sems = 15

    def __init__(self, copies, base, slices, lhs, rhs, scratch):
        self.c = copies
        self.base = base
        self.slices = slices
        self.lhs = lhs
        self.rhs = rhs
        n = len(slices)
        self.parts, half1, full1, self.half2, self.full2, self.last = (
            scratch[n * k : n * (k + 1)] for k in range(6)
        )
        self.orders = [AXIS_ORDERS[order] for order, _, _ in slices]
        self.rings = [
            RingSum(copies, base + 15 * k, self.orders[k][0], self.parts[k], half1[k], full1[k])
            for k in range(n)
        ]
        self.rings2 = [None] * n
        self.owns = [None] * n
        self.ends = [None] * n

    @staticmethod
    def scratch(slices):
        def each(make):
            return [pltpu.VMEM(make(width), bf16) for _, _, width in slices]

        return [
            *each(lambda w: (4, 4, 4, 16, w)),
            *each(lambda w: (2, 2, 4, 16, w)),
            *each(lambda w: (2, 4, 4, 16, w)),
            *each(lambda w: (2, 2, 16, w)),
            *each(lambda w: (2, 4, 16, w)),
            *each(lambda w: (3, 16, w)),
        ]

    def make(self, k):
        order, first, width = self.slices[k]
        part = self.parts[k]

        @pl.loop(0, 4)
        def _(z):
            cols = pl.ds(pl.multiple_of(z * 256, 256), 256)
            value = tn(self.lhs[:, cols], self.rhs[:, first : first + width]).astype(bf16)
            value = value.reshape(4, 4, 16, width)
            if order == 1:
                part[:, :, z] = value
            else:
                for y in range(4):
                    part[:, z, y] = value[y]

    def begin(self):
        for k in range(len(self.slices)):
            self.make(k)
            self.rings[k].start()

    def late(self, k):
        self.rings[k].late()

    def next_axis(self, k):
        own = self.rings[k].finish()
        self.rings2[k] = RingSum(
            self.c, self.base + 15 * k + 6, self.orders[k][1], own, self.half2[k], self.full2[k]
        )
        self.rings2[k].start()

    def late2(self, k):
        self.rings2[k].late()

    def last_axis(self, k):
        self.owns[k] = self.rings2[k].finish()
        axis = self.orders[k][2]
        i = lax.axis_index(axis)
        self.ends[k] = [
            self.c.start(
                self.base + 15 * k + 12 + n, self.owns[k].at[shift(i, by)], self.last[k].at[n], axis, by
            )
            for n, by in enumerate((1, 2, 3))
        ]

    def store(self, k, ref):
        i = lax.axis_index(self.orders[k][2])
        for end in self.ends[k]:
            end.wait_recv()
        value = self.owns[k][i].astype(f32)
        for n in range(3):
            value = value + self.last[k][n].astype(f32)
        _, first, width = self.slices[k]
        ref[:, first : first + width] = value


GAIN_ROWS = 40


def rear_kernel(
    starts_ref,
    dh2_ref,
    r1_ref,
    dy_ref,
    x_ref,
    q_ref,
    raw_ref,
    h1_ref,
    mix_ref,
    kva_ref,
    wqkv_ref,
    wout_ref,
    gsum_ref,
    outp_ref,
    ga_ref,
    gf_ref,
    qg_ref,
    kg_ref,
    cos_ref,
    sin_ref,
    y_ref,
    gx_ref,
    gain_ref,
    gpart_ref,
    h1_out,
    dq_out,
    right_ref,
    wbuf,
    wkv,
    kva,
    gsum,
    gl1,
    gl2,
    gpair,
    gpart,
    outp,
    mask,
    d_r1,
    d_o,
    dq,
    d_h1,
    da,
    h1c,
    dac,
    dqc,
    mxc,
    *scratch,
):
    landings, out_landings = scratch[:4], (scratch[4:7], scratch[7:10])
    send, recv, lsem = scratch[-3:]
    count, width = x_ref.shape
    q_cols = HEADS * HD
    k_cols = KV * HD
    seq, head = lax.axis_index("seq"), lax.axis_index("head")
    loads = [
        pltpu.make_async_copy(outp_ref.at[0], outp.at[0], lsem.at[6]),
        pltpu.make_async_copy(outp_ref.at[1], outp.at[1], lsem.at[7]),
        pltpu.make_async_copy(gsum_ref, gsum, lsem.at[3]),
    ]
    loads += [
        pltpu.make_async_copy(wout_ref, wbuf.at[pl.ds(0, q_cols)], lsem.at[0]),
        pltpu.make_async_copy(kva_ref, kva, lsem.at[1]),
        pltpu.make_async_copy(wqkv_ref.at[:, pl.ds(q_cols, 2 * k_cols)], wkv, lsem.at[2]),
    ]
    for load in loads:
        load.start()
    load_wo, load_kva, load_wkv = loads[-3:]
    load_wq = pltpu.make_async_copy(
        wqkv_ref.at[:, pl.ds(0, q_cols)], wbuf.at[:, pl.ds(0, q_cols)], lsem.at[5]
    )
    copies = Copies(send, recv)
    core = lax.axis_index("dp_1")
    mine, theirs = pl.ds(0, count), pl.ds(count, count)

    def piece(z, which):
        return pl.ds(pl.multiple_of(z * 512 + which * 256, 256), 256)

    barrier_with(PLANE + STACK + (("seq", 2), ("dp_0", 2), ("head", 2)), core=True)
    out_slices = Slices(copies, 70, OUT_SLICES, dac, mxc, scratch[10:-3])
    outs = [
        RingThenPairSum(copies, 24 + 7 * half, outp.at[half], *out_landings[half])
        for half in (0, 1)
    ]
    gring = RingSum(copies, 38, "dp_0", gsum, gl1, gl2)
    for half in (0, 1):
        loads[half].wait()
        outs[half].far()
    loads[2].wait()
    gring.start()
    for total in outs:
        total.early()
    lanes128 = gain_ref.shape[1]
    n_rows = width // lanes128

    def put_gain(first, value):
        for n in range(value.shape[1] // lanes128):
            gain_ref[first + n : first + n + 1] = value[:, n * lanes128 : (n + 1) * lanes128]

    n2, inv2 = rms_parts(r1_ref[...])
    d_h2 = dh2_ref[...]
    gain_ref[...] = jnp.zeros_like(gain_ref)
    put_gain(n_rows, jnp.sum(d_h2 * n2, axis=0, keepdims=True))
    d_r1[...] = dy_ref[...].astype(f32) + rms_back(d_h2 * gf_ref[...], n2, inv2)
    da[...] = d_r1[...].astype(bf16)
    swaps = [copies.start_to_core(58, mix_ref, mxc.at[theirs])]
    for z in range(4):
        cols = pl.ds(z * 256, 256)
        h1c[mine, cols] = h1_ref[:, piece(z, core)]
        dac[mine, cols] = da[:, piece(z, core)]
        swaps.append(
            copies.start_to_core(60 + 2 * z, h1_ref.at[:, piece(z, 1 - core)], h1c.at[theirs, cols])
        )
        swaps.append(
            copies.start_to_core(61 + 2 * z, da.at[:, piece(z, 1 - core)], dac.at[theirs, cols])
        )
    mxc[mine] = mix_ref[...]
    mask_rows(starts_ref, 0, False, mask)
    mask_rows(starts_ref, 1, True, mask)
    load_wo.wait()
    for g in range(KV):
        cols = slice(g * GROUP_COLS, (g + 1) * GROUP_COLS)
        d_o[:, cols] = nt(da[...], wbuf[cols]).astype(bf16)
    load_wq.start()
    for swap in swaps:
        swap.wait_recv()
    swaps = []
    load_kva.wait()
    sums = [PlaneSum(copies, 0, half, kva, *landings) for half in (0, 1)]
    for row in (0, 1):
        rows = slice(row * BLOCK, (row + 1) * BLOCK)
        for g in range(KV):
            if row == 1 and g == 2:
                gring.late()
            cols = slice(g * GROUP_COLS, (g + 1) * GROUP_COLS)
            lanes = slice(g * KV_COLS, (g + 1) * KV_COLS)
            q_rows = stacked(q_ref[rows, cols], 0)
            do_rows = stacked(d_o[rows, cols], 1)
            kv_rows = kva[4 * row : 4 * row + 4, :, :, lanes].reshape(16 * BLOCK, KV_COLS)
            e = weights_of(q_rows, kv_rows, mask[row])
            probs = e * (1.0 / jnp.sum(e, axis=1, keepdims=True))
            d_probs = nt(do_rows, kv_rows)
            delta = jnp.sum(probs * d_probs, axis=1, keepdims=True)
            d_scores = (probs * (d_probs - delta)).astype(bf16)
            dq_rows = nn(d_scores, kv_rows)[:, :HD] * SCALE
            dq[rows, cols] = unstacked(dq_rows.astype(bf16))
            dkv = tn(d_scores, q_rows * jnp.asarray(SCALE, bf16)) + tn(probs.astype(bf16), do_rows)
            kva[4 * row : 4 * row + 4, :, :, lanes] = dkv.astype(bf16).reshape(
                4, 4, BLOCK, KV_COLS
            )
        sums[row].far()
        sums[row].early()
        if row == 1:
            out_slices.begin()
    means = head_means()
    cosine, sine = cos_ref[...], sin_ref[...]
    q_gain, k_gain = (jnp.concatenate([ref[...]] * PER_GROUP, 1) for ref in (qg_ref, kg_ref))

    def queries(g):
        cols = slice(g * GROUP_COLS, (g + 1) * GROUP_COLS)
        value, gain = turned_back(
            dq[:, cols].astype(f32), raw_ref[:, cols], q_gain, cosine, sine, means
        )
        dqc[mine, cols] = value.astype(bf16)
        return gain

    gain = queries(0)
    for g in range(1, KV):
        gain += queries(g)
    put_gain(2 * n_rows, gain)
    swaps.append(
        copies.start_to_core(
            68, dqc.at[mine, pl.ds(0, q_cols)], dqc.at[theirs, pl.ds(0, q_cols)]
        )
    )
    for total in sums:
        total.late()
    for total in outs:
        total.late()
    for k in (0, 1):
        out_slices.late(k)
    load_wq.wait()
    load_wkv.wait()
    tile = 512
    for n in range(width // tile):
        cols = slice(n * tile, (n + 1) * tile)
        d_h1[:, cols] = nt(dqc[mine, :q_cols], wbuf[cols, :q_cols])
    for total in sums:
        total.inner_start()
    for total in outs:
        total.pair()
    for total in sums:
        total.inner_late()
    for k in (0, 1):
        out_slices.next_axis(k)
    own_sums = gring.finish()
    gmove = copies.start(44, own_sums.at[1], gpair, "seq", mate())
    d_kv = jnp.concatenate([total.result().astype(bf16) for total in sums], 0)
    pieces = [d_kv[:, g * KV_COLS : g * KV_COLS + HD] for g in range(KV)]
    pieces += [d_kv[:, g * KV_COLS + HD : (g + 1) * KV_COLS] for g in range(KV)]
    d_kv = jnp.concatenate(pieces, 1)
    first, gain1 = turned_back(
        d_kv[:, :GROUP_COLS].astype(f32),
        raw_ref[:, q_cols : q_cols + GROUP_COLS],
        k_gain,
        cosine,
        sine,
        means,
    )
    second, gain2 = turned_back(
        d_kv[:, GROUP_COLS : 2 * GROUP_COLS].astype(f32),
        raw_ref[:, q_cols + GROUP_COLS : q_cols + 2 * GROUP_COLS],
        k_gain,
        cosine,
        sine,
        means,
    )
    lane = lax.broadcasted_iota(jnp.int32, gain2.shape, 1)
    put_gain(
        2 * n_rows + GROUP_COLS // lanes128,
        gain1 + jnp.where(lane < k_cols - GROUP_COLS, gain2, 0.0),
    )
    dqc[mine, q_cols : q_cols + GROUP_COLS] = first.astype(bf16)
    lane = lax.broadcasted_iota(jnp.int32, second.shape, 1)
    dqc[mine, q_cols + GROUP_COLS : q_cols + 2 * GROUP_COLS] = jnp.where(
        lane < k_cols - GROUP_COLS,
        second.astype(bf16),
        d_kv[:, GROUP_COLS : 2 * GROUP_COLS],
    )
    dqc[mine, q_cols + 2 * GROUP_COLS :] = d_kv[:, 2 * GROUP_COLS :]
    kv_part = pl.ds(q_cols, 2 * k_cols)
    swaps.append(copies.start_to_core(69, dqc.at[mine, kv_part], dqc.at[theirs, kv_part]))
    for n in range(width // tile):
        cols = slice(n * tile, (n + 1) * tile)
        d_h1[:, cols] += nt(dqc[mine, q_cols:], wkv[cols])
    for k in (0, 1):
        out_slices.late2(k)
    n1, inv1 = rms_parts(x_ref[...].astype(f32))
    put_gain(0, jnp.sum(d_h1[...] * n1, axis=0, keepdims=True))
    gx_ref[...] = (d_r1[...] + rms_back(d_h1[...] * ga_ref[...], n1, inv1)).astype(bf16)
    for k in (0, 1):
        out_slices.last_axis(k)
    for half in (0, 1):
        rows = slice(half * BLOCK, (half + 1) * BLOCK)
        y_ref[rows] = (r1_ref[rows] + outs[half].result()).astype(bf16)
    gmove.wait_recv()
    gpart[...] = (own_sums[0].astype(f32) + gpair[...].astype(f32)).astype(bf16)
    gkeep = pltpu.make_async_copy(gpart, gpart_ref, lsem.at[4])
    gkeep.start()
    for swap in swaps:
        swap.wait_recv()
    keeps = [
        pltpu.make_async_copy(h1c, h1_out, lsem.at[0]),
        pltpu.make_async_copy(dqc, dq_out, lsem.at[2]),
    ]
    for keep in keeps:
        keep.start()
    for k in (0, 1):
        out_slices.store(k, right_ref)
    for keep in keeps:
        keep.wait()
    gkeep.wait()
    copies.finish()


def rear(
    starts,
    d_h2,
    r1,
    dy,
    x,
    q,
    raw,
    h1,
    mixed,
    kva,
    w_qkv,
    w_out,
    gsum,
    outp,
    g_attn,
    g_ffn,
    q_gain,
    k_gain,
    cosine,
    sine,
):
    count, width = x.shape
    q_cols = HEADS * HD
    kv_cols = 2 * KV * HD
    vmem_spec = pl.BlockSpec(memory_space=pltpu.VMEM)
    any_spec = pl.BlockSpec(memory_space=pl.ANY)
    sums = gsum.shape
    pair_shapes = [
        (2 * count, width // 2),
        (2 * count, width // 2),
        (2 * count, q_cols + kv_cols),
        (2 * count, q_cols),
    ]
    return pl.pallas_call(
        rear_kernel,
        out_shape=(
            jax.ShapeDtypeStruct((count, width), bf16),
            jax.ShapeDtypeStruct((count, width), bf16),
            jax.ShapeDtypeStruct((GAIN_ROWS, 128), f32),
            jax.ShapeDtypeStruct(sums[2:], bf16),
            jax.ShapeDtypeStruct(pair_shapes[0], bf16),
            jax.ShapeDtypeStruct(pair_shapes[2], bf16),
            jax.ShapeDtypeStruct((16, q_cols), f32),
        ),
        in_specs=[
            pl.BlockSpec(memory_space=pltpu.SMEM),
            *[vmem_spec] * 8,
            *[any_spec] * 5,
            *[vmem_spec] * 6,
        ],
        out_specs=(*[vmem_spec] * 3, *[any_spec] * 3, vmem_spec),
        scratch_shapes=[
            pltpu.VMEM((width, width), bf16),
            pltpu.VMEM((width, kv_cols), bf16),
            pltpu.VMEM((8, 4, BLOCK, kv_cols), bf16),
            pltpu.VMEM(sums, bf16),
            pltpu.VMEM((2, 1, *sums[2:]), bf16),
            pltpu.VMEM((2, 2, *sums[2:]), bf16),
            pltpu.VMEM(sums[2:], bf16),
            pltpu.VMEM(sums[2:], bf16),
            pltpu.VMEM((2, 4, 2, BLOCK, width), bf16),
            pltpu.VMEM((2, BLOCK, 16 * BLOCK), f32),
            pltpu.VMEM((count, width), f32),
            pltpu.VMEM((count, q_cols), bf16),
            pltpu.VMEM((count, q_cols), bf16),
            pltpu.VMEM((count, width), f32),
            pltpu.VMEM((count, width), bf16),
            *[pltpu.VMEM(shape, bf16) for shape in pair_shapes],
            *sum_landings(kv_cols),
            *ring_then_pair_landings(width),
            *ring_then_pair_landings(width),
            *Slices.scratch(OUT_SLICES),
            pltpu.SemaphoreType.DMA((100,)),
            pltpu.SemaphoreType.DMA((100,)),
            pltpu.SemaphoreType.DMA((8,)),
        ],
        compiler_params=pltpu.CompilerParams(
            collective_id=3, has_side_effects=True, vmem_limit_bytes=VMEM_BYTES
        ),
        name="rear",
    )(
        starts,
        d_h2,
        r1,
        dy,
        x,
        q,
        raw,
        h1,
        mixed,
        kva,
        w_qkv,
        w_out,
        gsum,
        outp,
        g_attn,
        g_ffn,
        q_gain,
        k_gain,
        cosine,
        sine,
    )


def projections_kernel(
    h1_ref, dq_ref, gain_ref, gpart_ref, left_ref, gain_out, gboth_ref, gsum, gboth, *scratch
):
    send, recv, lsem = scratch[-3:]
    copies = Copies(send, recv)
    barrier_with(tuple((axis, by) for axis in CHIP_AXES for by in (1, 2, 3)), core=True)
    core = lax.axis_index("dp_1")
    gain_move = copies.start_to_core(0, gain_ref, gsum.at[3, core])
    grows = gpart_ref.shape[0]
    place = pl.ds(pl.multiple_of(core * grows, 16), grows)
    stack = RingGather(copies, 10, "dp_0", gboth.at[:, place])
    z = lax.axis_index("dp_0")
    gboth[z, place] = gpart_ref[...]
    stack.step1()
    swaps = []

    def swap_rows(by):
        block = gboth.at[shift(z, by), place]
        swaps.append(copies.start_to_core(14 + by % 4, block, block))

    swap_rows(0)
    work = Slices(copies, 18, QKV_SLICES, h1_ref, dq_ref, scratch[:-3])
    first, second = (0, 1), (2, 3)

    def gain_step(k, axis, value):
        i = lax.axis_index(axis)
        gsum[k, i] = value
        out = []
        for n, by in enumerate((1, 2, 3)):
            src = gsum.at[k, i]
            out.append(copies.start(1 + 3 * k + n, src, src, axis, by))
        return out

    def gain_total(k, moves):
        for move in moves:
            move.wait_recv()
        return gsum[k, 0] + gsum[k, 1] + gsum[k, 2] + gsum[k, 3]

    for k in first:
        work.make(k)
        work.rings[k].start()
    gain_move.wait_recv()
    gsum[3, core] = gain_ref[...]
    gmoves = gain_step(0, CHIP_AXES[0], gsum[3, 0] + gsum[3, 1])
    for k in second:
        work.make(k)
    for k in first:
        work.late(k)
        work.rings[k + 2].start()
    gmoves = gain_step(1, CHIP_AXES[1], gain_total(0, gmoves))
    stack.step2()
    swap_rows(1)
    swap_rows(-1)
    for k in first:
        work.next_axis(k)
    for k in second:
        work.late(k)
    gmoves = gain_step(2, CHIP_AXES[2], gain_total(1, gmoves))
    for k in first:
        work.late2(k)
    for k in first:
        work.last_axis(k)
    for k in second:
        work.next_axis(k)
    gain_out[...] = gain_total(2, gmoves)
    stack.finish()
    swap_rows(2)
    for k in second:
        work.late2(k)
    for k in second:
        work.last_axis(k)
    for swap in swaps:
        swap.wait_recv()
    keep = pltpu.make_async_copy(gboth, gboth_ref, lsem.at[0])
    keep.start()
    for k in range(len(QKV_SLICES)):
        work.store(k, left_ref)
    keep.wait()
    copies.finish()


def projections(h1, d_qkv, gains, gpart):
    vmem_spec = pl.BlockSpec(memory_space=pltpu.VMEM)
    both = (4, 2 * gpart.shape[0], gpart.shape[1])
    return pl.pallas_call(
        projections_kernel,
        out_shape=(
            jax.ShapeDtypeStruct((16, d_qkv.shape[1]), f32),
            jax.ShapeDtypeStruct(gains.shape, f32),
            jax.ShapeDtypeStruct(both, bf16),
        ),
        in_specs=[vmem_spec] * 4,
        out_specs=(vmem_spec, vmem_spec, pl.BlockSpec(memory_space=pl.ANY)),
        scratch_shapes=[
            pltpu.VMEM((4, 4, *gains.shape), f32),
            pltpu.VMEM(both, bf16),
            *Slices.scratch(QKV_SLICES),
            pltpu.SemaphoreType.DMA((78,)),
            pltpu.SemaphoreType.DMA((78,)),
            pltpu.SemaphoreType.DMA((1,)),
        ],
        compiler_params=pltpu.CompilerParams(
            collective_id=4, has_side_effects=True, vmem_limit_bytes=VMEM_BYTES
        ),
        name="projections",
    )(h1, d_qkv, gains, gpart)


def widen_kernel(
    g_ref, y_ref, gx_ref, left_ref, right_ref, gain_ref,
    gin_out, gdn_out, y_out, gx_out, left_out, right_out, ga_out, gf_out, gq_out, gk_out,
):
    units = gdn_out.shape[0]
    gin_out[:, 0, :] = g_ref[:units].astype(f32)
    gin_out[:, 1, :] = g_ref[units : 2 * units].astype(f32)
    gdn_out[...] = g_ref[2 * units :].astype(f32)
    y_out[...] = y_ref[...]
    gx_out[...] = gx_ref[...]
    left_out[...] = left_ref[...]
    right_out[...] = right_ref[...]
    n = ga_out.shape[0]
    ga_out[...] = gain_ref[:n]
    gf_out[...] = gain_ref[n : 2 * n]
    for ref, first in ((gq_out, 2 * n), (gk_out, 2 * n + 2)):
        both = gain_ref[first : first + 1] + gain_ref[first + 1 : first + 2]
        ref[...] = both[:, :HD] + both[:, HD:]


def widen(g, y, gx, left, right, gains, units):
    tiles, _, tile = g.shape
    count, width = y.shape

    def whole(shape):
        return pl.BlockSpec(shape, lambda n: (0,) * len(shape))

    by_tile = pl.BlockSpec((count, tile), lambda n: (0, n))
    gain_rows = width // 128
    return pl.pallas_call(
        widen_kernel,
        grid=(tiles,),
        out_shape=(
            jax.ShapeDtypeStruct((units, 2, width), f32),
            jax.ShapeDtypeStruct((units, width), f32),
            jax.ShapeDtypeStruct(y.shape, bf16),
            jax.ShapeDtypeStruct(gx.shape, bf16),
            jax.ShapeDtypeStruct(left.shape, f32),
            jax.ShapeDtypeStruct(right.shape, f32),
            jax.ShapeDtypeStruct((gain_rows, 128), f32),
            jax.ShapeDtypeStruct((gain_rows, 128), f32),
            jax.ShapeDtypeStruct((1, HD), f32),
            jax.ShapeDtypeStruct((1, HD), f32),
        ),
        in_specs=[
            pl.BlockSpec((None, 3 * units, tile), lambda n: (n, 0, 0)),
            by_tile,
            by_tile,
            whole(left.shape),
            whole(right.shape),
            whole(gains.shape),
        ],
        out_specs=(
            pl.BlockSpec((units, 2, tile), lambda n: (0, 0, n)),
            pl.BlockSpec((units, tile), lambda n: (0, n)),
            by_tile,
            by_tile,
            whole(left.shape),
            whole(right.shape),
            whole((gain_rows, 128)),
            whole((gain_rows, 128)),
            whole((1, HD)),
            whole((1, HD)),
        ),
        compiler_params=pltpu.CompilerParams(vmem_limit_bytes=VMEM_BYTES),
        name="widen",
    )(g, y, gx, left, right, gains)


def angle_tables(positions, columns):
    lane = jnp.arange(columns)
    freq = jnp.exp((lane % (HD // 2)).astype(f32) * (-2.0 * math.log(10000.0) / HD))
    angle = positions.astype(f32)[:, None] * freq[None, :]
    sign = jnp.where(lane % HD < HD // 2, -1.0, 1.0)
    return (jnp.cos(angle), jnp.sin(angle) * sign[None, :])


def body(
    tokens, w_qkv, w_out, w_ffn_in, w_ffn_out, g_attn, g_ffn, q_gain, k_gain, doc_starts, d_out
):
    rows, tok, width = tokens.shape
    count = rows * tok
    n_seq = lax.axis_size("seq")
    n_head = lax.axis_size("head")
    first = (lax.axis_index("seq") * n_head + lax.axis_index("head")) * tok
    cosine, sine = angle_tables(first + jnp.arange(count) % tok, GROUP_COLS)
    x = tokens.reshape(count, width)
    dy = d_out.reshape(count, width)
    ga = g_attn[None]
    gf = g_ffn[None]
    qg = q_gain[None]
    kg = k_gain[None]
    h1, raw, q, kva, mixed, r1, h2, dy_all, weights = front(
        doc_starts, x, w_qkv, w_out, ga, gf, qg, kg, cosine, sine, d_out, w_ffn_in, w_ffn_out
    )
    outp, d_h2, gsum = ffn(
        h2.reshape(rows, tok, width), dy_all, w_ffn_in, w_ffn_out, weights
    )
    output, grad_x, gains, gpart, h1_pair, d_qkv, grad_out = rear(
        doc_starts,
        d_h2.reshape(count, width),
        r1,
        dy,
        x,
        q,
        raw,
        h1,
        mixed,
        kva,
        w_qkv,
        w_out,
        gsum,
        outp,
        ga,
        gf,
        qg,
        kg,
        cosine,
        sine,
    )
    grad_qkv, gains, gboth = projections(h1_pair, d_qkv, gains, gpart)
    grad_in, grad_down, output, grad_x, grad_qkv, grad_out, *gains = widen(
        gboth, output, grad_x, grad_qkv, grad_out, gains, w_ffn_out.shape[0]
    )
    return (
        output.reshape(rows, tok, width),
        grad_x.reshape(rows, tok, width),
        grad_qkv,
        grad_out.T,
        grad_in,
        grad_down,
        *[gain.reshape(-1) for gain in gains],
    )


def solution(mesh):
    split = Mesh(
        mesh.devices.reshape(4, 2, mesh.shape["seq"], mesh.shape["head"]),
        ("dp_0", "dp_1", "seq", "head"),
    )
    return jax.shard_map(
        body,
        mesh=split,
        in_specs=(
            P(DP, ("seq", "head"), None),
            P(),
            P(),
            P(("seq", "head"), None, None),
            P(("seq", "head"), None),
            P(),
            P(),
            P(),
            P(),
            P(DP, None),
            P(DP, ("seq", "head"), None),
        ),
        out_specs=(
            P(DP, ("seq", "head"), None),
            P(DP, ("seq", "head"), None),
            P(DP_SEQ_HEAD, None),
            P(None, DP_SEQ_HEAD),
            P(("seq", "head"), None, None),
            P(("seq", "head"), None),
            P(),
            P(),
            P(),
            P(),
        ),
        check_vma=False,
    )
```
